128 devices in a mesh: dp: 32 (over y, z, core), mp: 4 (over x).
Axes of the slice: x: 4, y: 4, z: 4, core: 2. Of those that a mesh axis runs over, the one named last changes fastest.
Arguments:
- patches: bfloat16 [32, 1024, 768], P('dp'), may hold values from -6 to 6
- image_ids: int32 [32, 1024], P('dp'), may hold values from 0 to 7, as said below
- keep: int32 [32, 1024], P('dp'), may hold values from 0 to 1, as said below
- labels: int32 [32, 8], P('dp'), may hold values from 0 to 999
- owners: int32 [96], replicated, may hold values from 0 to 95, as said below
- soap_weight: float32 [384, 36864], P(('dp', 'mp'))
- soap_first: float32 [384, 36864], P(('dp', 'mp')), may hold values from -3.8146973e-06 to 3.8146973e-06
- soap_second: float32 [384, 36864], P(('dp', 'mp')), may hold values from 3.4163574e-13 to 1.353651e-12
- stat_left: float32 [384, 36864], P(('dp', 'mp')), as said below
- stat_right: float32 [384, 36864], P(('dp', 'mp')), as said below
- basis_left: float32 [384, 36864], P(('dp', 'mp')), as said below
- basis_right: float32 [384, 36864], P(('dp', 'mp')), as said below
- embed_weight: float32 [768, 768], P(None, 'mp'), may hold values from -0.21875 to 0.21875
- embed_first: float32 [768, 768], P(None, 'mp'), may hold values from -3.8146973e-06 to 3.8146973e-06
- embed_second: float32 [768, 768], P(None, 'mp'), may hold values from 3.4163574e-13 to 1.353651e-12
- head_weight: float32 [768, 1000], P('mp'), may hold values from -0.625 to 0.625
- head_first: float32 [768, 1000], P('mp'), may hold values from -3.8146973e-06 to 3.8146973e-06
- head_second: float32 [768, 1000], P('mp'), may hold values from 3.4163574e-13 to 1.353651e-12
- vectors: float32 [5096], replicated
- vector_first: float32 [5096], replicated, may hold values from -3.8146973e-05 to 3.8146973e-05
- vector_second: float32 [5096], replicated, may hold values from 3.416357e-11 to 1.353651e-10
Outputs:
- loss_sum: float32 [], replicated
- image_count: float32 [], replicated
- grad_norm: float32 [], replicated
- soap_weight_new: float32 [384, 36864], P(('dp', 'mp'))
- soap_first_new: float32 [384, 36864], P(('dp', 'mp'))
- soap_second_new: float32 [384, 36864], P(('dp', 'mp'))
- stat_left_new: float32 [384, 36864], P(('dp', 'mp'))
- stat_right_new: float32 [384, 36864], P(('dp', 'mp'))
- basis_left_new: float32 [384, 36864], P(('dp', 'mp'))
- basis_right_new: float32 [384, 36864], P(('dp', 'mp'))
- soap_weight_low: bfloat16 [384, 36864], P(('dp', 'mp'))
- embed_new: float32 [768, 768], P(None, 'mp')
- embed_first_new: float32 [768, 768], P(None, 'mp')
- embed_second_new: float32 [768, 768], P(None, 'mp')
- head_new: float32 [768, 1000], P('mp')
- head_first_new: float32 [768, 1000], P('mp')
- head_second_new: float32 [768, 1000], P('mp')
- vectors_new: float32 [5096], replicated
- vector_first_new: float32 [5096], replicated
- vector_second_new: float32 [5096], replicated
The draws below stay inside these ranges and needn't reach their ends.
Inputs may be any that keep to these rules, and one draw needn't show every extreme that they name: `image_ids`: images are contiguous runs of positions numbered 0, 1, 2 ... in order, every position belongs to one; a sequence holds up to 8 images and the last sequence holds exactly 8. `keep`: the first position of every image is kept. `owners`: A permutation of the block numbers. `stat_left`: each block is symmetric positive definite. `stat_right`: each block is symmetric positive definite. `basis_left`: each block is an orthogonal matrix. `basis_right`: each block is an orthogonal matrix.
All inputs are finite; a program needn't handle non-finite values.
Results may differ from the reference program's by a relative error of at most 0.014.
The reference program's roundings to bfloat16 on the way count: a program that leaves them out, or rounds other values in their place, can miss the bound.
Values may be sent and summed in bfloat16 or wider, within the bound.
No kernel may reach another device: no remote copies, remote signals or barrier semaphores. Data moves between devices by JAX's collectives and lax.ppermute only.
A program may use at most 256 MiB of HBM per device.

```python
import math
import jax
import jax.numpy as jnp
from jax import lax

D = 768
FF = 3072
HEADS = 12
HD = 64
PD = 768
CLASSES = 1000
LAYERS = 2
LEN = 1024
IMGS = 8
STEP = 10
SEQS = 32
BLOCK = 192
BLOCKS = 96
BLK_DEV = 3
SLOTS = 384
PARAMS = 15513600
VEC = 5096
N_DP = 32
N_MP = 4


def pack_layout(key):
    key = jax.random.fold_in(key, 11)
    key_count, key_cut, key_rate, key_drop = jax.random.split(key, 4)
    seq_index = jnp.arange(SEQS)
    span = max(SEQS - 1, 1)
    base = (IMGS * span + 2 * IMGS * seq_index) // (3 * span)
    images = jnp.clip(base + jax.random.randint(key_count, (SEQS,), 0, 2), 1, IMGS)
    images = jnp.where(seq_index == SEQS - 1, IMGS, images)
    scores = jax.random.randint(key_cut, (SEQS, LEN - 1), 0, 1 << 20) * LEN + jnp.arange(LEN - 1)
    ranks = jnp.argsort(jnp.argsort(scores, axis=1), axis=1)
    cuts = (ranks < (images - 1)[:, None]).astype(jnp.int32)
    starts = jnp.concatenate([jnp.ones((SEQS, 1), jnp.int32), cuts], axis=1)
    image_ids = (jnp.cumsum(starts, axis=1) - 1).astype(jnp.int32)
    rates = jax.random.randint(key_rate, (SEQS, IMGS), 0, 51)
    rate_at = jnp.take_along_axis(rates, image_ids, axis=1)
    rolled = jax.random.randint(key_drop, (SEQS, LEN), 0, 100)
    kept = jnp.where((rolled >= rate_at) | (starts == 1), 1, 0).astype(jnp.int32)
    return (image_ids, kept)


def draw_image_ids(key, part):
    return pack_layout(key)[0]


def draw_keep(key, part):
    return pack_layout(key)[1]


def owner_order(key):
    return jax.random.permutation(jax.random.fold_in(key, 5), BLOCKS).astype(jnp.int32)


def draw_owners(key, part):
    return owner_order(key)


def draw_soap_weight(key, part):
    owners = owner_order(key)
    key = jax.random.fold_in(key, 6)
    inverse = jnp.argsort(owners)
    mp_count = SLOTS // BLOCKS
    slot = jnp.arange(SLOTS)
    local = slot // (mp_count * BLK_DEV) * BLK_DEV + slot % BLK_DEV
    within = inverse[local] % (BLOCKS // LAYERS)
    row_tiles = D // BLOCK
    scale = jnp.where(within < 3 * row_tiles, D ** (-0.5), jnp.where(within < 4 * row_tiles, (2 * D * IMGS // LEN) ** (-0.5), jnp.where(within < 4 * row_tiles + row_tiles * (FF // D), D ** (-0.5), FF ** (-0.5))))
    return jax.random.normal(key, (SLOTS, BLOCK * BLOCK), jnp.float32) * scale[:, None].astype(jnp.float32)


def statistics(key, scale):
    key_diag, key_off = jax.random.split(key)
    diagonal = jax.random.uniform(key_diag, (SLOTS, BLOCK), jnp.float32, 1.0, 4.0)
    spread = jax.random.uniform(key_off, (SLOTS, BLOCK, BLOCK), jnp.float32, -0.6 / BLOCK, 0.6 / BLOCK)
    spread = 0.5 * (spread + jnp.swapaxes(spread, 1, 2))
    identity = jnp.eye(BLOCK, dtype=jnp.float32)
    tiles = scale * (spread * (1.0 - identity) + diagonal[:, :, None] * identity)
    return tiles.reshape(SLOTS, BLOCK * BLOCK)


def draw_stat_left(key, part):
    key = jax.random.fold_in(key, 21)
    return statistics(key, BLOCK * 0.0001 / PARAMS)


def draw_stat_right(key, part):
    key = jax.random.fold_in(key, 22)
    return statistics(key, BLOCK * 0.0001 / PARAMS)


def cosine_basis(key):
    key_freq, key_sign = jax.random.split(key)
    frequency = jax.vmap(lambda part_key: jax.random.permutation(part_key, BLOCK))(jax.random.split(key_freq, SLOTS)).astype(jnp.float32)
    sign_flip = 2.0 * jax.random.randint(key_sign, (SLOTS, BLOCK), 0, 2).astype(jnp.float32) - 1.0
    places = jnp.arange(BLOCK, dtype=jnp.float32) + 0.5
    scaled = jnp.where(frequency == 0, math.sqrt(1.0 / BLOCK), math.sqrt(2.0 / BLOCK))
    tiles = jnp.cos(math.pi * places[None, :, None] * frequency[:, None, :] / BLOCK) * (scaled * sign_flip)[:, None, :]
    return tiles.reshape(SLOTS, BLOCK * BLOCK)


def draw_basis_left(key, part):
    key = jax.random.fold_in(key, 23)
    return cosine_basis(key)


def draw_basis_right(key, part):
    key = jax.random.fold_in(key, 24)
    return cosine_basis(key)


def draw_vectors(key, part):
    key = jax.random.fold_in(key, 31)
    gain_count = (2 * LAYERS + 1) * D
    head_count = 2 * LAYERS * HD
    index = jnp.arange(VEC)
    noise = jax.random.normal(key, (VEC,), jnp.float32)
    rising = 0.5 + (index % D).astype(jnp.float32) / D
    return jnp.where(index < gain_count, rising * (1.0 + 0.1 * noise), jnp.where(index < gain_count + head_count, 1.0 + 0.15 * noise, noise))


def with_ends(array, own_key, smallest, largest):
    spot = [jax.random.randint(jax.random.fold_in(own_key, axis), (), 0, length) for axis, length in enumerate(array.shape)]
    main_axis = array.shape.index(max(array.shape))
    beside = spot[:main_axis] + [(spot[main_axis] + 1) % array.shape[main_axis]] + spot[main_axis + 1:]
    return array.at[tuple(spot)].set(smallest).at[tuple(beside)].set(largest)


def levels(rng, shape, cuts, smallest, high):
    factor_of, own = 1.0, jax.random.fold_in(rng, 6)
    for axis_at, blocks in cuts:
        steps = jnp.exp(jax.random.uniform(jax.random.fold_in(own, axis_at), (blocks,), jnp.float32, smallest / len(cuts), high / len(cuts)))
        factor_of = factor_of * jnp.repeat(steps, shape[axis_at] // blocks).reshape([-1 if axis == axis_at else 1 for axis in range(len(shape))])
    return factor_of


def bell_draw(key, extent, deviation, most, pieces=(), held_as=jnp.bfloat16):
    loudness = levels(key, extent, pieces, -0.22, 0.18) if pieces else 1.0
    array = jax.random.normal(key, extent, jnp.float32) * deviation * loudness
    return jnp.minimum(jnp.maximum(array, -most), most).astype(held_as)


def setup_inputs(seed: int = 0) -> dict:
    seeds = jax.random.split(jax.random.key(seed), 22)
    patches = bell_draw(seeds[0], (SEQS, LEN, PD), 1.0, 6.0, ((0, 32),))
    image_ids = draw_image_ids(jax.random.fold_in(seeds[21], 71), 0)
    keep = draw_keep(jax.random.fold_in(seeds[21], 71), 0)
    labels = with_ends(jax.random.randint(seeds[3], (SEQS, IMGS), 0, CLASSES), jax.random.fold_in(seeds[3], 1), 0, CLASSES - 1).astype(jnp.int32)
    owners = draw_owners(jax.random.fold_in(seeds[21], 71), 0)
    soap_weight = draw_soap_weight(jax.random.fold_in(seeds[21], 71), 0)
    soap_first = bell_draw(seeds[6], (SLOTS, BLOCK * BLOCK), (0.0011 * PARAMS ** -0.5), 3.814697265625e-06, ((0, 128),), jnp.float32)
    soap_second = jnp.clip(3.4163573662746027e-13 + 1.0120152871100074e-12 * jax.random.uniform(seeds[7], (SLOTS, BLOCK * BLOCK), jnp.float32) ** levels(seeds[7], (SLOTS, BLOCK * BLOCK), ((0, 128),), -0.2, 0.2), 3.4163573662746027e-13, 1.3536510237374677e-12)
    stat_left = draw_stat_left(jax.random.fold_in(seeds[21], 71), 0)
    stat_right = draw_stat_right(jax.random.fold_in(seeds[21], 71), 0)
    basis_left = draw_basis_left(jax.random.fold_in(seeds[21], 71), 0)
    basis_right = draw_basis_right(jax.random.fold_in(seeds[21], 71), 0)
    embed_weight = bell_draw(seeds[12], (PD, D), PD ** -0.5, 0.21875, ((1, 4),), jnp.float32)
    embed_first = bell_draw(seeds[13], (PD, D), (0.0011 * PARAMS ** -0.5), 3.814697265625e-06, ((1, 4),), jnp.float32)
    embed_second = jnp.clip(3.4163573662746027e-13 + 1.0120152871100074e-12 * jax.random.uniform(seeds[14], (PD, D), jnp.float32) ** levels(seeds[14], (PD, D), ((1, 4),), -0.2, 0.2), 3.4163573662746027e-13, 1.3536510237374677e-12)
    head_weight = bell_draw(seeds[15], (D, CLASSES), (D // 9) ** -0.5, 0.625, ((0, 4),), jnp.float32)
    head_first = bell_draw(seeds[16], (D, CLASSES), (0.0011 * PARAMS ** -0.5), 3.814697265625e-06, ((0, 4),), jnp.float32)
    head_second = jnp.clip(3.4163573662746027e-13 + 1.0120152871100074e-12 * jax.random.uniform(seeds[17], (D, CLASSES), jnp.float32) ** levels(seeds[17], (D, CLASSES), ((0, 4),), -0.2, 0.2), 3.4163573662746027e-13, 1.3536510237374677e-12)
    vectors = draw_vectors(jax.random.fold_in(seeds[21], 71), 0)
    vector_first = bell_draw(seeds[19], (VEC,), (0.011 * PARAMS ** -0.5), 3.814697265625e-05, (), jnp.float32)
    vector_second = jnp.clip(jax.random.uniform(seeds[20], (VEC,), jnp.float32, 3.416357127750125e-11, 1.3536509413381026e-10), 3.416357127750125e-11, 1.3536509413381026e-10)
    return {"patches": patches, "image_ids": image_ids, "keep": keep, "labels": labels, "owners": owners, "soap_weight": soap_weight, "soap_first": soap_first, "soap_second": soap_second, "stat_left": stat_left, "stat_right": stat_right, "basis_left": basis_left, "basis_right": basis_right, "embed_weight": embed_weight, "embed_first": embed_first, "embed_second": embed_second, "head_weight": head_weight, "head_first": head_first, "head_second": head_second, "vectors": vectors, "vector_first": vector_first, "vector_second": vector_second}


@jax.custom_vjp
def low(v):
    return lax.optimization_barrier(v.astype(jnp.bfloat16)).astype(jnp.float32)

@jax.custom_vjp
def low_back(v):
    return v

def low_keep(v):
    return (low(v), None)

def low_pass(kept, grad):
    return (grad,)

def back_keep(v):
    return (v, None)

def back_low(kept, grad):
    return (low(grad),)
low.defvjp(low_keep, low_pass)
low_back.defvjp(back_keep, back_low)
first_decay = 0.9
second_decay = 0.95
weight_decay = 0.05
matrix_rate = 0.03
vector_rate = 0.3
clip_limit = 0.01
adam_epsilon = 1e-08
norm_epsilon = 1e-06
masked_score = -1e+30
highest = lax.Precision.HIGHEST

def layer_norm(values, gain_row):
    centered = values - lax.optimization_barrier(jnp.mean(values, -1, keepdims=True))
    return centered * lax.rsqrt(lax.optimization_barrier(jnp.mean(centered * centered, -1, keepdims=True)) + norm_epsilon) * gain_row

def product(left, right):
    return jnp.dot(left, right, precision=highest)

def as_tiles(flat_rows):
    return flat_rows.reshape(flat_rows.shape[0], BLOCK, BLOCK)

def as_rows(tiles):
    return tiles.reshape(tiles.shape[0], BLOCK * BLOCK)

def to_blocks(w_qkv, w_out, w_up, w_down):
    layers, breadth, triple, tile_size = w_qkv.shape
    row_tiles = breadth // tile_size
    hid_tiles = w_up.shape[2] // tile_size
    qkv_tiles = w_qkv.reshape(layers, row_tiles, tile_size, triple, tile_size).transpose(0, 1, 3, 2, 4).reshape(layers, row_tiles * triple, tile_size, tile_size)
    out_tiles = w_out.reshape(layers, tile_size, row_tiles, tile_size).transpose(0, 2, 1, 3)
    up_tiles = w_up.reshape(layers, row_tiles, tile_size, hid_tiles, tile_size).transpose(0, 1, 3, 2, 4).reshape(layers, row_tiles * hid_tiles, tile_size, tile_size)
    down_tiles = w_down.reshape(layers, hid_tiles, tile_size, row_tiles, tile_size).transpose(0, 1, 3, 2, 4).reshape(layers, hid_tiles * row_tiles, tile_size, tile_size)
    joined = jnp.concatenate([qkv_tiles, out_tiles, up_tiles, down_tiles], axis=1)
    return joined.reshape(layers * joined.shape[1], tile_size, tile_size)

def from_blocks(stack, row_tiles, hid_tiles):
    tile_size = stack.shape[-1]
    per_layer = stack.reshape(LAYERS, -1, tile_size, tile_size)
    cut_one = 3 * row_tiles
    cut_two = cut_one + row_tiles
    cut_three = cut_two + row_tiles * hid_tiles
    w_qkv = per_layer[:, :cut_one].reshape(LAYERS, row_tiles, 3, tile_size, tile_size).transpose(0, 1, 3, 2, 4).reshape(LAYERS, row_tiles * tile_size, 3, tile_size)
    w_out = per_layer[:, cut_one:cut_two].transpose(0, 2, 1, 3).reshape(LAYERS, tile_size, row_tiles * tile_size)
    w_up = per_layer[:, cut_two:cut_three].reshape(LAYERS, row_tiles, hid_tiles, tile_size, tile_size).transpose(0, 1, 3, 2, 4).reshape(LAYERS, row_tiles * tile_size, hid_tiles * tile_size)
    w_down = per_layer[:, cut_three:].reshape(LAYERS, hid_tiles, row_tiles, tile_size, tile_size).transpose(0, 1, 3, 2, 4).reshape(LAYERS, hid_tiles * tile_size, row_tiles * tile_size)
    return (w_qkv, w_out, w_up, w_down)

def to_slots(blocks, owners):
    tile_size = blocks.shape[-1]
    slotted = blocks[:, jnp.argsort(owners)]
    slotted = slotted.reshape(N_MP, N_DP, BLK_DEV, tile_size, tile_size)
    return jnp.swapaxes(slotted, 0, 1).reshape(SLOTS, tile_size, tile_size)

def from_slots(slots, owners):
    tile_size = slots.shape[-1]
    local = jnp.swapaxes(slots.reshape(N_DP, N_MP, BLK_DEV, tile_size, tile_size), 0, 1)
    return local.reshape(N_MP, BLOCKS, tile_size, tile_size)[:, owners]

def rotate(matrix, left_basis, right_basis):
    return jnp.einsum('nji,njk,nkl->nil', left_basis, matrix, right_basis, precision=highest)

def unrotate(matrix, left_basis, right_basis):
    return jnp.einsum('nij,njk,nlk->nil', left_basis, matrix, right_basis, precision=highest)

def power_step(statistic, basis_now):
    turned = jnp.einsum('nij,njk->nik', statistic, basis_now, precision=highest)
    gram_mat = jnp.einsum('nji,njk->nik', turned, turned, precision=highest)
    factor = jnp.linalg.cholesky(gram_mat)
    solved = jax.vmap(lambda lower_tri, right_side: jax.scipy.linalg.solve_triangular(lower_tri, right_side, lower=True))(factor, jnp.swapaxes(turned, 1, 2))
    return jnp.swapaxes(solved, 1, 2)

def soap_update(master, gradient, first, second, stat_l, stat_r, left_basis, right_basis):
    bias_one = 1.0 - first_decay ** STEP
    bias_two = 1.0 - second_decay ** STEP
    first_new = first_decay * first + (1.0 - first_decay) * gradient
    turned = rotate(gradient, left_basis, right_basis)
    second_new = second_decay * second + (1.0 - second_decay) * turned * turned
    scaled = rotate(first_new, left_basis, right_basis) / bias_one / (jnp.sqrt(second_new / bias_two) + adam_epsilon)
    master_new = master * (1.0 - matrix_rate * weight_decay) - matrix_rate * unrotate(scaled, left_basis, right_basis)
    stat_l_new = second_decay * stat_l + (1.0 - second_decay) * jnp.einsum('nij,nkj->nik', gradient, gradient, precision=highest)
    stat_r_new = second_decay * stat_r + (1.0 - second_decay) * jnp.einsum('nji,njk->nik', gradient, gradient, precision=highest)
    return (master_new, first_new, second_new, stat_l_new, stat_r_new, power_step(stat_l_new, left_basis), power_step(stat_r_new, right_basis), master_new.astype(jnp.bfloat16))

def adamw(master, gradient, first, second, rate, decay):
    first_new = first_decay * first + (1.0 - first_decay) * gradient
    second_new = second_decay * second + (1.0 - second_decay) * gradient * gradient
    step_dir = first_new / (1.0 - first_decay ** STEP) / (jnp.sqrt(second_new / (1.0 - second_decay ** STEP)) + adam_epsilon)
    return (master * (1.0 - rate * decay) - rate * step_dir, first_new, second_new)

@jax.checkpoint
def attention(queries, keys_in, values, allowed):
    scores = low_back(jnp.einsum('qhd,khd->hqk', queries, keys_in, precision=highest) * HD ** (-0.5))
    scores = jnp.where(allowed[None], scores, masked_score)
    row_max = lax.optimization_barrier(jnp.max(scores, -1, keepdims=True))
    weights = jnp.exp(scores - row_max)
    probs_low = low(weights / lax.optimization_barrier(jnp.sum(weights, -1, keepdims=True)))
    return jnp.einsum('hqk,khd->qhd', probs_low, values, precision=highest)

def sequence_loss(params, bundle):
    embed, w_qkv, w_out, w_up, w_down, head, vectors = params
    patch_rows, image_row, keep_row, label_row = bundle
    split_one = (2 * LAYERS + 1) * D
    gain_rows = vectors[:split_one].reshape(2 * LAYERS + 1, D)
    head_gains = vectors[split_one:split_one + 2 * LAYERS * HD].reshape(LAYERS, 2, HD)
    class_bias = vectors[VEC - CLASSES:]
    allowed = (image_row[:, None] == image_row[None, :]) & (keep_row[None, :] == 1)
    resid = low(low_back(product(patch_rows, embed)))
    for depth in range(LAYERS):
        normed = low(layer_norm(resid, gain_rows[2 * depth]))
        projected = low_back(jnp.einsum('rd,dcs->rcs', normed, w_qkv[depth], precision=highest))
        queries = low(layer_norm(projected[:, 0].reshape(LEN, HEADS, HD), head_gains[depth, 0]))
        keys_in = low(layer_norm(projected[:, 1].reshape(LEN, HEADS, HD), head_gains[depth, 1]))
        values = low(projected[:, 2].reshape(LEN, HEADS, HD))
        attended = low(low_back(attention(queries, keys_in, values, allowed)))
        resid = resid + low_back(product(attended.reshape(LEN, D), w_out[depth]))
        normed = low(layer_norm(resid, gain_rows[2 * depth + 1]))
        activated = low(jax.nn.gelu(low_back(product(normed, w_up[depth])), approximate=False))
        resid = resid + low_back(product(activated, w_down[depth]))
    final = layer_norm(resid, gain_rows[2 * LAYERS])
    member = ((image_row[:, None] == jnp.arange(IMGS)[None, :]) & (keep_row[:, None] == 1)).astype(jnp.float32)
    counts = lax.optimization_barrier(jnp.sum(member, axis=0))
    pooled = product(member.T, final) / jnp.maximum(counts, 1.0)[:, None]
    logits = low_back(product(low(pooled), head)) + class_bias
    row_max = lax.optimization_barrier(jnp.max(logits, -1, keepdims=True))
    log_norm = row_max[:, 0] + jnp.log(lax.optimization_barrier(jnp.sum(jnp.exp(logits - row_max), -1)))
    picked = lax.optimization_barrier(jnp.sum(jnp.where(jnp.arange(CLASSES)[None, :] == label_row[:, None], logits, 0.0), -1))
    return jnp.sum((log_norm - picked) * (counts > 0).astype(jnp.float32))

def reference(patches, image_ids, keep, labels, owners, soap_weight, soap_first, soap_second, stat_left, stat_right, basis_left, basis_right, embed_weight, embed_first, embed_second, head_weight, head_first, head_second, vectors, vector_first, vector_second):
    row_tiles = D // BLOCK
    hid_tiles = FF // D
    soap_weight = as_tiles(soap_weight)
    soap_first = as_tiles(soap_first)
    soap_second = as_tiles(soap_second)
    stat_left = as_tiles(stat_left)
    stat_right = as_tiles(stat_right)
    basis_left = as_tiles(basis_left)
    basis_right = as_tiles(basis_right)
    blocks = from_slots(low(soap_weight), owners)
    shard_qkv, shard_out, shard_up, shard_down = jax.vmap(lambda stack: from_blocks(stack, row_tiles, hid_tiles))(blocks)
    w_qkv = jnp.transpose(shard_qkv, (1, 2, 3, 0, 4)).reshape(LAYERS, D, 3, D)
    w_out = jnp.swapaxes(shard_out, 0, 1).reshape(LAYERS, D, D)
    w_up = jnp.transpose(shard_up, (1, 2, 0, 3)).reshape(LAYERS, D, FF)
    w_down = jnp.swapaxes(shard_down, 0, 1).reshape(LAYERS, FF, D)
    params = (low(embed_weight), w_qkv, w_out, w_up, w_down, low(head_weight), vectors)
    member_all = (image_ids[:, :, None] == jnp.arange(IMGS)[None, None, :]) & (keep[:, :, None] == 1)
    image_count = jnp.sum(jnp.any(member_all, axis=1).astype(jnp.float32))
    bundles = (patches.astype(jnp.float32), image_ids, keep, labels)

    def mean_loss(weights_in):
        sums = lax.map(lambda bundle: sequence_loss(weights_in, bundle), bundles)
        total = jnp.sum(sums)
        return (total / image_count, total)
    mean_value, pullback, loss_sum = jax.vjp(mean_loss, params, has_aux=True)
    grads = pullback(jnp.ones_like(mean_value))[0]
    grad_embed, grad_qkv, grad_out, grad_up, grad_down, grad_head, grad_vector = grads
    shards = (grad_qkv.reshape(LAYERS, D, 3, N_MP, BLOCK).transpose(3, 0, 1, 2, 4), jnp.swapaxes(grad_out.reshape(LAYERS, N_MP, BLOCK, D), 0, 1), grad_up.reshape(LAYERS, D, N_MP, FF // N_MP).transpose(2, 0, 1, 3), jnp.swapaxes(grad_down.reshape(LAYERS, N_MP, FF // N_MP, D), 0, 1))
    grad_slots = to_slots(jax.vmap(to_blocks)(*shards), owners)
    squares = jnp.sum(grad_slots * grad_slots) + jnp.sum(grad_embed * grad_embed) + jnp.sum(grad_head * grad_head) + jnp.sum(grad_vector * grad_vector)
    grad_norm = jnp.sqrt(squares)
    factor = clip_limit / jnp.maximum(grad_norm, clip_limit)
    soap_new = soap_update(soap_weight, grad_slots * factor, soap_first, soap_second, stat_left, stat_right, basis_left, basis_right)
    soap_new = tuple((as_rows(entry) for entry in soap_new))
    embed_new = adamw(embed_weight, grad_embed * factor, embed_first, embed_second, matrix_rate, weight_decay)
    head_new = adamw(head_weight, grad_head * factor, head_first, head_second, matrix_rate, weight_decay)
    vector_new = adamw(vectors, grad_vector * factor, vector_first, vector_second, vector_rate, 0.0)
    return (loss_sum, image_count, grad_norm, soap_new[0], soap_new[1], soap_new[2], soap_new[3], soap_new[4], soap_new[5], soap_new[6], soap_new[7], embed_new[0], embed_new[1], embed_new[2], head_new[0], head_new[1], head_new[2], vector_new[0], vector_new[1], vector_new[2])
```

```python
import jax
import jax.numpy as jnp
from jax import lax
from jax.experimental import pallas as pl
from jax.experimental.pallas import tpu as pltpu
from jax.sharding import PartitionSpec as P

D = 768
HD = 64
HEADS = 3
CLASSES = 1000
LAYERS = 2
IMGS = 8
STEP = 10
TILE = 192
TOKENS = 1024
OWN = 256
PACK = 288
SMALL = 96
ROWS = 3 * PACK + SMALL
EMBED_ROWS = 36
HEAD_ROWS = 48

first_decay = 0.9
second_decay = 0.95
weight_decay = 0.05
matrix_rate = 0.03
vector_rate = 0.3
clip_limit = 0.01
adam_epsilon = 1e-08
norm_epsilon = 1e-06
masked_score = -1e30
highest = lax.Precision.HIGHEST
f32 = jnp.float32
bf16 = jnp.bfloat16
MIB = 2**20
VM = pl.BlockSpec(memory_space=pltpu.VMEM)
SM = pl.BlockSpec(memory_space=pltpu.SMEM)
ANY = pl.BlockSpec(memory_space=pl.ANY)


def params(mib):
    return pltpu.CompilerParams(vmem_limit_bytes=mib * MIB)


def cost(flops, moved, exps=0):
    return pl.CostEstimate(flops=flops, bytes_accessed=moved, transcendentals=exps)


def shape(dims, kind=f32):
    return jax.ShapeDtypeStruct(dims, kind)


def mm(a, b, ca=1, cb=0):
    return lax.dot_general(a, b, (((ca,), (cb,)), ((), ())), preferred_element_type=f32)


def mm_full(a, b, ca, cb):
    return lax.dot_general(
        a, b, (((ca,), (cb,)), ((), ())), precision=highest, preferred_element_type=f32
    )


def mm_split(a, b, ca, cb):
    a_high, b_high = (a.astype(bf16), b.astype(bf16))
    a_low = (a - a_high.astype(f32)).astype(bf16)
    b_low = (b - b_high.astype(f32)).astype(bf16)
    return mm(a_high, b_high, ca, cb) + (mm(a_high, b_low, ca, cb) + mm(a_low, b_high, ca, cb))


def normalize(values):
    centered = values - jnp.mean(values, -1, keepdims=True)
    inverse = lax.rsqrt(jnp.mean(centered * centered, -1, keepdims=True) + norm_epsilon)
    return centered * inverse, inverse


def norm_back(grad, gain, normed, inverse):
    scaled = grad * gain
    return inverse * (
        scaled
        - jnp.mean(scaled, -1, keepdims=True)
        - normed * jnp.mean(scaled * normed, -1, keepdims=True)
    )


def gauss_parts(value):
    size = jnp.abs(value) * 0.7071067811865476
    bell = jnp.exp(-size * size)
    t = 1.0 / (1.0 + 0.3275911 * size)
    poly = t * (
        0.254829592
        + t * (-0.284496736 + t * (1.421413741 + t * (-1.453152027 + t * 1.061405429)))
    )
    tail = 0.5 * poly * bell
    return jnp.where(value >= 0, 1.0 - tail, tail), bell


def gelu(value):
    return value * gauss_parts(value)[0]


def pack_tile(tile):
    half = TILE // 2
    right = tile[..., 128:]
    return jnp.concatenate(
        [
            tile[..., :128],
            jnp.concatenate([right[..., :half, :], right[..., half:, :]], axis=-1),
        ],
        axis=-2,
    )


def unpack_tile(packed):
    half = TILE // 2
    right = packed[..., TILE:, :]
    return jnp.concatenate(
        [
            packed[..., :TILE, :],
            jnp.concatenate([right[..., :64], right[..., 64:]], axis=-2),
        ],
        axis=-1,
    )


def assemble(table, slots, blocks):
    rows = len(blocks)
    flat = [block for line in blocks for block in line]

    def kernel(table_ref, *refs):
        out_ref = refs[-1]
        for i in range(rows):
            for t in range(4):
                out_ref[0, TILE * i : TILE * i + TILE, TILE * t : TILE * t + TILE] = unpack_tile(
                    refs[4 * i + t][0]
                )

    def spec(block):
        return pl.BlockSpec((1, PACK, 128), lambda r, table_ref: (table_ref[r * 96 + block], 0, 0))

    return pl.pallas_call(
        kernel,
        grid_spec=pltpu.PrefetchScalarGridSpec(
            num_scalar_prefetch=1,
            grid=(4,),
            in_specs=[spec(block) for block in flat],
            out_specs=pl.BlockSpec((1, rows * TILE, D), lambda r, table_ref: (r, 0, 0)),
        ),
        out_shape=shape((4, rows * TILE, D), bf16),
        compiler_params=params(32),
        cost_estimate=cost(0, 16 * rows * TILE * TILE * 4),
        name="assemble",
    )(table, *([slots] * len(flat)))


def layer_weights(table, slots, depth):
    base = 48 * depth
    qkv = assemble(table, slots, [[base + 3 * r + c for r in range(4)] for c in range(3)])
    out = assemble(table, slots, [[base + 12 + t for t in range(4)]])
    up = assemble(table, slots, [[base + 16 + 4 * r + t for r in range(4)] for t in range(4)])
    down = assemble(table, slots, [[base + 32 + 4 * t + r for r in range(4)] for t in range(4)])
    return qkv, out.reshape(D, D), up, down


def column_norm(values):
    centered = values - jnp.mean(values, 0, keepdims=True)
    inverse = lax.rsqrt(jnp.mean(centered * centered, 0, keepdims=True) + norm_epsilon)
    return centered * inverse, inverse


def attend_fwd(w_ref, a0, a1, a2, a3, gain_ref, qid_ref, kid_ref, pre_ref, v_ref, lse_ref, o_ref, q_s, k_s):
    for c in range(3):
        for r, a_ref in enumerate((a0, a1, a2, a3)):
            cols = slice(OWN * r, OWN * r + OWN)
            part = mm(w_ref[0, TILE * c : TILE * c + TILE, :], a_ref[...], 1, 1)
            if c == 2:
                v_ref[:, cols] = part.astype(bf16)
                continue
            pre_ref[TILE * c : TILE * c + TILE, cols] = part
            for h in range(HEADS):
                rows = slice(HD * h, HD * h + HD)
                low = (column_norm(part[rows, :])[0] * gain_ref[:, c : c + 1]).astype(bf16)
                if c == 0:
                    q_s[r, rows, :] = low * bf16(0.125)
                else:
                    k_s[h, cols, :] = low.T

    def step(i, carry):
        h, t = (i // 4, i % 4)
        rows = pl.ds(pl.multiple_of(h * HD, HD), HD)
        cols = pl.ds(pl.multiple_of(t * OWN, OWN), OWN)
        scores = mm(k_s[h], q_s[t, rows, :])
        scores = jnp.where(kid_ref[...] == qid_ref[:, cols], scores, masked_score)
        top = jnp.max(scores, 0, keepdims=True)
        weights = jnp.exp(scores - top)
        total = jnp.sum(weights, 0, keepdims=True)
        lse_ref[h, :, cols] = top + jnp.log(total)
        probs = (weights * (1.0 / total)).astype(bf16)
        o_ref[t, rows, :] = mm(v_ref[rows, :], probs).astype(bf16)
        return carry

    lax.fori_loop(0, 4 * HEADS, step, 0)


def run_attend_fwd(w, acts, gains, qid, kid):
    return pl.pallas_call(
        attend_fwd,
        grid=(1,),
        in_specs=[pl.BlockSpec((1, 3 * TILE, D), lambda i: (0, 0, 0))] + [VM] * 7,
        out_specs=[VM] * 4,
        out_shape=[
            shape((2 * TILE, TOKENS)),
            shape((TILE, TOKENS), bf16),
            shape((HEADS, 1, TOKENS)),
            shape((4, TILE, OWN), bf16),
        ],
        scratch_shapes=[pltpu.VMEM((4, TILE, OWN), bf16), pltpu.VMEM((HEADS, TOKENS, HD), bf16)],
        compiler_params=params(48),
        cost_estimate=cost(10**10, 6 * 10**6, 3 * 2**20),
        name="attend_fwd",
    )(w, *acts, gains, qid, kid)


def attend_bwd(
    pre_ref, v_ref, lse_ref, g0, g1, g2, g3, gain_ref, qid_ref, kid_ref,
    dp_ref, dgain_ref, q_s, qn_s, k_s, kt_s, vn_s, do_s, dq_s, dk_s, dv_s,
):
    for r, ref in enumerate((g0, g1, g2, g3)):
        do_s[r] = ref[...]
    for h in range(HEADS):
        rows = slice(HD * h, HD * h + HD)
        low = (column_norm(pre_ref[rows, :])[0] * gain_ref[:, 0:1]).astype(bf16)
        q_s[rows, :] = low * bf16(0.125)
        qn_s[h] = q_s[rows, :].T
        low = (column_norm(pre_ref[TILE + HD * h : TILE + HD * h + HD, :])[0] * gain_ref[:, 1:2]).astype(bf16)
        kt_s[rows, :] = low
        k_s[h] = low.T
        vn_s[h] = v_ref[rows, :].T
    dk_s[...] = jnp.zeros_like(dk_s)
    dv_s[...] = jnp.zeros_like(dv_s)

    def step(i, carry):
        h, t = (i // 4, i % 4)
        rows = pl.ds(pl.multiple_of(h * HD, HD), HD)
        cols = pl.ds(pl.multiple_of(t * OWN, OWN), OWN)
        scores = mm(k_s[h], q_s[rows, cols])
        scores = jnp.where(kid_ref[...] == qid_ref[:, cols], scores, masked_score)
        weights = jnp.exp(scores - lse_ref[h, :, cols])
        grad_out = do_s[t, rows, :]
        grad_weights = mm(vn_s[h], grad_out)
        dv_s[h] += mm(weights.astype(bf16), grad_out.T)
        inner = jnp.sum(weights * grad_weights, 0, keepdims=True)
        grad_scores = (weights * (grad_weights - inner)).astype(bf16)
        dq_s[rows, cols] = mm(kt_s[rows, :], grad_scores) * 0.125
        dk_s[h] += mm(grad_scores, qn_s[h, cols, :])
        return carry

    lax.fori_loop(0, 4 * HEADS, step, 0)
    for c in range(2):
        total = jnp.zeros((HD, 1), f32)
        for h in range(HEADS):
            grad = dq_s[HD * h : HD * h + HD, :] if c == 0 else dk_s[h].T
            base = TILE * c + HD * h
            normed, inverse = column_norm(pre_ref[base : base + HD, :])
            total = total + jnp.sum(grad * normed, 1, keepdims=True)
            scaled = grad * gain_ref[:, c : c + 1]
            back = inverse * (
                scaled
                - jnp.mean(scaled, 0, keepdims=True)
                - normed * jnp.mean(scaled * normed, 0, keepdims=True)
            )
            for r in range(4):
                dp_ref[r, base : base + HD, :] = back[:, OWN * r : OWN * r + OWN].astype(bf16)
        dgain_ref[:, c : c + 1] = total
    for h in range(HEADS):
        back = dv_s[h].T.astype(bf16)
        for r in range(4):
            dp_ref[r, 2 * TILE + HD * h : 2 * TILE + HD * h + HD, :] = back[:, OWN * r : OWN * r + OWN]


def run_attend_bwd(pre, v, lse, grads, gains, qid, kid):
    return pl.pallas_call(
        attend_bwd,
        in_specs=[VM] * 10,
        out_specs=[VM] * 2,
        out_shape=[shape((4, 3 * TILE, OWN), bf16), shape((HD, 2))],
        scratch_shapes=[
            pltpu.VMEM((TILE, TOKENS), bf16),
            pltpu.VMEM((HEADS, TOKENS, HD), bf16),
            pltpu.VMEM((HEADS, TOKENS, HD), bf16),
            pltpu.VMEM((TILE, TOKENS), bf16),
            pltpu.VMEM((HEADS, TOKENS, HD), bf16),
            pltpu.VMEM((4, TILE, OWN), bf16),
            pltpu.VMEM((TILE, TOKENS), f32),
            pltpu.VMEM((HEADS, TOKENS, HD), f32),
            pltpu.VMEM((HEADS, TOKENS, HD), f32),
        ],
        compiler_params=params(48),
        cost_estimate=cost(2 * 10**10, 6 * 10**6, 3 * 2**20),
        name="attend_bwd",
    )(pre, v, lse, *grads, gains, qid, kid)


def mix_fwd(x_ref, o0, o1, o2, o3, w_out, gain_ref, next_ref, up_ref, down_ref,
            mid_ref, u_ref, ct_ref, x_out, a_out, c_s):
    r = pl.program_id(0)

    @pl.when(r == 0)
    def _():
        mid = x_ref[...]
        for k, ref in enumerate((o0, o1, o2, o3)):
            mid = mid + mm(ref[...], w_out[TILE * k : TILE * k + TILE, :], 0, 0)
        mid_ref[...] = mid
        low = (normalize(mid)[0] * gain_ref[...]).astype(bf16)
        c_s[...] = low
        ct_ref[...] = low.T
        x_out[...] = mid

    u = mm(c_s[...], up_ref[0], 1, 1)
    u_ref[0] = u
    x_out[...] += mm(gelu(u).astype(bf16), down_ref[0])

    @pl.when(r == 3)
    def _():
        a_out[...] = (normalize(x_out[...])[0] * next_ref[...]).astype(bf16)


def whole(*dims):
    return pl.BlockSpec(dims, lambda r: (0,) * len(dims))


def part(*dims):
    return pl.BlockSpec((1, *dims), lambda r: (r,) + (0,) * len(dims))


def run_mix_fwd(x, outs, w_out, gain, gain_next, up, down):
    return pl.pallas_call(
        mix_fwd,
        grid=(4,),
        in_specs=[whole(OWN, D)] + [whole(TILE, OWN)] * 4 + [whole(D, D), whole(1, D), whole(1, D), part(D, D), part(D, D)],
        out_specs=[whole(OWN, D), part(OWN, D), whole(D, OWN), whole(OWN, D), whole(OWN, D)],
        out_shape=[shape((OWN, D)), shape((4, OWN, D)), shape((D, OWN), bf16), shape((OWN, D)), shape((OWN, D), bf16)],
        scratch_shapes=[pltpu.VMEM((OWN, D), bf16)],
        compiler_params=params(48),
        cost_estimate=cost(6 * 10**9, 17 * 10**6, 10**6),
        name="mix_fwd",
    )(x, *outs, w_out, gain, gain_next, up, down)


def mix_bwd(g_ref, low_ref, mid_ref, u_ref, gain_ref, w_out, up_ref, down_ref,
            du_ref, mid_grad, mid_low, dgain_ref, do_ref, acc):
    r = pl.program_id(0)

    @pl.when(r == 0)
    def _():
        acc[...] = jnp.zeros_like(acc)

    df = mm(low_ref[...], down_ref[0], 1, 1)
    u = u_ref[0]
    cdf, bell = gauss_parts(u)
    du = (df * (cdf + u * bell * 0.3989422804014327)).astype(bf16)
    du_ref[0] = du
    acc[...] += mm(du, up_ref[0])

    @pl.when(r == 3)
    def _():
        normed, inverse = normalize(mid_ref[...])
        grad = acc[...]
        dgain_ref[...] = jnp.sum(grad * normed, 0, keepdims=True)
        total = g_ref[...] + norm_back(grad, gain_ref[...], normed, inverse)
        mid_grad[...] = total
        low = total.astype(bf16)
        mid_low[...] = low
        for k in range(4):
            do_ref[k] = mm(w_out[TILE * k : TILE * k + TILE, :], low, 1, 1).astype(bf16)


def run_mix_bwd(grad, grad_low, mid, u, gain, w_out, up, down):
    return pl.pallas_call(
        mix_bwd,
        grid=(4,),
        in_specs=[whole(OWN, D), whole(OWN, D), whole(OWN, D), part(OWN, D), whole(1, D), whole(D, D), part(D, D), part(D, D)],
        out_specs=[part(OWN, D), whole(OWN, D), whole(OWN, D), whole(1, D), whole(4, TILE, OWN)],
        out_shape=[shape((4, OWN, D), bf16), shape((OWN, D)), shape((OWN, D), bf16), shape((1, D)), shape((4, TILE, OWN), bf16)],
        scratch_shapes=[pltpu.VMEM((OWN, D), f32)],
        compiler_params=params(48),
        cost_estimate=cost(6 * 10**9, 17 * 10**6, 10**6),
        name="mix_bwd",
    )(grad, grad_low, mid, u, gain, w_out, up, down)


def input_bwd(mid_grad, d0, d1, d2, d3, w_ref, x_ref, gain_ref, grad_ref, low_ref, dgain_ref):
    grad = mm(d0[...], w_ref[0], 0, 0)
    for k, ref in ((1, d1), (2, d2), (3, d3)):
        grad = grad + mm(ref[...], w_ref[k], 0, 0)
    normed, inverse = normalize(x_ref[...])
    dgain_ref[...] = jnp.sum(grad * normed, 0, keepdims=True)
    total = mid_grad[...] + norm_back(grad, gain_ref[...], normed, inverse)
    grad_ref[...] = total
    low_ref[...] = total.astype(bf16)


def run_input_bwd(mid_grad, grads, w, x, gain):
    return pl.pallas_call(
        input_bwd,
        in_specs=[VM] * 8,
        out_specs=[VM] * 3,
        out_shape=[shape((OWN, D)), shape((OWN, D), bf16), shape((1, D))],
        compiler_params=params(48),
        cost_estimate=cost(10**9, 6 * 10**6),
        name="input_bwd",
    )(mid_grad, *grads, w, x, gain)


def send_tiles(places, stage, sems, keep, send, tiles, base):
    for i, (block, tile) in enumerate(tiles):
        at = base + i
        stage[at] = pack_tile(tile.astype(bf16))
        place = places[block]
        rows = pl.ds(pl.multiple_of((place % 3) * PACK, 16), PACK)

        @pl.when(place < 48)
        def _():
            pltpu.make_async_copy(stage.at[at], keep.at[place // 3, rows], sems.at[at]).start()

        @pl.when(place >= 48)
        def _():
            pltpu.make_async_copy(stage.at[at], send.at[place // 3 - 16, rows], sems.at[at]).start()


def wait_tiles(stage, sems, keep, count):
    for at in range(count):
        pltpu.make_async_copy(stage.at[at], keep.at[0, pl.ds(0, PACK)], sems.at[at]).wait()


def cut(line, count=4):
    return [line[:, TILE * t : TILE * t + TILE] for t in range(count)]


def mlp_grads(depth, places, *refs):
    ct, du, low, mid_low = (refs[0:4], refs[4:8], refs[8:12], refs[12:16])
    o_ref, up_ref = refs[16:18]
    keep, send, stage, f_s, sems = refs[-5:]
    base = 48 * depth
    for r in range(4):
        f_s[r] = gelu(mm(up_ref[0], ct[r][...])).astype(bf16)

    def rows_of(pieces, others, i):
        rows = slice(TILE * i, TILE * i + TILE)
        total = mm(pieces[0][rows, :], others[0][...])
        for r in range(1, 4):
            total = total + mm(pieces[r][rows, :], others[r][...])
        return total

    line = rows_of([o_ref.at[r] for r in range(4)], mid_low, 0)
    send_tiles(places, stage, sems, keep, send, [(base + 12 + t, x) for t, x in enumerate(cut(line))], 0)
    for i in range(4):
        line = rows_of(ct, du, i)
        tiles = [(base + 16 + 4 * i + t, x) for t, x in enumerate(cut(line))]
        send_tiles(places, stage, sems, keep, send, tiles, 4 + 4 * i)
    for i in range(4):
        line = rows_of([f_s.at[r] for r in range(4)], low, i)
        tiles = [(base + 32 + 4 * i + t, x) for t, x in enumerate(cut(line))]
        send_tiles(places, stage, sems, keep, send, tiles, 20 + 4 * i)
    wait_tiles(stage, sems, keep, 36)


def qkv_grads(depth, places, *refs):
    dp_ref, acts = (refs[0], refs[1:5])
    keep, send, stage, sems = refs[-4:]
    base = 48 * depth
    for c in range(3):
        rows = slice(TILE * c, TILE * c + TILE)
        line = mm(dp_ref[0, rows, :], acts[0][...])
        for r in range(1, 4):
            line = line + mm(dp_ref[r, rows, :], acts[r][...])
        tiles = [(base + 3 * t + c, x) for t, x in enumerate(cut(line))]
        send_tiles(places, stage, sems, keep, send, tiles, 4 * c)
    wait_tiles(stage, sems, keep, 12)


def grads_call(kernel, name, places, args, specs, buffers, scratch, flops):
    out = [shape((16, ROWS, 128), bf16)] * 2
    given = list(buffers) if buffers is not None else []
    first = 1 + len(args)
    return pl.pallas_call(
        kernel,
        grid=(1,),
        in_specs=[SM] + specs + [ANY] * len(given),
        out_specs=[ANY] * 2,
        out_shape=out,
        input_output_aliases={first + i: i for i in range(len(given))},
        scratch_shapes=scratch,
        compiler_params=params(56),
        cost_estimate=cost(flops, 10**7),
        name=name,
    )(places, *args, *given)


def run_mlp_grads(depth, places, ct, du, low, mid_low, o, up, buffers):
    specs = [VM] * 17 + [pl.BlockSpec((1, D, D), lambda i: (0, 0, 0))]
    return grads_call(
        lambda *refs: mlp_grads(depth, *refs), "mlp_grads", places,
        [*ct, *du, *low, *mid_low, o, up], specs, buffers,
        [pltpu.VMEM((36, PACK, 128), bf16), pltpu.VMEM((4, D, OWN), bf16), pltpu.SemaphoreType.DMA((36,))],
        4 * 10**9,
    )


def run_qkv_grads(depth, places, dp, acts, buffers):
    return grads_call(
        lambda *refs: qkv_grads(depth, *refs), "qkv_grads", places, [dp, *acts], [VM] * 5, buffers,
        [pltpu.VMEM((12, PACK, 128), bf16), pltpu.SemaphoreType.DMA((12,))], 10**9,
    )


def soap_early(first, stat_l, stat_r, left, right, turned_ref, l_ref, r_ref):
    turned_ref[0] = mm_split(mm_split(left[0], first[0], 0, 0), right[0], 1, 0)
    l_ref[0] = mm_full(stat_l[0], left[0], 1, 0)
    r_ref[0] = mm_full(stat_r[0], right[0], 1, 0)


def soap_mid(flip_ref, packed, left, right, grad_ref, turned_ref, yl_ref, yr_ref, gl_ref, gr_ref):
    tile = unpack_tile(packed[0])
    turned_tile = tile.T
    flip = flip_ref[pl.program_id(0)] == 1
    grad = jnp.where(flip, turned_tile, tile)
    grad_t = jnp.where(flip, tile, turned_tile)
    grad_ref[0] = grad
    right_part = mm_full(grad, right[0], 1, 0)
    turned_ref[0] = mm_split(left[0], right_part, 0, 0)
    yr_ref[0] = mm_full(grad_t, right_part, 1, 0)
    yl_ref[0] = mm_full(grad, mm_full(grad_t, left[0], 1, 0), 1, 0)
    gl_ref[0] = mm_full(grad, grad_t, 1, 0)
    gr_ref[0] = mm_full(grad_t, grad, 1, 0)


def factor_inverses(grams):
    size = 64
    row = lax.broadcasted_iota(jnp.int32, (8, 128), 0)
    lane = lax.broadcasted_iota(jnp.int32, (8, 128), 1)
    states = []
    for gram in grams:
        wide = jnp.concatenate([gram, jnp.zeros((size, size), f32)], axis=1)
        states.append(
            [jnp.where(lane == row + (size + 8 * t), 1.0, wide[8 * t : 8 * t + 8, :]) for t in range(8)]
        )
    for k in range(size):
        home, at = divmod(k, 8)
        for tiles in states:
            pivot = tiles[home][at : at + 1, k : k + 1]
            line = tiles[home][at : at + 1, :] * (1.0 / pivot)
            for t in range(home, 8):
                update = tiles[t][:, k : k + 1] * line
                if t == home:
                    update = jnp.where(row > at, update, 0.0)
                tiles[t] = tiles[t] - update
    inverses = []
    for tiles in states:
        done = []
        for t in range(8):
            diagonal = jnp.sum(jnp.where(lane == row + 8 * t, tiles[t], 0.0), axis=1, keepdims=True)
            done.append(tiles[t] * lax.rsqrt(diagonal))
        inverses.append(jnp.concatenate(done, axis=0)[:, size:])
    return inverses


def soap_late(
    f_ref, grad, first, second, stat_l, stat_r, left, right, weight, turned, turned_first, xl, xr, yl, yr, gl, gr,
    weight_ref, first_ref, second_ref, sl_ref, sr_ref, left_ref, right_ref, low_ref, panels,
):
    factor = f_ref[0, 0]
    bias_one = 1.0 - first_decay**STEP
    bias_two = 1.0 - second_decay**STEP
    for n in range(3):
        first_ref[n] = first_decay * first[n] + (1.0 - first_decay) * (grad[n] * factor)
        rotated = turned[n] * factor
        second_new = second_decay * second[n] + (1.0 - second_decay) * rotated * rotated
        second_ref[n] = second_new
        scaled = (
            (first_decay * turned_first[n] + (1.0 - first_decay) * rotated)
            / bias_one
            / (jnp.sqrt(second_new / bias_two) + adam_epsilon)
        )
        back = mm_split(mm_split(left[n], scaled, 1, 0), right[n], 1, 1)
        weight_new = weight[n] * (1.0 - matrix_rate * weight_decay) - matrix_rate * back
        weight_ref[n] = weight_new
        low_ref[n] = weight_new.astype(bf16)
        sl_ref[n] = second_decay * stat_l[n] + (1.0 - second_decay) * (factor * (factor * gl[n]))
        sr_ref[n] = second_decay * stat_r[n] + (1.0 - second_decay) * (factor * (factor * gr[n]))
        for side, (old, new) in enumerate(((xl, yl), (xr, yr))):
            product = second_decay * old[n] + (1.0 - second_decay) * (factor * (factor * new[n]))
            for j in range(3):
                panels[2 * n + side, j] = product[:, 64 * j : 64 * j + 64]
    outs = (left_ref, right_ref)
    for j in range(3):
        inverses = factor_inverses([mm_full(panels[i, j], panels[i, j], 0, 0) for i in range(6)])
        for i in range(6):
            basis = mm_full(panels[i, j], inverses[i], 1, 1)
            outs[i % 2][i // 2, :, 64 * j : 64 * j + 64] = basis
            for k in range(j + 1, 3):
                panel = panels[i, k]
                panels[i, k] = panel - mm_full(basis, mm_full(basis, panel, 0, 0), 1, 0)


def tile_spec():
    return pl.BlockSpec((1, TILE, TILE), lambda i: (i, 0, 0))


def tiles_of_three(count):
    return [shape((3, TILE, TILE))] * count


def run_soap_early(first, stat_l, stat_r, left, right):
    return pl.pallas_call(
        soap_early, grid=(3,), in_specs=[tile_spec()] * 5, out_specs=[tile_spec()] * 3,
        out_shape=tiles_of_three(3), compiler_params=params(32), cost_estimate=cost(10**9, 4 * 10**6), name="soap_early",
    )(first, stat_l, stat_r, left, right)


def run_soap_mid(flips, packed, left, right):
    return pl.pallas_call(
        soap_mid, grid=(3,),
        in_specs=[SM, pl.BlockSpec((1, PACK, 128), lambda i: (i, 0, 0)), tile_spec(), tile_spec()],
        out_specs=[tile_spec()] * 6, out_shape=tiles_of_three(6),
        compiler_params=params(32), cost_estimate=cost(10**9, 4 * 10**6), name="soap_mid",
    )(flips, packed, left, right)


def run_soap_late(*args):
    return pl.pallas_call(
        soap_late, in_specs=[SM] + [VM] * 16, out_specs=[VM] * 8,
        out_shape=tiles_of_three(7) + [shape((3, TILE, TILE), bf16)],
        scratch_shapes=[pltpu.VMEM((6, 3, TILE, 64), f32)],
        compiler_params=params(56), cost_estimate=cost(10**9, 10**7), name="soap_late",
    )(*args)


def adamw(master, gradient, first, second, rate, decay):
    first_new = first_decay * first + (1.0 - first_decay) * gradient
    second_new = second_decay * second + (1.0 - second_decay) * gradient * gradient
    step_dir = (
        first_new
        / (1.0 - first_decay**STEP)
        / (jnp.sqrt(second_new / (1.0 - second_decay**STEP)) + adam_epsilon)
    )
    return (master * (1.0 - rate * decay) - rate * step_dir, first_new, second_new)


def swap(array, axis, r, size):
    return lax.ppermute(array, axis, [(i, i ^ r) for i in range(size)])


def swap_mp(array, r):
    return swap(array, "mp", r, 4)


def swap_dp(array, r):
    return swap(array, "dp", r, 32)


def gather_mp(array):
    return [array] + [swap_mp(array, r) for r in (1, 2, 3)]


def trade_mp(pieces):
    return [pieces[0]] + [swap_mp(pieces[r], r) for r in (1, 2, 3)]


def sum_four(pieces):
    return (pieces[0] + pieces[1]) + (pieces[2] + pieces[3])


def total_mp(array):
    return sum_four(gather_mp(array))


def total_dp(array):
    array = array + swap_dp(array, 1)
    array = sum_four([array] + [swap_dp(array, 2 * r) for r in (1, 2, 3)])
    return sum_four([array] + [swap_dp(array, 8 * r) for r in (1, 2, 3)])


def by_partner(array, index):
    return jnp.take(array, jnp.arange(array.shape[0]) ^ index, axis=0)


def shards(
    patches, image_ids, keep, labels, owners,
    soap_weight, soap_first, soap_second, stat_left, stat_right, basis_left, basis_right,
    embed_weight, embed_first, embed_second, head_weight, head_first, head_second,
    vectors, vector_first, vector_second,
):
    mp_index = lax.axis_index("mp")
    dp_index = lax.axis_index("dp")

    def tiled(flat_rows):
        return flat_rows.reshape(3, TILE, TILE)

    device, within = (owners // 3, owners % 3)
    partners = jnp.arange(4) ^ mp_index
    table = (device * 12 + within)[None, :] + 3 * partners[:, None]
    table = table.reshape(-1).astype(jnp.int32)
    relative = device ^ dp_index
    places = (((relative & 1) * 16 + (relative >> 1)) * 3 + within).astype(jnp.int32)
    my_slots = dp_index * 3 + jnp.arange(3)
    my_blocks = jnp.sum(
        jnp.where(owners[None, :] == my_slots[:, None], jnp.arange(96)[None, :], 0), axis=1
    )
    kind = my_blocks % 48
    grad_flips = (kind < 12).astype(jnp.int32)
    weight_flips = (kind < 12) | ((kind >= 16) & (kind < 32))

    master = tiled(soap_weight)
    low = master.astype(bf16)
    low = jnp.where(weight_flips[:, None, None], jnp.swapaxes(low, 1, 2), low)
    slots = lax.all_gather(pack_tile(low), ("dp", "mp"), axis=0, tiled=True)

    embed_parts = jnp.stack(gather_mp(embed_weight.astype(bf16)))
    embed_low = by_partner(embed_parts, mp_index).transpose(1, 0, 2).reshape(D, D)
    head_mine = head_weight.astype(bf16)
    head_low = by_partner(jnp.stack(gather_mp(head_mine)), mp_index).reshape(D, CLASSES)

    split_one = (2 * LAYERS + 1) * D
    gain_rows = vectors[:split_one].reshape(2 * LAYERS + 1, 1, D)
    head_gains = vectors[split_one : split_one + 2 * LAYERS * HD].reshape(LAYERS, 2, HD)
    class_bias = vectors[vectors.shape[0] - CLASSES :]

    tokens = by_partner(patches.reshape(4, OWN, D), mp_index)
    ids = by_partner(image_ids.reshape(4, OWN), mp_index)
    kept = by_partner(keep.reshape(4, OWN), mp_index) == 1
    query_ids = ids.reshape(1, TOKENS)
    key_ids = jnp.where(kept, ids, -1).reshape(TOKENS, 1)
    member_all = (image_ids[0, :, None] == jnp.arange(IMGS)[None, :]) & (keep[0, :, None] == 1)
    counts = jnp.sum(member_all.astype(f32), axis=0)
    present = (counts > 0).astype(f32)
    divisor = jnp.maximum(counts, 1.0)
    member = ((ids[0][:, None] == jnp.arange(IMGS)[None, :]) & kept[0][:, None]).astype(f32)
    image_total = total_dp(jnp.full((8, 128), jnp.sum(present), f32))[0, 0]

    first_tiles, second_tiles = (tiled(soap_first), tiled(soap_second))
    left_stat, right_stat = (tiled(stat_left), tiled(stat_right))
    left, right = (tiled(basis_left), tiled(basis_right))
    turned_first, left_old, right_old = run_soap_early(first_tiles, left_stat, right_stat, left, right)

    resid = jnp.dot(tokens[0], embed_low, preferred_element_type=f32).astype(bf16).astype(f32)
    act = (normalize(resid)[0] * gain_rows[0]).astype(bf16)

    weights = [layer_weights(table, slots, depth) for depth in range(LAYERS)]
    saved = []
    for depth in range(LAYERS):
        qkv, out, up, down = weights[depth]
        gains = head_gains[depth].T
        acts = gather_mp(act)
        pre, v, lse, o = run_attend_fwd(qkv, acts, gains, query_ids, key_ids)
        outs = trade_mp([o[r] for r in range(4)])
        mid, u, ct, resid_next, act = run_mix_fwd(
            resid, outs, out, gain_rows[2 * depth + 1], gain_rows[2 * depth + 2], up, down
        )
        saved.append((resid, acts, pre, v, lse, o, mid, u, gather_mp(ct)))
        resid = resid_next

    final, final_inverse = normalize(resid)
    gain_last = gain_rows[2 * LAYERS]
    pooled = total_mp(jnp.dot(member.T, final * gain_last, precision=highest)) / divisor[:, None]
    pooled_low = pooled.astype(bf16)
    logits = jnp.dot(pooled_low, head_low, preferred_element_type=f32) + class_bias
    row_max = jnp.max(logits, -1, keepdims=True)
    exps = jnp.exp(logits - row_max)
    row_sum = jnp.sum(exps, -1, keepdims=True)
    log_norm = row_max[:, 0] + jnp.log(row_sum[:, 0])
    onehot = (jnp.arange(CLASSES)[None, :] == labels.reshape(-1)[:, None]).astype(f32)
    local_loss = jnp.sum((log_norm - jnp.sum(onehot * logits, -1)) * present)
    loss_total = total_dp(jnp.full((8, 128), local_loss, f32))[0, 0]
    grad_logits = (exps / row_sum - onehot) * present[:, None] / image_total
    grad_bias = jnp.sum(grad_logits, 0)
    grad_logit_low = grad_logits.astype(bf16)
    pooled_mine = lax.dynamic_slice_in_dim(pooled_low, mp_index * TILE, TILE, 1)
    grad_head = jnp.dot(pooled_mine.T, grad_logit_low, preferred_element_type=f32)
    grad_pooled = jnp.dot(grad_logit_low, head_low.T, preferred_element_type=f32)
    grad_final = jnp.dot(member, grad_pooled / divisor[:, None], precision=highest)
    gain_grads = [jnp.sum(grad_final * final, 0)]
    grad = norm_back(grad_final, gain_last, final, final_inverse)
    grad_low = grad.astype(bf16)

    buffers = None
    head_gain_grads = []
    for depth in reversed(range(LAYERS)):
        qkv, out, up, down = weights[depth]
        resid, acts, pre, v, lse, o, mid, u, ct = saved[depth]
        gains = head_gains[depth].T
        lows = gather_mp(grad_low)
        du, mid_grad, mid_low, gain_two, do = run_mix_bwd(
            grad, grad_low, mid, u, gain_rows[2 * depth + 1], out, up, down
        )
        dos = trade_mp([do[r] for r in range(4)])
        dus = trade_mp([du[r] for r in range(4)])
        mid_lows = gather_mp(mid_low)
        dp, gain_heads = run_attend_bwd(pre, v, lse, dos, gains, query_ids, key_ids)
        dps = trade_mp([dp[r] for r in range(4)])
        grad, grad_low, gain_one = run_input_bwd(mid_grad, dps, qkv, resid, gain_rows[2 * depth])
        buffers = run_mlp_grads(depth, places, ct, dus, lows, mid_lows, o, up, buffers)
        buffers = run_qkv_grads(depth, places, dp, acts, buffers)
        gain_grads = [gain_one[0], gain_two[0]] + gain_grads
        head_gain_grads.insert(0, gain_heads.T)

    pieces = [
        lax.dynamic_slice_in_dim(grad_low, (mp_index ^ r) * TILE, TILE, 1) for r in range(4)
    ]
    columns = jnp.concatenate(trade_mp(pieces), axis=0)
    grad_embed = jnp.dot(tokens.reshape(TOKENS, D).T, columns, preferred_element_type=f32)
    embed_rows = pack_rows(grad_embed)
    head_rows = jnp.pad(grad_head, ((0, 0), (0, 24))).reshape(32, HEAD_ROWS, 128)
    vector_part = jnp.concatenate([jnp.concatenate(gain_grads), jnp.stack(head_gain_grads).reshape(-1)])
    vector_sum = jnp.concatenate([total_mp(vector_part), grad_bias, jnp.zeros((24,), f32)])
    vector_rows = jnp.pad(vector_sum.reshape(32, 160), ((0, 0), (0, 1536 - 160))).reshape(32, 12, 128)
    small = jnp.concatenate([embed_rows, head_rows, vector_rows], axis=1).astype(bf16)
    small = by_partner(small, dp_index).reshape(16, 2, SMALL, 128)
    keep_buffer = buffers[0].at[:, 3 * PACK :].set(small[:, 0])
    send_buffer = buffers[1].at[:, 3 * PACK :].set(small[:, 1])

    both = keep_buffer.astype(f32) + swap_dp(send_buffer, 1).astype(f32)
    both = both.reshape(4, 4, ROWS, 128)
    both = sum_four([both[0]] + [swap_dp(both[r].astype(bf16), 8 * r).astype(f32) for r in (1, 2, 3)])
    mine = sum_four([both[0]] + [swap_dp(both[r].astype(bf16), 2 * r).astype(f32) for r in (1, 2, 3)])
    mine_slots = mine[: 3 * PACK]
    share = mine[3 * PACK :]
    cut_at = EMBED_ROWS + HEAD_ROWS
    local_squares = (
        jnp.sum(mine_slots * mine_slots)
        + jnp.sum(share[:cut_at] * share[:cut_at])
        + jnp.sum(share[cut_at:] * share[cut_at:]) * 0.25
    )
    squares = total_dp(total_mp(jnp.full((8, 128), local_squares, f32)))[0, 0]
    grad_norm = jnp.sqrt(squares)
    factor = clip_limit / jnp.maximum(grad_norm, clip_limit)

    grad_tiles, turned, left_new, right_new, gram_left, gram_right = run_soap_mid(
        grad_flips, mine_slots.reshape(3, PACK, 128), left, right
    )
    soap_new = run_soap_late(
        factor.reshape(1, 1), grad_tiles, first_tiles, second_tiles, left_stat, right_stat, left, right, master,
        turned, turned_first, left_old, right_old, left_new, right_new, gram_left, gram_right,
    )
    soap_new = [entry.reshape(3, TILE * TILE) for entry in soap_new]

    shares = jnp.stack([share] + [swap_dp(share, 2 * r) for r in (1, 2, 3)])
    shares = jnp.stack([shares] + [swap_dp(shares, 8 * r) for r in (1, 2, 3)])
    shares = jnp.stack([shares, swap_dp(shares, 1)], axis=2).reshape(32, SMALL, 128)
    shares = by_partner(shares, dp_index)
    grad_embed = unpack_rows(shares[:, :EMBED_ROWS])
    grad_head = shares[:, EMBED_ROWS:cut_at].reshape(TILE, 1024)[:, :CLASSES]
    grad_vector = shares[:, cut_at:].reshape(32, 1536)[:, :160].reshape(-1)[: vectors.shape[0]]
    embed_new = adamw(
        embed_weight, grad_embed * factor, embed_first, embed_second, matrix_rate, weight_decay
    )
    head_new = adamw(
        head_weight, grad_head * factor, head_first, head_second, matrix_rate, weight_decay
    )
    vector_new = adamw(vectors, grad_vector * factor, vector_first, vector_second, vector_rate, 0.0)
    return (loss_total, image_total, grad_norm, *soap_new, *embed_new, *head_new, *vector_new)


def pack_rows(array):
    rows = array.reshape(32, 24, TILE)
    right = rows[:, :, 128:]
    right = jnp.concatenate([right[:, :12], right[:, 12:]], axis=2)
    return jnp.concatenate([rows[:, :, :128], right], axis=1)


def unpack_rows(packed):
    right = packed[:, 24:]
    right = jnp.concatenate([right[:, :, :64], right[:, :, 64:]], axis=1)
    return jnp.concatenate([packed[:, :24], right], axis=2).reshape(D, TILE)


def solution(mesh):
    by_slot = P(("dp", "mp"), None)
    columns = P(None, "mp")
    rows = P("mp", None)
    return jax.shard_map(
        shards,
        mesh=mesh,
        in_specs=(P("dp", None, None), P("dp", None), P("dp", None), P("dp", None), P())
        + (by_slot,) * 7
        + (columns,) * 3
        + (rows,) * 3
        + (P(),) * 3,
        out_specs=(P(),) * 3 + (by_slot,) * 8 + (columns,) * 3 + (rows,) * 3 + (P(),) * 3,
        check_vma=False,
    )
```

```python
import jax
import jax.numpy as jnp
from jax import lax
from jax.experimental import pallas as pl
from jax.experimental.pallas import tpu as pltpu
from jax.sharding import PartitionSpec as P

D = 768
HD = 64
HEADS = 3
CLASSES = 1000
LAYERS = 2
IMGS = 8
STEP = 10
TILE = 192
TOKENS = 1024
OWN = 256
PACK = 288
SMALL = 96
ROWS = 3 * PACK + SMALL
EMBED_ROWS = 36
HEAD_ROWS = 48

first_decay = 0.9
second_decay = 0.95
weight_decay = 0.05
matrix_rate = 0.03
vector_rate = 0.3
clip_limit = 0.01
adam_epsilon = 1e-08
norm_epsilon = 1e-06
masked_score = -1e30
highest = lax.Precision.HIGHEST
f32 = jnp.float32
bf16 = jnp.bfloat16
MIB = 2**20
VM = pl.BlockSpec(memory_space=pltpu.VMEM)
SM = pl.BlockSpec(memory_space=pltpu.SMEM)
ANY = pl.BlockSpec(memory_space=pl.ANY)


def params(mib):
    return pltpu.CompilerParams(vmem_limit_bytes=mib * MIB)


def cost(flops, moved, exps=0):
    return pl.CostEstimate(flops=flops, bytes_accessed=moved, transcendentals=exps)


def shape(dims, kind=f32):
    return jax.ShapeDtypeStruct(dims, kind)


def mm(a, b, ca=1, cb=0):
    return lax.dot_general(a, b, (((ca,), (cb,)), ((), ())), preferred_element_type=f32)


def mm_full(a, b, ca, cb):
    return lax.dot_general(
        a, b, (((ca,), (cb,)), ((), ())), precision=highest, preferred_element_type=f32
    )


def mm_split(a, b, ca, cb):
    a_high, b_high = (a.astype(bf16), b.astype(bf16))
    a_low = (a - a_high.astype(f32)).astype(bf16)
    b_low = (b - b_high.astype(f32)).astype(bf16)
    return mm(a_high, b_high, ca, cb) + (mm(a_high, b_low, ca, cb) + mm(a_low, b_high, ca, cb))


def normalize(values):
    centered = values - jnp.mean(values, -1, keepdims=True)
    inverse = lax.rsqrt(jnp.mean(centered * centered, -1, keepdims=True) + norm_epsilon)
    return centered * inverse, inverse


def norm_back(grad, gain, normed, inverse):
    scaled = grad * gain
    return inverse * (
        scaled
        - jnp.mean(scaled, -1, keepdims=True)
        - normed * jnp.mean(scaled * normed, -1, keepdims=True)
    )


def gauss_parts(value):
    size = jnp.abs(value) * 0.7071067811865476
    bell = jnp.exp(-size * size)
    t = 1.0 / (1.0 + 0.3275911 * size)
    poly = t * (
        0.254829592
        + t * (-0.284496736 + t * (1.421413741 + t * (-1.453152027 + t * 1.061405429)))
    )
    tail = 0.5 * poly * bell
    return jnp.where(value >= 0, 1.0 - tail, tail), bell


def gelu(value):
    return value * gauss_parts(value)[0]


def widen(parts, axis):
    return jnp.concatenate(
        [lax.slice_in_dim(x, 0, 128, axis=axis) for x in parts]
        + [lax.slice_in_dim(x, 128, TILE, axis=axis) for x in parts],
        axis=axis,
    )


def wide_part(array, k, axis):
    return jnp.concatenate(
        [
            lax.dynamic_slice_in_dim(array, 128 * k, 128, axis),
            lax.dynamic_slice_in_dim(array, 512 + 64 * k, 64, axis),
        ],
        axis=axis,
    )


def wide_back(vector):
    return jnp.concatenate([vector[:512].reshape(4, 128), vector[512:].reshape(4, 64)], axis=1).reshape(D)


def pack_tile(tile):
    half = TILE // 2
    right = tile[..., 128:]
    return jnp.concatenate(
        [
            tile[..., :128],
            jnp.concatenate([right[..., :half, :], right[..., half:, :]], axis=-1),
        ],
        axis=-2,
    )


def unpack_tile(packed):
    half = TILE // 2
    right = packed[..., TILE:, :]
    return jnp.concatenate(
        [
            packed[..., :TILE, :],
            jnp.concatenate([right[..., :64], right[..., 64:]], axis=-2),
        ],
        axis=-1,
    )


def assemble(table, slots, groups):
    half = TILE // 2
    sizes = [4 * len(group) for group in groups]
    lines = sum(sizes)
    wanted = [96 * r + block for group in groups for r in range(4) for line in group for block in line]

    def kernel(table_ref, slots_ref, *refs):
        outs = refs[: len(groups)]
        tiles, stage, in_sems, out_sems = refs[len(groups) :]

        def fetch(at, place):
            return pltpu.make_async_copy(slots_ref.at[place], tiles.at[at], in_sems.at[at])

        for at, entry in enumerate(wanted):
            fetch(at, table_ref[entry]).start()
        base = 0
        for out_ref, size in zip(outs, sizes):

            def step(line, carry):
                at = base + line
                for t in range(4):
                    fetch(4 * at + t, 0).wait()
                for t in range(4):
                    stage[at, :, 128 * t : 128 * t + 128] = tiles[4 * at + t, :TILE]
                for t in (0, 2):
                    first = tiles[4 * at + t, TILE:]
                    second = tiles[4 * at + t + 1, TILE:]
                    cols = slice(512 + 64 * t, 640 + 64 * t)
                    stage[at, :half, cols] = jnp.concatenate([first[:, :64], second[:, :64]], axis=1)
                    stage[at, half:, cols] = jnp.concatenate([first[:, 64:], second[:, 64:]], axis=1)
                pltpu.make_async_copy(stage.at[at], out_ref.at[line], out_sems.at[at]).start()
                return carry

            lax.fori_loop(0, size, step, 0)
            base += size
        base = 0
        for out_ref, size in zip(outs, sizes):

            def finish(line, carry):
                pltpu.make_async_copy(stage.at[base + line], out_ref.at[line], out_sems.at[base + line]).wait()
                return carry

            lax.fori_loop(0, size, finish, 0)
            base += size

    mats = pl.pallas_call(
        kernel,
        in_specs=[SM, ANY],
        out_specs=[ANY] * len(groups),
        out_shape=[shape((size, TILE, D), bf16) for size in sizes],
        scratch_shapes=[
            pltpu.VMEM((4 * lines, PACK, 128), bf16),
            pltpu.VMEM((lines, TILE, D), bf16),
            pltpu.SemaphoreType.DMA((4 * lines,)),
            pltpu.SemaphoreType.DMA((lines,)),
        ],
        compiler_params=params(60),
        cost_estimate=cost(0, 4 * lines * TILE * TILE * 4),
        name="assemble",
    )(table, slots)
    return [mat.reshape(4, len(group) * TILE, D) for mat, group in zip(mats, groups)]


def layer_blocks(depth):
    base = 48 * depth
    qkv = [[base + 3 * r + c for r in range(4)] for c in range(3)]
    out = [[base + 12 + t for t in range(4)]]
    up = [[base + 16 + 4 * r + t for r in range(4)] for t in range(4)]
    down = [[base + 32 + 4 * t + r for r in range(4)] for t in range(4)]
    return [qkv, out, up, down]


def column_norm(values):
    centered = values - jnp.mean(values, 0, keepdims=True)
    inverse = lax.rsqrt(jnp.mean(centered * centered, 0, keepdims=True) + norm_epsilon)
    return centered * inverse, inverse


def attend_fwd(w_ref, a0, a1, a2, a3, gain_ref, qid_ref, kid_ref, pre_ref, v_ref, lse_ref, o0, o1, o2, o3, q_s, k_s, o_s):
    for c in range(3):
        for r, a_ref in enumerate((a0, a1, a2, a3)):
            cols = slice(OWN * r, OWN * r + OWN)
            part = mm(w_ref[0, TILE * c : TILE * c + TILE, :], a_ref[...], 1, 1)
            if c == 2:
                v_ref[:, cols] = part.astype(bf16)
                continue
            pre_ref[TILE * c : TILE * c + TILE, cols] = part
            for h in range(HEADS):
                rows = slice(HD * h, HD * h + HD)
                low = (column_norm(part[rows, :])[0] * gain_ref[:, c : c + 1]).astype(bf16)
                if c == 0:
                    q_s[r, rows, :] = low * bf16(0.125)
                else:
                    k_s[h, cols, :] = low.T

    def step(i, carry):
        h, t = (i // 4, i % 4)
        rows = pl.ds(pl.multiple_of(h * HD, HD), HD)
        cols = pl.ds(pl.multiple_of(t * OWN, OWN), OWN)
        scores = mm(k_s[h], q_s[t, rows, :])
        scores = jnp.where(kid_ref[...] == qid_ref[:, cols], scores, masked_score)
        top = jnp.max(scores, 0, keepdims=True)
        weights = jnp.exp(scores - top)
        total = jnp.sum(weights, 0, keepdims=True)
        lse_ref[h, :, cols] = top + jnp.log(total)
        probs = (weights * (1.0 / total)).astype(bf16)
        o_s[t, rows, :] = mm(v_ref[rows, :], probs).astype(bf16)
        return carry

    lax.fori_loop(0, 4 * HEADS, step, 0)
    for r, ref in enumerate((o0, o1, o2, o3)):
        ref[...] = o_s[r]


def run_attend_fwd(w, acts, gains, qid, kid):
    return pl.pallas_call(
        attend_fwd,
        grid=(1,),
        in_specs=[pl.BlockSpec((1, 3 * TILE, D), lambda i: (0, 0, 0))] + [VM] * 7,
        out_specs=[VM] * 7,
        out_shape=[
            shape((2 * TILE, TOKENS)),
            shape((TILE, TOKENS), bf16),
            shape((HEADS, 1, TOKENS)),
        ]
        + [shape((TILE, OWN), bf16)] * 4,
        scratch_shapes=[
            pltpu.VMEM((4, TILE, OWN), bf16),
            pltpu.VMEM((HEADS, TOKENS, HD), bf16),
            pltpu.VMEM((4, TILE, OWN), bf16),
        ],
        compiler_params=params(60),
        cost_estimate=cost(10**10, 6 * 10**6, 3 * 2**20),
        name="attend_fwd",
    )(w, *acts, gains, qid, kid)


def attend_bwd(
    pre_ref, v_ref, lse_ref, g0, g1, g2, g3, gain_ref, qid_ref, kid_ref,
    p0, p1, p2, p3, dgain_ref, q_s, qn_s, k_s, kt_s, vn_s, do_s, dq_s, dk_s, dv_s,
):
    dp_refs = (p0, p1, p2, p3)
    for r, ref in enumerate((g0, g1, g2, g3)):
        do_s[r] = ref[...]
    for h in range(HEADS):
        rows = slice(HD * h, HD * h + HD)
        low = (column_norm(pre_ref[rows, :])[0] * gain_ref[:, 0:1]).astype(bf16)
        q_s[rows, :] = low * bf16(0.125)
        qn_s[h] = q_s[rows, :].T
        low = (column_norm(pre_ref[TILE + HD * h : TILE + HD * h + HD, :])[0] * gain_ref[:, 1:2]).astype(bf16)
        kt_s[rows, :] = low
        k_s[h] = low.T
        vn_s[h] = v_ref[rows, :].T
    dk_s[...] = jnp.zeros_like(dk_s)
    dv_s[...] = jnp.zeros_like(dv_s)

    def step(i, carry):
        h, t = (i // 4, i % 4)
        rows = pl.ds(pl.multiple_of(h * HD, HD), HD)
        cols = pl.ds(pl.multiple_of(t * OWN, OWN), OWN)
        scores = mm(k_s[h], q_s[rows, cols])
        scores = jnp.where(kid_ref[...] == qid_ref[:, cols], scores, masked_score)
        weights = jnp.exp(scores - lse_ref[h, :, cols])
        grad_out = do_s[t, rows, :]
        grad_weights = mm(vn_s[h], grad_out)
        dv_s[h] += mm(weights.astype(bf16), grad_out.T)
        inner = jnp.sum(weights * grad_weights, 0, keepdims=True)
        grad_scores = (weights * (grad_weights - inner)).astype(bf16)
        dq_s[rows, cols] = mm(kt_s[rows, :], grad_scores) * 0.125
        dk_s[h] += mm(grad_scores, qn_s[h, cols, :])
        return carry

    lax.fori_loop(0, 4 * HEADS, step, 0)
    for c in range(2):
        total = jnp.zeros((HD, 1), f32)
        for h in range(HEADS):
            grad = dq_s[HD * h : HD * h + HD, :] if c == 0 else dk_s[h].T
            base = TILE * c + HD * h
            normed, inverse = column_norm(pre_ref[base : base + HD, :])
            total = total + jnp.sum(grad * normed, 1, keepdims=True)
            scaled = grad * gain_ref[:, c : c + 1]
            back = inverse * (
                scaled
                - jnp.mean(scaled, 0, keepdims=True)
                - normed * jnp.mean(scaled * normed, 0, keepdims=True)
            )
            for r in range(4):
                dp_refs[r][base : base + HD, :] = back[:, OWN * r : OWN * r + OWN].astype(bf16)
        dgain_ref[:, c : c + 1] = total
    for h in range(HEADS):
        back = dv_s[h].T.astype(bf16)
        for r in range(4):
            dp_refs[r][2 * TILE + HD * h : 2 * TILE + HD * h + HD, :] = back[:, OWN * r : OWN * r + OWN]


def run_attend_bwd(pre, v, lse, grads, gains, qid, kid):
    return pl.pallas_call(
        attend_bwd,
        in_specs=[VM] * 10,
        out_specs=[VM] * 5,
        out_shape=[shape((3 * TILE, OWN), bf16)] * 4 + [shape((HD, 2))],
        scratch_shapes=[
            pltpu.VMEM((TILE, TOKENS), bf16),
            pltpu.VMEM((HEADS, TOKENS, HD), bf16),
            pltpu.VMEM((HEADS, TOKENS, HD), bf16),
            pltpu.VMEM((TILE, TOKENS), bf16),
            pltpu.VMEM((HEADS, TOKENS, HD), bf16),
            pltpu.VMEM((4, TILE, OWN), bf16),
            pltpu.VMEM((TILE, TOKENS), f32),
            pltpu.VMEM((HEADS, TOKENS, HD), f32),
            pltpu.VMEM((HEADS, TOKENS, HD), f32),
        ],
        compiler_params=params(48),
        cost_estimate=cost(2 * 10**10, 6 * 10**6, 3 * 2**20),
        name="attend_bwd",
    )(pre, v, lse, *grads, gains, qid, kid)


def mix_fwd(x_ref, o0, o1, o2, o3, w_out, gain_ref, next_ref, up_ref, down_ref,
            mid_ref, u_ref, c_ref, x_out, a_out):
    r = pl.program_id(0)

    @pl.when(r == 0)
    def _():
        mid = x_ref[...]
        for k, ref in enumerate((o0, o1, o2, o3)):
            mid = mid + mm(ref[...], w_out[TILE * k : TILE * k + TILE, :], 0, 0)
        mid_ref[...] = mid
        low = (normalize(mid)[0] * gain_ref[...]).astype(bf16)
        c_ref[...] = low
        x_out[...] = mid

    u = mm(c_ref[...], up_ref[0], 1, 1)
    u_ref[0] = u
    x_out[...] += mm(gelu(u).astype(bf16), down_ref[0])

    @pl.when(r == 3)
    def _():
        a_out[...] = (normalize(x_out[...])[0] * next_ref[...]).astype(bf16)


def whole(*dims):
    return pl.BlockSpec(dims, lambda r: (0,) * len(dims))


def part(*dims):
    return pl.BlockSpec((1, *dims), lambda r: (r,) + (0,) * len(dims))


def run_mix_fwd(x, outs, w_out, gain, gain_next, up, down):
    return pl.pallas_call(
        mix_fwd,
        grid=(4,),
        in_specs=[whole(OWN, D)] + [whole(TILE, OWN)] * 4 + [whole(D, D), whole(1, D), whole(1, D), part(D, D), part(D, D)],
        out_specs=[whole(OWN, D), part(OWN, D), whole(OWN, D), whole(OWN, D), whole(OWN, D)],
        out_shape=[shape((OWN, D)), shape((4, OWN, D)), shape((OWN, D), bf16), shape((OWN, D)), shape((OWN, D), bf16)],
        compiler_params=params(60),
        cost_estimate=cost(6 * 10**9, 17 * 10**6, 10**6),
        name="mix_fwd",
    )(x, *outs, w_out, gain, gain_next, up, down)


def mix_bwd(g_ref, low_ref, mid_ref, u_ref, gain_ref, w_out, up_ref, down_ref,
            mid_grad, mid_low, dgain_ref, do0, do1, do2, do3, acc):
    r = pl.program_id(0)

    @pl.when(r == 0)
    def _():
        acc[...] = jnp.zeros_like(acc)

    df = mm(low_ref[...], down_ref[0], 1, 1)
    u = u_ref[0]
    cdf, bell = gauss_parts(u)
    du = (df * (cdf + u * bell * 0.3989422804014327)).astype(bf16)
    acc[...] += mm(du, up_ref[0])

    @pl.when(r == 3)
    def _():
        normed, inverse = normalize(mid_ref[...])
        grad = acc[...]
        dgain_ref[...] = jnp.sum(grad * normed, 0, keepdims=True)
        total = g_ref[...] + norm_back(grad, gain_ref[...], normed, inverse)
        mid_grad[...] = total
        low = total.astype(bf16)
        mid_low[...] = low
        for k, ref in enumerate((do0, do1, do2, do3)):
            ref[...] = mm(w_out[TILE * k : TILE * k + TILE, :], low, 1, 1).astype(bf16)


def run_mix_bwd(grad, grad_low, mid, u, gain, w_out, up, down):
    return pl.pallas_call(
        mix_bwd,
        grid=(4,),
        in_specs=[whole(OWN, D), whole(OWN, D), whole(OWN, D), part(OWN, D), whole(1, D), whole(D, D), part(D, D), part(D, D)],
        out_specs=[whole(OWN, D), whole(OWN, D), whole(1, D)] + [whole(TILE, OWN)] * 4,
        out_shape=[shape((OWN, D)), shape((OWN, D), bf16), shape((1, D))] + [shape((TILE, OWN), bf16)] * 4,
        scratch_shapes=[pltpu.VMEM((OWN, D), f32)],
        compiler_params=params(60),
        cost_estimate=cost(6 * 10**9, 17 * 10**6, 10**6),
        name="mix_bwd",
    )(grad, grad_low, mid, u, gain, w_out, up, down)


def input_bwd(mid_grad, d0, d1, d2, d3, w_ref, x_ref, gain_ref, grad_ref, low_ref, dgain_ref):
    grad = mm(d0[...], w_ref[0], 0, 0)
    for k, ref in ((1, d1), (2, d2), (3, d3)):
        grad = grad + mm(ref[...], w_ref[k], 0, 0)
    normed, inverse = normalize(x_ref[...])
    dgain_ref[...] = jnp.sum(grad * normed, 0, keepdims=True)
    total = mid_grad[...] + norm_back(grad, gain_ref[...], normed, inverse)
    grad_ref[...] = total
    low_ref[...] = total.astype(bf16)


def run_input_bwd(mid_grad, grads, w, x, gain):
    return pl.pallas_call(
        input_bwd,
        in_specs=[VM] * 8,
        out_specs=[VM] * 3,
        out_shape=[shape((OWN, D)), shape((OWN, D), bf16), shape((1, D))],
        compiler_params=params(48),
        cost_estimate=cost(10**9, 6 * 10**6),
        name="input_bwd",
    )(mid_grad, *grads, w, x, gain)


def pack_wide(line, t):
    half = TILE // 2
    right = line[:, 512 + 64 * t : 576 + 64 * t]
    return jnp.concatenate(
        [
            line[:, 128 * t : 128 * t + 128],
            jnp.concatenate([right[:half], right[half:]], axis=1),
        ],
        axis=0,
    )


def send_line(places, stage, sems, keep, send, line, blocks, base):
    line = line.astype(bf16)
    for t, block in enumerate(blocks):
        at = base + t
        stage[at] = pack_wide(line, t)
        place = places[block]
        rows = pl.ds(pl.multiple_of((place % 3) * PACK, 16), PACK)

        @pl.when(place < 48)
        def _():
            pltpu.make_async_copy(stage.at[at], keep.at[place // 3, rows], sems.at[at]).start()

        @pl.when(place >= 48)
        def _():
            pltpu.make_async_copy(stage.at[at], send.at[place // 3 - 16, rows], sems.at[at]).start()


def wait_tiles(stage, sems, keep, count):
    for at in range(count):
        pltpu.make_async_copy(stage.at[at], keep.at[0, pl.ds(0, PACK)], sems.at[at]).wait()


def mlp_grads(depth, places, act_ref, low_ref, up_ref, down_ref, *refs):
    keep, send, token, stage, sems = refs[-5:]
    base = 48 * depth
    for i in range(4):
        rows = slice(TILE * i, TILE * i + TILE)
        u = mm(up_ref[0, rows, :], act_ref[...], 1, 1)
        df = mm(down_ref[0, rows, :], low_ref[...], 1, 1)
        cdf, bell = gauss_parts(u)
        f_low = (u * cdf).astype(bf16)
        du_low = (df * (cdf + u * bell * 0.3989422804014327)).astype(bf16)
        line = mm(du_low, act_ref[...])
        send_line(places, stage, sems, keep, send, line, [base + 16 + 4 * t + i for t in range(4)], 4 * i)
        line = mm(f_low, low_ref[...])
        send_line(places, stage, sems, keep, send, line, [base + 32 + 4 * i + t for t in range(4)], 16 + 4 * i)
    token[...] = jnp.zeros_like(token)
    wait_tiles(stage, sems, keep, 32)


def head_grads(depth, places, index, mid_ref, *refs):
    outs, grads, acts = (refs[0:4], refs[4:8], refs[8:12])
    keep, send, token, stage, sems = refs[-5:]
    base = 48 * depth
    parts = []
    for r in range(4):
        rows = pl.ds(pl.multiple_of((index[0] ^ r) * OWN, OWN), OWN)
        parts.append(mm(outs[r][...], mid_ref[rows, :]))
    line = (parts[0] + parts[1]) + (parts[2] + parts[3])
    send_line(places, stage, sems, keep, send, line, [base + 12 + t for t in range(4)], 12)
    for c in range(3):
        rows = slice(TILE * c, TILE * c + TILE)
        parts = [mm(grads[r][rows, :], acts[r][...]) for r in range(4)]
        line = (parts[0] + parts[1]) + (parts[2] + parts[3])
        send_line(places, stage, sems, keep, send, line, [base + 3 * t + c for t in range(4)], 4 * c)
    token[...] = jnp.zeros_like(token)
    wait_tiles(stage, sems, keep, 16)


def grads_call(kernel, name, scalars, args, specs, buffers, count, flops):
    given = list(buffers) if buffers is not None else []
    first = len(scalars) + len(args)
    *buffers, token = pl.pallas_call(
        kernel,
        grid=(1,),
        in_specs=[SM] * len(scalars) + specs + [ANY] * len(given),
        out_specs=[ANY, ANY, VM],
        out_shape=[shape((16, ROWS, 128), bf16)] * 2 + [shape((8, 128))],
        input_output_aliases={first + i: i for i in range(len(given))},
        scratch_shapes=[pltpu.VMEM((count, PACK, 128), bf16), pltpu.SemaphoreType.DMA((count,))],
        compiler_params=params(56),
        cost_estimate=cost(flops, 10**7),
        name=name,
    )(*scalars, *args, *given)
    return buffers, token


def run_mlp_grads(depth, places, act, low, up, down, buffers):
    first = pl.BlockSpec((1, D, D), lambda i: (0, 0, 0))
    return grads_call(
        lambda *refs: mlp_grads(depth, *refs), "mlp_grads", [places],
        [act, low, up, down], [VM] * 2 + [first] * 2, buffers, 32, 5 * 10**9,
    )


def run_head_grads(depth, places, index, mid_low, outs, grads, acts, buffers):
    return grads_call(
        lambda *refs: head_grads(depth, *refs), "head_grads", [places, index],
        [mid_low, *outs, *grads, *acts], [VM] * 13, buffers, 16, 2 * 10**9,
    )


def add_core(keep, got, own_a, a1, a2, a3, own_b, b1, b2, b3):
    step = pl.program_id(0)
    half = ROWS // 2
    total = keep[...].astype(f32) + got[...].astype(f32)

    @pl.when(step == 0)
    def _():
        own_a[...] = total[:, :half]

    for k, ref in ((1, a1), (2, a2), (3, a3)):

        @pl.when(step == k)
        def _():
            ref[...] = total[:, :half].astype(bf16)

    own_b[0] = total[0, half:]
    for k, ref in ((1, b1), (2, b2), (3, b3)):
        ref[0] = total[k, half:].astype(bf16)


def run_add_core(keep, got):
    half = ROWS // 2
    block = pl.BlockSpec((4, ROWS, 128), lambda r: (r, 0, 0))
    one, many = (whole(4, half, 128), part(half, 128))
    return pl.pallas_call(
        add_core, grid=(4,), in_specs=[block] * 2, out_specs=[one] * 4 + [many] * 4,
        out_shape=([shape((4, half, 128))] + [shape((4, half, 128), bf16)] * 3) * 2,
        compiler_params=params(32), cost_estimate=cost(10**7, 14 * 10**6), name="add_core",
    )(keep, got)


def add_axis(*refs):
    ins, outs = (refs[:8], refs[8:])
    for side in range(2):
        own, r1, r2, r3 = ins[4 * side : 4 * side + 4]
        for k in range(4):
            total = (own[k] + r1[k].astype(f32)) + (r2[k].astype(f32) + r3[k].astype(f32))
            out = outs[4 * side + k]
            out[...] = total.astype(out.dtype)


def run_add_axis(a, b):
    half = ROWS // 2
    return pl.pallas_call(
        add_axis, in_specs=[VM] * 8, out_specs=[VM] * 8,
        out_shape=([shape((half, 128))] + [shape((half, 128), bf16)] * 3) * 2,
        compiler_params=params(32), cost_estimate=cost(10**7, 6 * 10**6), name="add_axis",
    )(*a, *b)


def gate(array, *others):
    return pl.pallas_call(
        lambda *refs: None, in_specs=[ANY] * (1 + len(others)), out_specs=ANY,
        out_shape=shape(array.shape, array.dtype), input_output_aliases={0: 0},
        compiler_params=params(16), name="gate",
    )(array, *others)


def soap_early(first, stat_l, stat_r, left, right, turned_ref, l_ref, r_ref):
    turned_ref[0] = mm_split(mm_split(left[0], first[0], 0, 0), right[0], 1, 0)
    l_ref[0] = mm_full(stat_l[0], left[0], 1, 0)
    r_ref[0] = mm_full(stat_r[0], right[0], 1, 0)


def soap_mid(flip_ref, packed, left, right, grad_ref, turned_ref, yl_ref, yr_ref, gl_ref, gr_ref):
    tile = unpack_tile(packed[0])
    turned_tile = tile.T
    flip = flip_ref[pl.program_id(0)] == 1
    grad = jnp.where(flip, turned_tile, tile)
    grad_t = jnp.where(flip, tile, turned_tile)
    grad_ref[0] = grad
    right_part = mm_full(grad, right[0], 1, 0)
    turned_ref[0] = mm_split(left[0], right_part, 0, 0)
    yr_ref[0] = mm_full(grad_t, right_part, 1, 0)
    yl_ref[0] = mm_full(grad, mm_full(grad_t, left[0], 1, 0), 1, 0)
    gl_ref[0] = mm_full(grad, grad_t, 1, 0)
    gr_ref[0] = mm_full(grad_t, grad, 1, 0)


def factor_inverses(grams):
    size = 64
    row = lax.broadcasted_iota(jnp.int32, (8, 128), 0)
    lane = lax.broadcasted_iota(jnp.int32, (8, 128), 1)
    states = []
    for gram in grams:
        wide = jnp.concatenate([gram, jnp.zeros((size, size), f32)], axis=1)
        states.append(
            [jnp.where(lane == row + (size + 8 * t), 1.0, wide[8 * t : 8 * t + 8, :]) for t in range(8)]
        )
    for k in range(size):
        home, at = divmod(k, 8)
        for tiles in states:
            pivot = tiles[home][at : at + 1, k : k + 1]
            line = tiles[home][at : at + 1, :] * (1.0 / pivot)
            for t in range(home, 8):
                update = tiles[t][:, k : k + 1] * line
                if t == home:
                    update = jnp.where(row > at, update, 0.0)
                tiles[t] = tiles[t] - update
    inverses = []
    for tiles in states:
        done = []
        for t in range(8):
            diagonal = jnp.sum(jnp.where(lane == row + 8 * t, tiles[t], 0.0), axis=1, keepdims=True)
            done.append(tiles[t] * lax.rsqrt(diagonal))
        inverses.append(jnp.concatenate(done, axis=0)[:, size:])
    return inverses


def soap_late(
    f_ref, second, left, right, weight, turned, turned_first, xl, xr, yl, yr,
    weight_ref, left_ref, right_ref, low_ref, panels,
):
    factor = f_ref[0, 0]
    bias_one = 1.0 - first_decay**STEP
    bias_two = 1.0 - second_decay**STEP
    for n in range(3):
        rotated = turned[n] * factor
        second_new = second_decay * second[n] + (1.0 - second_decay) * rotated * rotated
        scaled = (
            (first_decay * turned_first[n] + (1.0 - first_decay) * rotated)
            / bias_one
            / (jnp.sqrt(second_new / bias_two) + adam_epsilon)
        )
        back = mm_split(mm_split(left[n], scaled, 1, 0), right[n], 1, 1)
        weight_new = weight[n] * (1.0 - matrix_rate * weight_decay) - matrix_rate * back
        weight_ref[n] = weight_new
        low_ref[n] = weight_new.astype(bf16)
        for side, (old, new) in enumerate(((xl, yl), (xr, yr))):
            product = second_decay * old[n] + (1.0 - second_decay) * (factor * (factor * new[n]))
            for j in range(3):
                panels[2 * n + side, j] = product[:, 64 * j : 64 * j + 64]
    outs = (left_ref, right_ref)
    for j in range(3):
        inverses = factor_inverses([mm_full(panels[i, j], panels[i, j], 0, 0) for i in range(6)])
        for i in range(6):
            basis = mm_full(panels[i, j], inverses[i], 1, 1)
            outs[i % 2][i // 2, :, 64 * j : 64 * j + 64] = basis
            for k in range(j + 1, 3):
                panel = panels[i, k]
                panels[i, k] = panel - mm_full(basis, mm_full(basis, panel, 0, 0), 1, 0)


def tile_spec():
    return pl.BlockSpec((1, TILE, TILE), lambda i: (i, 0, 0))


def tiles_of_three(count):
    return [shape((3, TILE, TILE))] * count


def run_soap_early(first, stat_l, stat_r, left, right):
    return pl.pallas_call(
        soap_early, grid=(3,), in_specs=[tile_spec()] * 5, out_specs=[tile_spec()] * 3,
        out_shape=tiles_of_three(3), compiler_params=params(32), cost_estimate=cost(10**9, 4 * 10**6), name="soap_early",
    )(first, stat_l, stat_r, left, right)


def run_soap_mid(flips, packed, left, right):
    return pl.pallas_call(
        soap_mid, grid=(3,),
        in_specs=[SM, pl.BlockSpec((1, PACK, 128), lambda i: (i, 0, 0)), tile_spec(), tile_spec()],
        out_specs=[tile_spec()] * 6, out_shape=tiles_of_three(6),
        compiler_params=params(32), cost_estimate=cost(10**9, 4 * 10**6), name="soap_mid",
    )(flips, packed, left, right)


def run_soap_late(*args):
    return pl.pallas_call(
        soap_late, in_specs=[SM] + [VM] * 10, out_specs=[VM] * 4,
        out_shape=tiles_of_three(3) + [shape((3, TILE, TILE), bf16)],
        scratch_shapes=[pltpu.VMEM((6, 3, TILE, 64), f32)],
        compiler_params=params(56), cost_estimate=cost(10**9, 10**7), name="soap_late",
    )(*args)


def adamw(master, gradient, first, second, rate, decay):
    first_new = first_decay * first + (1.0 - first_decay) * gradient
    second_new = second_decay * second + (1.0 - second_decay) * gradient * gradient
    step_dir = (
        first_new
        / (1.0 - first_decay**STEP)
        / (jnp.sqrt(second_new / (1.0 - second_decay**STEP)) + adam_epsilon)
    )
    return (master * (1.0 - rate * decay) - rate * step_dir, first_new, second_new)


def swap(array, axis, r, size):
    return lax.ppermute(array, axis, [(i, i ^ r) for i in range(size)])


def swap_mp(array, r):
    return swap(array, "mp", r, 4)


def swap_dp(array, r):
    return swap(array, "dp", r, 32)


def gather_mp(array):
    return [array] + [swap_mp(array, r) for r in (1, 2, 3)]


def trade_mp(pieces):
    return [pieces[0]] + [swap_mp(pieces[r], r) for r in (1, 2, 3)]


def sum_four(pieces):
    return (pieces[0] + pieces[1]) + (pieces[2] + pieces[3])


def total_mp(array):
    return sum_four(gather_mp(array))


def total_dp(array):
    array = array + swap_dp(array, 1)
    array = sum_four([array] + [swap_dp(array, 2 * r) for r in (1, 2, 3)])
    return sum_four([array] + [swap_dp(array, 8 * r) for r in (1, 2, 3)])


def by_partner(array, index):
    return jnp.take(array, jnp.arange(array.shape[0]) ^ index, axis=0)


def shards(
    patches, image_ids, keep, labels, owners,
    soap_weight, soap_first, soap_second, stat_left, stat_right, basis_left, basis_right,
    embed_weight, embed_first, embed_second, head_weight, head_first, head_second,
    vectors, vector_first, vector_second,
):
    mp_index = lax.axis_index("mp")
    dp_index = lax.axis_index("dp")

    def tiled(flat_rows):
        return flat_rows.reshape(3, TILE, TILE)

    device, within = (owners // 3, owners % 3)
    partners = jnp.arange(4) ^ mp_index
    table = (device * 12 + within)[None, :] + 3 * partners[:, None]
    table = table.reshape(-1).astype(jnp.int32)
    relative = device ^ dp_index
    places = (((relative & 1) * 16 + (relative >> 1)) * 3 + within).astype(jnp.int32)
    my_slots = dp_index * 3 + jnp.arange(3)
    my_blocks = jnp.sum(
        jnp.where(owners[None, :] == my_slots[:, None], jnp.arange(96)[None, :], 0), axis=1
    )
    kind = my_blocks % 48
    flips = (kind < 12) | ((kind >= 16) & (kind < 32))

    master = tiled(soap_weight)
    low = master.astype(bf16)
    low = jnp.where(flips[:, None, None], jnp.swapaxes(low, 1, 2), low)
    slots = lax.all_gather(pack_tile(low), ("dp", "mp"), axis=0, tiled=True)

    head_low = lax.all_gather(head_weight.astype(bf16), "mp", axis=0, tiled=True)

    split_one = (2 * LAYERS + 1) * D
    gain_rows = vectors[:split_one].reshape(2 * LAYERS + 1, 4, TILE)
    gain_rows = widen([gain_rows[:, t] for t in range(4)], 1)[:, None, :]
    head_gains = vectors[split_one : split_one + 2 * LAYERS * HD].reshape(LAYERS, 2, HD)
    class_bias = vectors[vectors.shape[0] - CLASSES :]

    tokens = by_partner(patches.reshape(4, OWN, D), mp_index)
    ids = by_partner(image_ids.reshape(4, OWN), mp_index)
    kept = by_partner(keep.reshape(4, OWN), mp_index) == 1
    query_ids = ids.reshape(1, TOKENS)
    key_ids = jnp.where(kept, ids, -1).reshape(TOKENS, 1)
    member_all = (image_ids[0, :, None] == jnp.arange(IMGS)[None, :]) & (keep[0, :, None] == 1)
    counts = jnp.sum(member_all.astype(f32), axis=0)
    present = (counts > 0).astype(f32)
    divisor = jnp.maximum(counts, 1.0)
    member = ((ids[0][:, None] == jnp.arange(IMGS)[None, :]) & kept[0][:, None]).astype(f32)
    image_total = total_dp(jnp.full((8, 128), jnp.sum(present), f32))[0, 0]

    first_tiles, second_tiles = (tiled(soap_first), tiled(soap_second))
    left_stat, right_stat = (tiled(stat_left), tiled(stat_right))
    left, right = (tiled(basis_left), tiled(basis_right))
    turned_first, left_old, right_old = run_soap_early(first_tiles, left_stat, right_stat, left, right)

    embedded = jnp.dot(tokens.reshape(TOKENS, D), embed_weight.astype(bf16), preferred_element_type=f32)
    embedded = embedded.astype(bf16).reshape(4, OWN, TILE)
    embedded = by_partner(jnp.stack(trade_mp([embedded[r] for r in range(4)])), mp_index)
    resid = widen([embedded[t] for t in range(4)], 1).astype(f32)
    act = (normalize(resid)[0] * gain_rows[0]).astype(bf16)

    blocks = [layer_blocks(depth) for depth in range(LAYERS)]
    weights = [assemble(table, slots, blocks[0][:1]) + assemble(table, slots, blocks[0][1:])]
    weights += [assemble(table, slots, blocks[depth]) for depth in range(1, LAYERS)]
    index = jnp.full((1,), mp_index, jnp.int32)
    saved = []
    normed = None
    for depth in range(LAYERS):
        qkv, out, up, down = weights[depth]
        out = out.reshape(D, D)
        gains = head_gains[depth].T
        acts = gather_mp(act)
        if depth == 0:
            acts[0] = gate(acts[0], turned_first, second_tiles)
        else:
            normed = gate(normed, *acts[1:], qkv)
            saved[-1].append(lax.all_gather(normed, "mp", axis=0, tiled=True))
        pre, v, lse, *o = run_attend_fwd(qkv, acts, gains, query_ids, key_ids)
        outs = trade_mp(o)
        if depth == 0:
            outs[0] = gate(outs[0], head_low)
        mid, u, normed, resid_next, act = run_mix_fwd(
            resid, outs, out, gain_rows[2 * depth + 1], gain_rows[2 * depth + 2], up, down
        )
        saved.append([resid, acts, pre, v, lse, o, mid, u])
        resid = resid_next
    saved[-1].append(lax.all_gather(normed, "mp", axis=0, tiled=True))

    resid = gate(resid, saved[0][-1])
    final, final_inverse = normalize(resid)
    gain_last = gain_rows[2 * LAYERS]
    pooled = total_mp(jnp.dot(member.T, final * gain_last, precision=highest)) / divisor[:, None]
    pooled = jnp.concatenate([pooled[:, :512].reshape(IMGS, 4, 128), pooled[:, 512:].reshape(IMGS, 4, 64)], axis=2)
    pooled_low = pooled.reshape(IMGS, D).astype(bf16)
    logits = jnp.dot(pooled_low, head_low, preferred_element_type=f32) + class_bias
    row_max = jnp.max(logits, -1, keepdims=True)
    exps = jnp.exp(logits - row_max)
    row_sum = jnp.sum(exps, -1, keepdims=True)
    log_norm = row_max[:, 0] + jnp.log(row_sum[:, 0])
    onehot = (jnp.arange(CLASSES)[None, :] == labels.reshape(-1)[:, None]).astype(f32)
    local_loss = jnp.sum((log_norm - jnp.sum(onehot * logits, -1)) * present)
    grad_logits = (exps / row_sum - onehot) * present[:, None] / image_total
    grad_bias = jnp.sum(grad_logits, 0)
    grad_logit_low = grad_logits.astype(bf16)
    pooled_mine = lax.dynamic_slice_in_dim(pooled_low, mp_index * TILE, TILE, 1)
    grad_head = jnp.dot(pooled_mine.T, grad_logit_low, preferred_element_type=f32)
    grad_pooled = jnp.dot(grad_logit_low, head_low.T, preferred_element_type=f32)
    grad_pooled = grad_pooled / divisor[:, None]
    grad_pooled = widen([grad_pooled[:, TILE * t : TILE * t + TILE] for t in range(4)], 1)
    grad_final = jnp.dot(member, grad_pooled, precision=highest)
    gain_grads = [wide_back(jnp.sum(grad_final * final, 0))]
    grad = norm_back(grad_final, gain_last, final, final_inverse)
    grad_low = grad.astype(bf16)

    buffers = waiting = None
    head_gain_grads = []
    for depth in reversed(range(LAYERS)):
        qkv, out, up, down = weights[depth]
        resid, acts, pre, v, lse, o, mid, u, normed = saved[depth]
        gains = head_gains[depth].T
        out = out.reshape(D, D)
        lows = lax.all_gather(grad_low, "mp", axis=0, tiled=True)
        mid_grad, mid_low, gain_two, *do = run_mix_bwd(
            grad, grad_low, mid, u, gain_rows[2 * depth + 1], out, up, down
        )
        dos = trade_mp(do)
        mid_lows = lax.all_gather(gate(mid_low, *dos[1:]), "mp", axis=0, tiled=True)
        if waiting is None:
            pre = gate(pre, normed)
        else:
            deeper, given, *rest = waiting
            buffers, token = run_head_grads(deeper, places, index, gate(given, do[0]), *rest, buffers)
            pre = gate(pre, token)
        *dp, gain_heads = run_attend_bwd(pre, v, lse, dos, gains, query_ids, key_ids)
        dps = trade_mp(dp)
        buffers, token = run_mlp_grads(depth, places, normed, lows, up, down, buffers)
        mid_grad = gate(mid_grad, token)
        grad, grad_low, gain_one = run_input_bwd(mid_grad, dps, qkv, resid, gain_rows[2 * depth])
        waiting = (depth, mid_lows, o, dp, acts)
        gain_grads = [wide_back(gain_one[0]), wide_back(gain_two[0])] + gain_grads
        head_gain_grads.insert(0, gain_heads.T)

    deeper, *rest = waiting
    buffers, token = run_head_grads(deeper, places, index, *rest, buffers)

    columns = trade_mp([wide_part(grad_low, mp_index ^ r, 1) for r in range(4)])
    columns[0] = gate(columns[0], token)
    columns = jnp.concatenate(columns, axis=0)
    grad_embed = jnp.dot(columns.T, tokens.reshape(TOKENS, D), preferred_element_type=f32)
    embed_rows = grad_embed.reshape(32, EMBED_ROWS, 128)
    head_rows = jnp.pad(grad_head, ((0, 0), (0, 24))).reshape(32, HEAD_ROWS, 128)
    vector_part = jnp.concatenate([jnp.concatenate(gain_grads), jnp.stack(head_gain_grads).reshape(-1)])
    vector_sum = jnp.concatenate([total_mp(vector_part), grad_bias, jnp.zeros((24,), f32)])
    vector_rows = jnp.pad(vector_sum.reshape(32, 160), ((0, 0), (0, 1536 - 160))).reshape(32, 12, 128)
    small = jnp.concatenate([embed_rows, head_rows, vector_rows], axis=1).astype(bf16)
    small = by_partner(small, dp_index).reshape(16, 2, SMALL, 128)
    keep_buffer = buffers[0].at[:, 3 * PACK :].set(small[:, 0])
    send_buffer = buffers[1].at[:, 3 * PACK :].set(small[:, 1])

    sums = run_add_core(keep_buffer, swap_dp(send_buffer, 1))
    sums = run_add_axis(
        [sums[0]] + [swap_dp(sums[r], 8 * r) for r in (1, 2, 3)],
        [sums[4]] + [swap_dp(sums[4 + r], 2 * r) for r in (1, 2, 3)],
    )
    mine = jnp.concatenate(
        [
            sum_four([sums[0]] + [swap_dp(sums[r], 2 * r).astype(f32) for r in (1, 2, 3)]),
            sum_four([sums[4]] + [swap_dp(sums[4 + r], 8 * r).astype(f32) for r in (1, 2, 3)]),
        ],
        axis=0,
    )
    mine_slots = mine[: 3 * PACK]
    share = mine[3 * PACK :]
    cut_at = EMBED_ROWS + HEAD_ROWS
    local_squares = (
        jnp.sum(mine_slots * mine_slots)
        + jnp.sum(share[:cut_at] * share[:cut_at])
        + jnp.sum(share[cut_at:] * share[cut_at:]) * 0.25
    )
    def flat(tiles):
        return tiles.reshape(3, TILE * TILE)

    grad_tiles, turned, left_new, right_new, gram_left, gram_right = run_soap_mid(
        flips.astype(jnp.int32), mine_slots.reshape(3, PACK, 128), left, right
    )
    rows = jnp.arange(8)[:, None] + jnp.zeros((8, 128), jnp.int32)
    squares = total_mp(jnp.where(rows == 0, local_squares, local_loss * 0.25))
    squares = squares + swap_dp(squares, 1)
    squares = sum_four([squares] + [swap_dp(squares, 2 * r) for r in (1, 2, 3)])
    flats = [flat(grad_tiles), flat(turned), flat(gram_left), flat(gram_right)]
    squares = gate(squares, *flats)
    squares = sum_four([squares] + [swap_dp(squares, 8 * r) for r in (1, 2, 3)])
    squares, loss_total = (squares[0, 0], squares[1, 0])
    shares = lax.all_gather(share, "dp", axis=0)
    grad_norm = jnp.sqrt(squares)
    factor = clip_limit / jnp.maximum(grad_norm, clip_limit)

    grad_flat, turned_flat, gram_left, gram_right = flats
    weight_new, left_basis, right_basis, weight_low = run_soap_late(
        factor.reshape(1, 1), second_tiles, left, right, master, turned, turned_first,
        left_old, right_old, left_new, right_new,
    )
    turned_flat = turned_flat * factor
    soap_new = (
        flat(weight_new),
        first_decay * soap_first + (1.0 - first_decay) * (grad_flat * factor),
        second_decay * soap_second + (1.0 - second_decay) * turned_flat * turned_flat,
        second_decay * stat_left + (1.0 - second_decay) * (factor * (factor * gram_left)),
        second_decay * stat_right + (1.0 - second_decay) * (factor * (factor * gram_right)),
        flat(left_basis),
        flat(right_basis),
        flat(weight_low),
    )

    grad_embed = shares[:, :EMBED_ROWS].reshape(TILE, D)
    grad_head = shares[:, EMBED_ROWS:cut_at].reshape(TILE, 1024)[:, :CLASSES]
    grad_vector = shares[:, cut_at:].reshape(32, 1536)[:, :160].reshape(-1)[: vectors.shape[0]]
    embed_new = adamw(
        embed_weight.T, grad_embed * factor, embed_first.T, embed_second.T, matrix_rate, weight_decay
    )
    embed_new = tuple(entry.T for entry in embed_new)
    head_new = adamw(
        head_weight, grad_head * factor, head_first, head_second, matrix_rate, weight_decay
    )
    vector_new = adamw(vectors, grad_vector * factor, vector_first, vector_second, vector_rate, 0.0)
    return (loss_total, image_total, grad_norm, *soap_new, *embed_new, *head_new, *vector_new)


def solution(mesh):
    by_slot = P(("dp", "mp"), None)
    columns = P(None, "mp")
    rows = P("mp", None)
    return jax.shard_map(
        shards,
        mesh=mesh,
        in_specs=(P("dp", None, None), P("dp", None), P("dp", None), P("dp", None), P())
        + (by_slot,) * 7
        + (columns,) * 3
        + (rows,) * 3
        + (P(),) * 3,
        out_specs=(P(),) * 3 + (by_slot,) * 8 + (columns,) * 3 + (rows,) * 3 + (P(),) * 3,
        check_vma=False,
    )
```

```python
import jax
import jax.numpy as jnp
from jax import lax
from jax.experimental import pallas as pl
from jax.experimental.pallas import tpu as pltpu
from jax.sharding import PartitionSpec as P

D = 768
HD = 64
HEADS = 3
CLASSES = 1000
LAYERS = 2
IMGS = 8
STEP = 10
TILE = 192
TOKENS = 1024
OWN = 256
PACK = 288
SMALL = 96
ROWS = 3 * PACK + SMALL
EMBED_ROWS = 36
HEAD_ROWS = 48

first_decay = 0.9
second_decay = 0.95
weight_decay = 0.05
matrix_rate = 0.03
vector_rate = 0.3
clip_limit = 0.01
adam_epsilon = 1e-08
norm_epsilon = 1e-06
masked_score = -1e30
highest = lax.Precision.HIGHEST
f32 = jnp.float32
bf16 = jnp.bfloat16
MIB = 2**20
VM = pl.BlockSpec(memory_space=pltpu.VMEM)
SM = pl.BlockSpec(memory_space=pltpu.SMEM)
ANY = pl.BlockSpec(memory_space=pl.ANY)


def params(mib):
    return pltpu.CompilerParams(vmem_limit_bytes=mib * MIB)


def cost(flops, moved, exps=0):
    return pl.CostEstimate(flops=flops, bytes_accessed=moved, transcendentals=exps)


def shape(dims, kind=f32):
    return jax.ShapeDtypeStruct(dims, kind)


def mm(a, b, ca=1, cb=0):
    return lax.dot_general(a, b, (((ca,), (cb,)), ((), ())), preferred_element_type=f32)


def mm_full(a, b, ca, cb):
    return lax.dot_general(
        a, b, (((ca,), (cb,)), ((), ())), precision=highest, preferred_element_type=f32
    )


def mm_split(a, b, ca, cb):
    a_high, b_high = (a.astype(bf16), b.astype(bf16))
    a_low = (a - a_high.astype(f32)).astype(bf16)
    b_low = (b - b_high.astype(f32)).astype(bf16)
    return mm(a_high, b_high, ca, cb) + (mm(a_high, b_low, ca, cb) + mm(a_low, b_high, ca, cb))


def normalize(values):
    centered = values - jnp.mean(values, -1, keepdims=True)
    inverse = lax.rsqrt(jnp.mean(centered * centered, -1, keepdims=True) + norm_epsilon)
    return centered * inverse, inverse


def norm_back(grad, gain, normed, inverse):
    scaled = grad * gain
    return inverse * (
        scaled
        - jnp.mean(scaled, -1, keepdims=True)
        - normed * jnp.mean(scaled * normed, -1, keepdims=True)
    )


def gauss_parts(value):
    size = jnp.abs(value) * 0.7071067811865476
    bell = jnp.exp(-size * size)
    t = 1.0 / (1.0 + 0.3275911 * size)
    poly = t * (
        0.254829592
        + t * (-0.284496736 + t * (1.421413741 + t * (-1.453152027 + t * 1.061405429)))
    )
    tail = 0.5 * poly * bell
    return jnp.where(value >= 0, 1.0 - tail, tail), bell


def gelu(value):
    return value * gauss_parts(value)[0]


def widen(parts, axis):
    return jnp.concatenate(
        [lax.slice_in_dim(x, 0, 128, axis=axis) for x in parts]
        + [lax.slice_in_dim(x, 128, TILE, axis=axis) for x in parts],
        axis=axis,
    )


def wide_part(array, k, axis):
    return jnp.concatenate(
        [
            lax.dynamic_slice_in_dim(array, 128 * k, 128, axis),
            lax.dynamic_slice_in_dim(array, 512 + 64 * k, 64, axis),
        ],
        axis=axis,
    )


def wide_back(vector):
    return jnp.concatenate([vector[:512].reshape(4, 128), vector[512:].reshape(4, 64)], axis=1).reshape(D)


def pack_tile(tile):
    half = TILE // 2
    right = tile[..., 128:]
    return jnp.concatenate(
        [
            tile[..., :128],
            jnp.concatenate([right[..., :half, :], right[..., half:, :]], axis=-1),
        ],
        axis=-2,
    )


def unpack_tile(packed):
    half = TILE // 2
    right = packed[..., TILE:, :]
    return jnp.concatenate(
        [
            packed[..., :TILE, :],
            jnp.concatenate([right[..., :64], right[..., 64:]], axis=-2),
        ],
        axis=-1,
    )


def assemble(table, slots, groups):
    half = TILE // 2
    sizes = [4 * len(group) for group in groups]
    lines = sum(sizes)
    wanted = [96 * r + block for group in groups for r in range(4) for line in group for block in line]

    def kernel(table_ref, slots_ref, *refs):
        outs = refs[: len(groups)]
        tiles, stage, in_sems, out_sems = refs[len(groups) :]

        def fetch(at, place):
            return pltpu.make_async_copy(slots_ref.at[place], tiles.at[at], in_sems.at[at])

        for at, entry in enumerate(wanted):
            fetch(at, table_ref[entry]).start()
        base = 0
        for out_ref, size in zip(outs, sizes):

            def step(line, carry):
                at = base + line
                for t in range(4):
                    fetch(4 * at + t, 0).wait()
                for t in range(4):
                    stage[at, :, 128 * t : 128 * t + 128] = tiles[4 * at + t, :TILE]
                for t in (0, 2):
                    first = tiles[4 * at + t, TILE:]
                    second = tiles[4 * at + t + 1, TILE:]
                    cols = slice(512 + 64 * t, 640 + 64 * t)
                    stage[at, :half, cols] = jnp.concatenate([first[:, :64], second[:, :64]], axis=1)
                    stage[at, half:, cols] = jnp.concatenate([first[:, 64:], second[:, 64:]], axis=1)
                pltpu.make_async_copy(stage.at[at], out_ref.at[line], out_sems.at[at]).start()
                return carry

            lax.fori_loop(0, size, step, 0)
            base += size
        base = 0
        for out_ref, size in zip(outs, sizes):

            def finish(line, carry):
                pltpu.make_async_copy(stage.at[base + line], out_ref.at[line], out_sems.at[base + line]).wait()
                return carry

            lax.fori_loop(0, size, finish, 0)
            base += size

    mats = pl.pallas_call(
        kernel,
        in_specs=[SM, ANY],
        out_specs=[ANY] * len(groups),
        out_shape=[shape((size, TILE, D), bf16) for size in sizes],
        scratch_shapes=[
            pltpu.VMEM((4 * lines, PACK, 128), bf16),
            pltpu.VMEM((lines, TILE, D), bf16),
            pltpu.SemaphoreType.DMA((4 * lines,)),
            pltpu.SemaphoreType.DMA((lines,)),
        ],
        compiler_params=params(60),
        cost_estimate=cost(0, 4 * lines * TILE * TILE * 4),
        name="assemble",
    )(table, slots)
    return [mat.reshape(4, len(group) * TILE, D) for mat, group in zip(mats, groups)]


def layer_blocks(depth):
    base = 48 * depth
    qkv = [[base + 3 * r + c for r in range(4)] for c in range(3)]
    out = [[base + 12 + t for t in range(4)]]
    up = [[base + 16 + 4 * r + t for r in range(4)] for t in range(4)]
    down = [[base + 32 + 4 * t + r for r in range(4)] for t in range(4)]
    return [qkv, out, up, down]


def column_norm(values):
    centered = values - jnp.mean(values, 0, keepdims=True)
    inverse = lax.rsqrt(jnp.mean(centered * centered, 0, keepdims=True) + norm_epsilon)
    return centered * inverse, inverse


def by_three(step):
    def turn(i, carry):
        for j in range(3):
            carry = step(3 * i + j, carry)
        return carry

    lax.fori_loop(0, 4 * HEADS // 3, turn, 0)


def attend_fwd(w_ref, a0, a1, a2, a3, gain_ref, qid_ref, kid_ref, pre_ref, v_ref, lse_ref, o0, o1, o2, o3, q_s, k_s, o_s):
    for r, a_ref in enumerate((a0, a1, a2, a3)):
        cols = slice(OWN * r, OWN * r + OWN)
        projected = mm(w_ref[0], a_ref[...], 1, 1)
        v_ref[:, cols] = projected[2 * TILE :].astype(bf16)
        pre_ref[:, cols] = projected[: 2 * TILE]
        for c in range(2):
            for h in range(HEADS):
                rows = slice(HD * h, HD * h + HD)
                part = projected[TILE * c + HD * h : TILE * c + HD * h + HD]
                low = (column_norm(part)[0] * gain_ref[:, c : c + 1]).astype(bf16)
                if c == 0:
                    q_s[r, rows, :] = low * bf16(0.125)
                else:
                    k_s[h, cols, :] = low.T

    def step(i, carry):
        h, t = (i // 4, i % 4)
        rows = pl.ds(pl.multiple_of(h * HD, HD), HD)
        cols = pl.ds(pl.multiple_of(t * OWN, OWN), OWN)
        scores = mm(k_s[h], q_s[t, rows, :])
        scores = jnp.where(kid_ref[...] == qid_ref[:, cols], scores, masked_score)
        top = jnp.max(scores, 0, keepdims=True)
        weights = jnp.exp(scores - top)
        total = jnp.sum(weights, 0, keepdims=True)
        lse_ref[h, :, cols] = top + jnp.log(total)
        probs = (weights * (1.0 / total)).astype(bf16)
        o_s[t, rows, :] = mm(v_ref[rows, :], probs).astype(bf16)
        return carry

    by_three(step)
    for r, ref in enumerate((o0, o1, o2, o3)):
        ref[...] = o_s[r]


def run_attend_fwd(w, acts, gains, qid, kid):
    return pl.pallas_call(
        attend_fwd,
        grid=(1,),
        in_specs=[pl.BlockSpec((1, 3 * TILE, D), lambda i: (0, 0, 0))] + [VM] * 7,
        out_specs=[VM] * 7,
        out_shape=[
            shape((2 * TILE, TOKENS)),
            shape((TILE, TOKENS), bf16),
            shape((HEADS, 1, TOKENS)),
        ]
        + [shape((TILE, OWN), bf16)] * 4,
        scratch_shapes=[
            pltpu.VMEM((4, TILE, OWN), bf16),
            pltpu.VMEM((HEADS, TOKENS, HD), bf16),
            pltpu.VMEM((4, TILE, OWN), bf16),
        ],
        compiler_params=params(60),
        cost_estimate=cost(10**10, 6 * 10**6, 3 * 2**20),
        name="attend_fwd",
    )(w, *acts, gains, qid, kid)


def attend_bwd(
    pre_ref, v_ref, lse_ref, g0, g1, g2, g3, gain_ref, qid_ref, kid_ref,
    p0, p1, p2, p3, dgain_ref, q_s, qn_s, k_s, kt_s, vn_s, do_s, dq_s, dk_s, dv_s,
):
    dp_refs = (p0, p1, p2, p3)
    for r, ref in enumerate((g0, g1, g2, g3)):
        do_s[r] = ref[...]
    for h in range(HEADS):
        rows = slice(HD * h, HD * h + HD)
        low = (column_norm(pre_ref[rows, :])[0] * gain_ref[:, 0:1]).astype(bf16)
        q_s[rows, :] = low * bf16(0.125)
        qn_s[h] = q_s[rows, :].T
        low = (column_norm(pre_ref[TILE + HD * h : TILE + HD * h + HD, :])[0] * gain_ref[:, 1:2]).astype(bf16)
        kt_s[rows, :] = low
        k_s[h] = low.T
        vn_s[h] = v_ref[rows, :].T
    dk_s[...] = jnp.zeros_like(dk_s)
    dv_s[...] = jnp.zeros_like(dv_s)

    def step(i, carry):
        h, t = (i // 4, i % 4)
        rows = pl.ds(pl.multiple_of(h * HD, HD), HD)
        cols = pl.ds(pl.multiple_of(t * OWN, OWN), OWN)
        scores = mm(k_s[h], q_s[rows, cols])
        scores = jnp.where(kid_ref[...] == qid_ref[:, cols], scores, masked_score)
        weights = jnp.exp(scores - lse_ref[h, :, cols])
        grad_out = do_s[t, rows, :]
        grad_weights = mm(vn_s[h], grad_out)
        dv_s[h] += mm(weights.astype(bf16), grad_out.T)
        inner = jnp.sum(weights * grad_weights, 0, keepdims=True)
        grad_scores = (weights * (grad_weights - inner)).astype(bf16)
        dq_s[rows, cols] = mm(kt_s[rows, :], grad_scores) * 0.125
        dk_s[h] += mm(grad_scores, qn_s[h, cols, :])
        return carry

    by_three(step)
    for c in range(2):
        total = jnp.zeros((HD, 1), f32)
        for h in range(HEADS):
            grad = dq_s[HD * h : HD * h + HD, :] if c == 0 else dk_s[h].T
            base = TILE * c + HD * h
            normed, inverse = column_norm(pre_ref[base : base + HD, :])
            total = total + jnp.sum(grad * normed, 1, keepdims=True)
            scaled = grad * gain_ref[:, c : c + 1]
            back = inverse * (
                scaled
                - jnp.mean(scaled, 0, keepdims=True)
                - normed * jnp.mean(scaled * normed, 0, keepdims=True)
            )
            for r in range(4):
                dp_refs[r][base : base + HD, :] = back[:, OWN * r : OWN * r + OWN].astype(bf16)
        dgain_ref[:, c : c + 1] = total
    for h in range(HEADS):
        back = dv_s[h].T.astype(bf16)
        for r in range(4):
            dp_refs[r][2 * TILE + HD * h : 2 * TILE + HD * h + HD, :] = back[:, OWN * r : OWN * r + OWN]


def run_attend_bwd(pre, v, lse, grads, gains, qid, kid):
    return pl.pallas_call(
        attend_bwd,
        in_specs=[VM] * 10,
        out_specs=[VM] * 5,
        out_shape=[shape((3 * TILE, OWN), bf16)] * 4 + [shape((HD, 2))],
        scratch_shapes=[
            pltpu.VMEM((TILE, TOKENS), bf16),
            pltpu.VMEM((HEADS, TOKENS, HD), bf16),
            pltpu.VMEM((HEADS, TOKENS, HD), bf16),
            pltpu.VMEM((TILE, TOKENS), bf16),
            pltpu.VMEM((HEADS, TOKENS, HD), bf16),
            pltpu.VMEM((4, TILE, OWN), bf16),
            pltpu.VMEM((TILE, TOKENS), f32),
            pltpu.VMEM((HEADS, TOKENS, HD), f32),
            pltpu.VMEM((HEADS, TOKENS, HD), f32),
        ],
        compiler_params=params(60),
        cost_estimate=cost(2 * 10**10, 6 * 10**6, 3 * 2**20),
        name="attend_bwd",
    )(pre, v, lse, *grads, gains, qid, kid)


def mix_fwd(x_ref, o0, o1, o2, o3, w_out, gain_ref, next_ref, up_ref, down_ref,
            mid_ref, u_ref, c_ref, x_out, a_out):
    r = pl.program_id(0)

    @pl.when(r == 0)
    def _():
        mid = x_ref[...]
        for k, ref in enumerate((o0, o1, o2, o3)):
            mid = mid + mm(ref[...], w_out[TILE * k : TILE * k + TILE, :], 0, 0)
        mid_ref[...] = mid
        low = (normalize(mid)[0] * gain_ref[...]).astype(bf16)
        c_ref[...] = low
        x_out[...] = mid

    u = mm(c_ref[...], up_ref[0], 1, 1)
    u_ref[0] = u
    x_out[...] += mm(gelu(u).astype(bf16), down_ref[0])

    @pl.when(r == 3)
    def _():
        a_out[...] = (normalize(x_out[...])[0] * next_ref[...]).astype(bf16)


def whole(*dims):
    return pl.BlockSpec(dims, lambda r: (0,) * len(dims))


def part(*dims):
    return pl.BlockSpec((1, *dims), lambda r: (r,) + (0,) * len(dims))


def run_mix_fwd(x, outs, w_out, gain, gain_next, up, down):
    return pl.pallas_call(
        mix_fwd,
        grid=(4,),
        in_specs=[whole(OWN, D)] + [whole(TILE, OWN)] * 4 + [whole(D, D), whole(1, D), whole(1, D), part(D, D), part(D, D)],
        out_specs=[whole(OWN, D), part(OWN, D), whole(OWN, D), whole(OWN, D), whole(OWN, D)],
        out_shape=[shape((OWN, D)), shape((4, OWN, D)), shape((OWN, D), bf16), shape((OWN, D)), shape((OWN, D), bf16)],
        compiler_params=params(60),
        cost_estimate=cost(6 * 10**9, 17 * 10**6, 10**6),
        name="mix_fwd",
    )(x, *outs, w_out, gain, gain_next, up, down)


def mix_bwd(g_ref, low_ref, mid_ref, u_ref, gain_ref, w_out, up_ref, down_ref,
            mid_grad, mid_low, dgain_ref, do0, do1, do2, do3, acc):
    r = pl.program_id(0)

    @pl.when(r == 0)
    def _():
        acc[...] = jnp.zeros_like(acc)

    df = mm(low_ref[...], down_ref[0], 1, 1)
    u = u_ref[0]
    cdf, bell = gauss_parts(u)
    du = (df * (cdf + u * bell * 0.3989422804014327)).astype(bf16)
    acc[...] += mm(du, up_ref[0])

    @pl.when(r == 3)
    def _():
        normed, inverse = normalize(mid_ref[...])
        grad = acc[...]
        dgain_ref[...] = jnp.sum(grad * normed, 0, keepdims=True)
        total = g_ref[...] + norm_back(grad, gain_ref[...], normed, inverse)
        mid_grad[...] = total
        low = total.astype(bf16)
        mid_low[...] = low
        for k, ref in enumerate((do0, do1, do2, do3)):
            ref[...] = mm(w_out[TILE * k : TILE * k + TILE, :], low, 1, 1).astype(bf16)


def run_mix_bwd(grad, grad_low, mid, u, gain, w_out, up, down):
    return pl.pallas_call(
        mix_bwd,
        grid=(4,),
        in_specs=[whole(OWN, D), whole(OWN, D), whole(OWN, D), part(OWN, D), whole(1, D), whole(D, D), part(D, D), part(D, D)],
        out_specs=[whole(OWN, D), whole(OWN, D), whole(1, D)] + [whole(TILE, OWN)] * 4,
        out_shape=[shape((OWN, D)), shape((OWN, D), bf16), shape((1, D))] + [shape((TILE, OWN), bf16)] * 4,
        scratch_shapes=[pltpu.VMEM((OWN, D), f32)],
        compiler_params=params(60),
        cost_estimate=cost(6 * 10**9, 17 * 10**6, 10**6),
        name="mix_bwd",
    )(grad, grad_low, mid, u, gain, w_out, up, down)


def input_bwd(mid_grad, d0, d1, d2, d3, w_ref, x_ref, gain_ref, grad_ref, low_ref, dgain_ref):
    grad = mm(d0[...], w_ref[0], 0, 0)
    for k, ref in ((1, d1), (2, d2), (3, d3)):
        grad = grad + mm(ref[...], w_ref[k], 0, 0)
    normed, inverse = normalize(x_ref[...])
    dgain_ref[...] = jnp.sum(grad * normed, 0, keepdims=True)
    total = mid_grad[...] + norm_back(grad, gain_ref[...], normed, inverse)
    grad_ref[...] = total
    low_ref[...] = total.astype(bf16)


def run_input_bwd(mid_grad, grads, w, x, gain):
    return pl.pallas_call(
        input_bwd,
        in_specs=[VM] * 8,
        out_specs=[VM] * 3,
        out_shape=[shape((OWN, D)), shape((OWN, D), bf16), shape((1, D))],
        compiler_params=params(48),
        cost_estimate=cost(10**9, 6 * 10**6),
        name="input_bwd",
    )(mid_grad, *grads, w, x, gain)


def pack_wide(line, t):
    half = TILE // 2
    right = line[:, 512 + 64 * t : 576 + 64 * t]
    return jnp.concatenate(
        [
            line[:, 128 * t : 128 * t + 128],
            jnp.concatenate([right[:half], right[half:]], axis=1),
        ],
        axis=0,
    )


def send_line(places, stage, sems, keep, send, line, blocks, base):
    line = line.astype(bf16)
    for t, block in enumerate(blocks):
        at = base + t
        stage[at] = pack_wide(line, t)
        place = places[block]
        rows = pl.ds(pl.multiple_of((place % 3) * PACK, 16), PACK)

        @pl.when(place < 48)
        def _():
            pltpu.make_async_copy(stage.at[at], keep.at[place // 3, rows], sems.at[at]).start()

        @pl.when(place >= 48)
        def _():
            pltpu.make_async_copy(stage.at[at], send.at[place // 3 - 16, rows], sems.at[at]).start()


def wait_tiles(stage, sems, keep, count):
    for at in range(count):
        pltpu.make_async_copy(stage.at[at], keep.at[0, pl.ds(0, PACK)], sems.at[at]).wait()


def mlp_grads(depth, places, act_ref, low_ref, up_ref, down_ref, *refs):
    keep, send, token, stage, sems = refs[-5:]
    base = 48 * depth
    for i in range(4):
        rows = slice(TILE * i, TILE * i + TILE)
        u = mm(up_ref[0, rows, :], act_ref[...], 1, 1)
        df = mm(down_ref[0, rows, :], low_ref[...], 1, 1)
        cdf, bell = gauss_parts(u)
        f_low = (u * cdf).astype(bf16)
        du_low = (df * (cdf + u * bell * 0.3989422804014327)).astype(bf16)
        line = mm(du_low, act_ref[...])
        send_line(places, stage, sems, keep, send, line, [base + 16 + 4 * t + i for t in range(4)], 4 * i)
        line = mm(f_low, low_ref[...])
        send_line(places, stage, sems, keep, send, line, [base + 32 + 4 * i + t for t in range(4)], 16 + 4 * i)
    token[...] = jnp.zeros_like(token)
    wait_tiles(stage, sems, keep, 32)


def head_grads(depth, places, index, mid_ref, *refs):
    outs, grads, acts = (refs[0:4], refs[4:8], refs[8:12])
    keep, send, token, stage, sems = refs[-5:]
    base = 48 * depth
    parts = []
    for r in range(4):
        rows = pl.ds(pl.multiple_of((index[0] ^ r) * OWN, OWN), OWN)
        parts.append(mm(outs[r][...], mid_ref[rows, :]))
    line = (parts[0] + parts[1]) + (parts[2] + parts[3])
    send_line(places, stage, sems, keep, send, line, [base + 12 + t for t in range(4)], 12)
    for c in range(3):
        rows = slice(TILE * c, TILE * c + TILE)
        parts = [mm(grads[r][rows, :], acts[r][...]) for r in range(4)]
        line = (parts[0] + parts[1]) + (parts[2] + parts[3])
        send_line(places, stage, sems, keep, send, line, [base + 3 * t + c for t in range(4)], 4 * c)
    token[...] = jnp.zeros_like(token)
    wait_tiles(stage, sems, keep, 16)


def grads_call(kernel, name, scalars, args, specs, buffers, count, flops):
    given = list(buffers) if buffers is not None else []
    first = len(scalars) + len(args)
    *buffers, token = pl.pallas_call(
        kernel,
        grid=(1,),
        in_specs=[SM] * len(scalars) + specs + [ANY] * len(given),
        out_specs=[ANY, ANY, VM],
        out_shape=[shape((16, ROWS, 128), bf16)] * 2 + [shape((8, 128))],
        input_output_aliases={first + i: i for i in range(len(given))},
        scratch_shapes=[pltpu.VMEM((count, PACK, 128), bf16), pltpu.SemaphoreType.DMA((count,))],
        compiler_params=params(56),
        cost_estimate=cost(flops, 10**7),
        name=name,
    )(*scalars, *args, *given)
    return buffers, token


def run_mlp_grads(depth, places, act, low, up, down, buffers):
    first = pl.BlockSpec((1, D, D), lambda i: (0, 0, 0))
    return grads_call(
        lambda *refs: mlp_grads(depth, *refs), "mlp_grads", [places],
        [act, low, up, down], [VM] * 2 + [first] * 2, buffers, 32, 5 * 10**9,
    )


def run_head_grads(depth, places, index, mid_low, outs, grads, acts, buffers):
    return grads_call(
        lambda *refs: head_grads(depth, *refs), "head_grads", [places, index],
        [mid_low, *outs, *grads, *acts], [VM] * 13, buffers, 16, 2 * 10**9,
    )


def add_core(keep, got, own_a, a1, a2, a3, own_b, b1, b2, b3):
    step = pl.program_id(0)
    half = ROWS // 2
    total = keep[...].astype(f32) + got[...].astype(f32)

    @pl.when(step == 0)
    def _():
        own_a[...] = total[:, :half]

    for k, ref in ((1, a1), (2, a2), (3, a3)):

        @pl.when(step == k)
        def _():
            ref[...] = total[:, :half].astype(bf16)

    own_b[0] = total[0, half:]
    for k, ref in ((1, b1), (2, b2), (3, b3)):
        ref[0] = total[k, half:].astype(bf16)


def run_add_core(keep, got):
    half = ROWS // 2
    block = pl.BlockSpec((4, ROWS, 128), lambda r: (r, 0, 0))
    one, many = (whole(4, half, 128), part(half, 128))
    return pl.pallas_call(
        add_core, grid=(4,), in_specs=[block] * 2, out_specs=[one] * 4 + [many] * 4,
        out_shape=([shape((4, half, 128))] + [shape((4, half, 128), bf16)] * 3) * 2,
        compiler_params=params(32), cost_estimate=cost(10**7, 14 * 10**6), name="add_core",
    )(keep, got)


def add_axis(*refs):
    ins, outs = (refs[:8], refs[8:])
    for side in range(2):
        own, r1, r2, r3 = ins[4 * side : 4 * side + 4]
        for k in range(4):
            total = (own[k] + r1[k].astype(f32)) + (r2[k].astype(f32) + r3[k].astype(f32))
            out = outs[4 * side + k]
            out[...] = total.astype(out.dtype)


def run_add_axis(a, b):
    half = ROWS // 2
    return pl.pallas_call(
        add_axis, in_specs=[VM] * 8, out_specs=[VM] * 8,
        out_shape=([shape((half, 128))] + [shape((half, 128), bf16)] * 3) * 2,
        compiler_params=params(32), cost_estimate=cost(10**7, 6 * 10**6), name="add_axis",
    )(*a, *b)


def gate(array, *others):
    return pl.pallas_call(
        lambda *refs: None, in_specs=[ANY] * (1 + len(others)), out_specs=ANY,
        out_shape=shape(array.shape, array.dtype), input_output_aliases={0: 0},
        compiler_params=params(16), name="gate",
    )(array, *others)


def soap_early(first, stat_l, stat_r, left, right, turned_ref, l_ref, r_ref):
    turned_ref[0] = mm_split(mm_split(left[0], first[0], 0, 0), right[0], 1, 0)
    l_ref[0] = mm_full(stat_l[0], left[0], 1, 0)
    r_ref[0] = mm_full(stat_r[0], right[0], 1, 0)


def soap_mid(flip_ref, packed, left, right, grad_ref, turned_ref, yl_ref, yr_ref, gl_ref, gr_ref):
    tile = unpack_tile(packed[0])
    turned_tile = tile.T
    flip = flip_ref[pl.program_id(0)] == 1
    grad = jnp.where(flip, turned_tile, tile)
    grad_t = jnp.where(flip, tile, turned_tile)
    grad_ref[0] = grad
    right_part = mm_full(grad, right[0], 1, 0)
    turned_ref[0] = mm_split(left[0], right_part, 0, 0)
    yr_ref[0] = mm_full(grad_t, right_part, 1, 0)
    yl_ref[0] = mm_full(grad, mm_full(grad_t, left[0], 1, 0), 1, 0)
    gl_ref[0] = mm_full(grad, grad_t, 1, 0)
    gr_ref[0] = mm_full(grad_t, grad, 1, 0)


def factor_inverses(grams, fillers=()):
    size = 64
    fillers = list(fillers)
    row = lax.broadcasted_iota(jnp.int32, (8, 128), 0)
    lane = lax.broadcasted_iota(jnp.int32, (8, 128), 1)
    on_diagonal = lax.broadcasted_iota(jnp.int32, (size, size), 0) == lax.broadcasted_iota(
        jnp.int32, (size, size), 1
    )
    states, scales = ([], [])
    for gram in grams:
        diagonal = jnp.where(on_diagonal, gram, 0.0)
        scale_row = lax.rsqrt(jnp.sum(diagonal, axis=0, keepdims=True))
        scale_column = lax.rsqrt(jnp.sum(diagonal, axis=1, keepdims=True))
        scales.append(scale_row)
        wide = jnp.concatenate([gram * scale_row * scale_column, jnp.zeros((size, size), f32)], axis=1)
        states.append(
            [jnp.where(lane == row + (size + 8 * t), 1.0, wide[8 * t : 8 * t + 8, :]) for t in range(8)]
        )
    for k in range(0, size, 2):
        home, at = divmod(k, 8)
        for tiles in states:
            own = tiles[home]
            first, second = (own[at : at + 1, :], own[at + 1 : at + 2, :])
            a, b, c = (
                jnp.broadcast_to(entry, (1, 128))
                for entry in (first[:, k : k + 1], first[:, k + 1 : k + 2], second[:, k + 1 : k + 2])
            )
            inverse = 1.0 / (a * c - b * b)
            line_first = (c * first - b * second) * inverse
            line_second = (a * second - b * first) * inverse
            for t in range(home, 8):
                update = tiles[t][:, k : k + 1] * line_first + tiles[t][:, k + 1 : k + 2] * line_second
                if t == home:
                    inside = jnp.where(row == at + 1, first * (b / a), 0.0)
                    update = jnp.where(row > at + 1, update, inside)
                tiles[t] = tiles[t] - update
        if fillers:
            fillers.pop(0)()
    for filler in fillers:
        filler()
    inverses = []
    for tiles, scale_row in zip(states, scales):
        done = []
        for t in range(8):
            diagonal = jnp.sum(jnp.where(lane == row + 8 * t, tiles[t], 0.0), axis=1, keepdims=True)
            done.append(tiles[t] * lax.rsqrt(diagonal))
        inverses.append(jnp.concatenate(done, axis=0)[:, size:] * scale_row)
    return inverses


def soap_late(
    f_ref, second, left, right, weight, turned, turned_first, xl, xr, yl, yr,
    weight_ref, left_ref, right_ref, low_ref, panels, work,
):
    factor = f_ref[0, 0]
    bias_one = 1.0 - first_decay**STEP
    bias_two = 1.0 - second_decay**STEP
    outs = (left_ref, right_ref)

    def product(i):
        n, (old, new) = (i // 2, ((xl, yl), (xr, yr))[i % 2])
        total = second_decay * old[n] + (1.0 - second_decay) * (factor * (factor * new[n]))
        for j in range(3):
            panels[i, j] = total[:, 64 * j : 64 * j + 64]

    def scaled(n):
        rotated = turned[n] * factor
        second_new = second_decay * second[n] + (1.0 - second_decay) * rotated * rotated
        work[n] = (
            (first_decay * turned_first[n] + (1.0 - first_decay) * rotated)
            / bias_one
            / (jnp.sqrt(second_new / bias_two) + adam_epsilon)
        )

    def half_back(n):
        work[n] = mm_split(left[n], work[n], 1, 0)

    def move(n):
        back = mm_split(work[n], right[n], 1, 1)
        weight_new = weight[n] * (1.0 - matrix_rate * weight_decay) - matrix_rate * back
        weight_ref[n] = weight_new
        low_ref[n] = weight_new.astype(bf16)

    def remove(i, basis, k):
        panel = panels[i, k]
        panels[i, k] = panel - mm_full(basis, mm_full(basis, panel, 0, 0), 1, 0)

    def grams(j):
        return [mm_full(panels[i, j], panels[i, j], 0, 0) for i in range(6)]

    def bases(j, inverses):
        found = []
        for i in range(6):
            basis = mm_full(panels[i, j], inverses[i], 1, 1)
            outs[i % 2][i // 2, :, 64 * j : 64 * j + 64] = basis
            found.append(basis)
        return found

    for i in range(6):
        product(i)
    pieces = [lambda step=step, n=n: step(n) for n in range(3) for step in (scaled, half_back, move)]
    found = bases(0, factor_inverses(grams(0), pieces))
    for i in range(6):
        remove(i, found[i], 1)
    pieces = [lambda i=i, basis=found[i]: remove(i, basis, 2) for i in range(6)]
    found = bases(1, factor_inverses(grams(1), pieces))
    for i in range(6):
        remove(i, found[i], 2)
    bases(2, factor_inverses(grams(2)))


def tile_spec():
    return pl.BlockSpec((1, TILE, TILE), lambda i: (i, 0, 0))


def tiles_of_three(count):
    return [shape((3, TILE, TILE))] * count


def run_soap_early(first, stat_l, stat_r, left, right):
    return pl.pallas_call(
        soap_early, grid=(3,), in_specs=[tile_spec()] * 5, out_specs=[tile_spec()] * 3,
        out_shape=tiles_of_three(3), compiler_params=params(32), cost_estimate=cost(10**9, 4 * 10**6), name="soap_early",
    )(first, stat_l, stat_r, left, right)


def run_soap_mid(flips, packed, left, right):
    return pl.pallas_call(
        soap_mid, grid=(3,),
        in_specs=[SM, pl.BlockSpec((1, PACK, 128), lambda i: (i, 0, 0)), tile_spec(), tile_spec()],
        out_specs=[tile_spec()] * 6, out_shape=tiles_of_three(6),
        compiler_params=params(32), cost_estimate=cost(10**9, 4 * 10**6), name="soap_mid",
    )(flips, packed, left, right)


def run_soap_late(*args):
    return pl.pallas_call(
        soap_late, in_specs=[SM] + [VM] * 10, out_specs=[VM] * 4,
        out_shape=tiles_of_three(3) + [shape((3, TILE, TILE), bf16)],
        scratch_shapes=[pltpu.VMEM((6, 3, TILE, 64), f32), pltpu.VMEM((3, TILE, TILE), f32)],
        compiler_params=params(56), cost_estimate=cost(10**9, 10**7), name="soap_late",
    )(*args)


def adamw(master, gradient, first, second, rate, decay):
    first_new = first_decay * first + (1.0 - first_decay) * gradient
    second_new = second_decay * second + (1.0 - second_decay) * gradient * gradient
    step_dir = (
        first_new
        / (1.0 - first_decay**STEP)
        / (jnp.sqrt(second_new / (1.0 - second_decay**STEP)) + adam_epsilon)
    )
    return (master * (1.0 - rate * decay) - rate * step_dir, first_new, second_new)


def swap(array, axis, r, size):
    return lax.ppermute(array, axis, [(i, i ^ r) for i in range(size)])


def swap_mp(array, r):
    return swap(array, "mp", r, 4)


def swap_dp(array, r):
    return swap(array, "dp", r, 32)


def gather_mp(array):
    return [array] + [swap_mp(array, r) for r in (1, 2, 3)]


def trade_mp(pieces):
    return [pieces[0]] + [swap_mp(pieces[r], r) for r in (1, 2, 3)]


def sum_four(pieces):
    return (pieces[0] + pieces[1]) + (pieces[2] + pieces[3])


def total_mp(array):
    return sum_four(gather_mp(array))


def total_dp(array):
    array = array + swap_dp(array, 1)
    array = sum_four([array] + [swap_dp(array, 2 * r) for r in (1, 2, 3)])
    return sum_four([array] + [swap_dp(array, 8 * r) for r in (1, 2, 3)])


def by_partner(array, index):
    return jnp.take(array, jnp.arange(array.shape[0]) ^ index, axis=0)


def shards(
    patches, image_ids, keep, labels, owners,
    soap_weight, soap_first, soap_second, stat_left, stat_right, basis_left, basis_right,
    embed_weight, embed_first, embed_second, head_weight, head_first, head_second,
    vectors, vector_first, vector_second,
):
    mp_index = lax.axis_index("mp")
    dp_index = lax.axis_index("dp")

    def tiled(flat_rows):
        return flat_rows.reshape(3, TILE, TILE)

    device, within = (owners // 3, owners % 3)
    partners = jnp.arange(4) ^ mp_index
    table = (device * 12 + within)[None, :] + 3 * partners[:, None]
    table = table.reshape(-1).astype(jnp.int32)
    relative = device ^ dp_index
    places = (((relative & 1) * 16 + (relative >> 1)) * 3 + within).astype(jnp.int32)
    my_slots = dp_index * 3 + jnp.arange(3)
    my_blocks = jnp.sum(
        jnp.where(owners[None, :] == my_slots[:, None], jnp.arange(96)[None, :], 0), axis=1
    )
    kind = my_blocks % 48
    flips = (kind < 12) | ((kind >= 16) & (kind < 32))

    master = tiled(soap_weight)
    low = master.astype(bf16)
    low = jnp.where(flips[:, None, None], jnp.swapaxes(low, 1, 2), low)
    slots = lax.all_gather(pack_tile(low), ("dp", "mp"), axis=0, tiled=True)

    head_low = lax.all_gather(head_weight.astype(bf16), "mp", axis=0, tiled=True)

    split_one = (2 * LAYERS + 1) * D
    gain_rows = vectors[:split_one].reshape(2 * LAYERS + 1, 4, TILE)
    gain_rows = widen([gain_rows[:, t] for t in range(4)], 1)[:, None, :]
    head_gains = vectors[split_one : split_one + 2 * LAYERS * HD].reshape(LAYERS, 2, HD)
    class_bias = vectors[vectors.shape[0] - CLASSES :]

    tokens = by_partner(patches.reshape(4, OWN, D), mp_index)
    ids = by_partner(image_ids.reshape(4, OWN), mp_index)
    kept = by_partner(keep.reshape(4, OWN), mp_index) == 1
    query_ids = ids.reshape(1, TOKENS)
    key_ids = jnp.where(kept, ids, -1).reshape(TOKENS, 1)
    member_all = (image_ids[0, :, None] == jnp.arange(IMGS)[None, :]) & (keep[0, :, None] == 1)
    counts = jnp.sum(member_all.astype(f32), axis=0)
    present = (counts > 0).astype(f32)
    divisor = jnp.maximum(counts, 1.0)
    member = ((ids[0][:, None] == jnp.arange(IMGS)[None, :]) & kept[0][:, None]).astype(f32)
    image_sum = total_dp(jnp.full((8, 128), jnp.sum(present), f32))
    image_total = image_sum[0, 0]

    first_tiles, second_tiles = (tiled(soap_first), tiled(soap_second))
    left_stat, right_stat = (tiled(stat_left), tiled(stat_right))
    left, right = (tiled(basis_left), tiled(basis_right))
    turned_first, left_old, right_old = run_soap_early(first_tiles, left_stat, right_stat, left, right)

    embedded = jnp.dot(tokens.reshape(TOKENS, D), embed_weight.astype(bf16), preferred_element_type=f32)
    embedded = embedded.astype(bf16).reshape(4, OWN, TILE)
    embedded = by_partner(jnp.stack(trade_mp([embedded[r] for r in range(4)])), mp_index)
    resid = widen([embedded[t] for t in range(4)], 1).astype(f32)
    act = (normalize(resid)[0] * gain_rows[0]).astype(bf16)

    blocks = [layer_blocks(depth) for depth in range(LAYERS)]
    weights = [assemble(table, slots, blocks[0][:1]) + assemble(table, slots, blocks[0][1:])]
    weights += [assemble(table, slots, blocks[depth]) for depth in range(1, LAYERS)]
    index = jnp.full((1,), mp_index, jnp.int32)
    saved = []
    normed = None
    for depth in range(LAYERS):
        qkv, out, up, down = weights[depth]
        out = out.reshape(D, D)
        gains = head_gains[depth].T
        acts = gather_mp(act)
        if depth == 0:
            acts[0] = gate(acts[0], turned_first, second_tiles, image_sum)
        else:
            normed = gate(normed, *acts[1:], qkv)
            saved[-1].append(lax.all_gather(normed, "mp", axis=0, tiled=True))
        pre, v, lse, *o = run_attend_fwd(qkv, acts, gains, query_ids, key_ids)
        outs = trade_mp(o)
        if depth == 0:
            outs[0] = gate(outs[0], head_low)
        mid, u, normed, resid_next, act = run_mix_fwd(
            resid, outs, out, gain_rows[2 * depth + 1], gain_rows[2 * depth + 2], up, down
        )
        saved.append([resid, acts, pre, v, lse, o, mid, u])
        resid = resid_next
    saved[-1].append(lax.all_gather(normed, "mp", axis=0, tiled=True))

    resid = gate(resid, saved[0][-1])
    final, final_inverse = normalize(resid)
    gain_last = gain_rows[2 * LAYERS]
    pooled = total_mp(jnp.dot(member.T, final * gain_last, precision=highest)) / divisor[:, None]
    pooled = jnp.concatenate([pooled[:, :512].reshape(IMGS, 4, 128), pooled[:, 512:].reshape(IMGS, 4, 64)], axis=2)
    pooled_low = pooled.reshape(IMGS, D).astype(bf16)
    logits = jnp.dot(pooled_low, head_low, preferred_element_type=f32) + class_bias
    row_max = jnp.max(logits, -1, keepdims=True)
    exps = jnp.exp(logits - row_max)
    row_sum = jnp.sum(exps, -1, keepdims=True)
    log_norm = row_max[:, 0] + jnp.log(row_sum[:, 0])
    onehot = (jnp.arange(CLASSES)[None, :] == labels.reshape(-1)[:, None]).astype(f32)
    local_loss = jnp.sum((log_norm - jnp.sum(onehot * logits, -1)) * present)
    grad_logits = (exps / row_sum - onehot) * present[:, None] / image_total
    grad_bias = jnp.sum(grad_logits, 0)
    grad_logit_low = grad_logits.astype(bf16)
    pooled_mine = lax.dynamic_slice_in_dim(pooled_low, mp_index * TILE, TILE, 1)
    grad_head = jnp.dot(pooled_mine.T, grad_logit_low, preferred_element_type=f32)
    grad_pooled = jnp.dot(grad_logit_low, head_low.T, preferred_element_type=f32)
    grad_pooled = grad_pooled / divisor[:, None]
    grad_pooled = widen([grad_pooled[:, TILE * t : TILE * t + TILE] for t in range(4)], 1)
    grad_final = jnp.dot(member, grad_pooled, precision=highest)
    gain_grads = [wide_back(jnp.sum(grad_final * final, 0))]
    grad = norm_back(grad_final, gain_last, final, final_inverse)
    grad_low = grad.astype(bf16)

    buffers = waiting = None
    head_gain_grads = []
    for depth in reversed(range(LAYERS)):
        qkv, out, up, down = weights[depth]
        resid, acts, pre, v, lse, o, mid, u, normed = saved[depth]
        gains = head_gains[depth].T
        out = out.reshape(D, D)
        lows = lax.all_gather(grad_low, "mp", axis=0, tiled=True)
        mid_grad, mid_low, gain_two, *do = run_mix_bwd(
            grad, grad_low, mid, u, gain_rows[2 * depth + 1], out, up, down
        )
        dos = trade_mp(do)
        mid_lows = lax.all_gather(gate(mid_low, *dos[1:]), "mp", axis=0, tiled=True)
        if waiting is None:
            pre = gate(pre, normed)
        else:
            deeper, given, *rest = waiting
            buffers, token = run_head_grads(deeper, places, index, gate(given, do[0]), *rest, buffers)
            pre = gate(pre, token)
        *dp, gain_heads = run_attend_bwd(pre, v, lse, dos, gains, query_ids, key_ids)
        dps = trade_mp(dp)
        buffers, token = run_mlp_grads(depth, places, normed, lows, up, down, buffers)
        mid_grad = gate(mid_grad, token)
        grad, grad_low, gain_one = run_input_bwd(mid_grad, dps, qkv, resid, gain_rows[2 * depth])
        waiting = (depth, mid_lows, o, dp, acts)
        gain_grads = [wide_back(gain_one[0]), wide_back(gain_two[0])] + gain_grads
        head_gain_grads.insert(0, gain_heads.T)

    deeper, *rest = waiting
    buffers, token = run_head_grads(deeper, places, index, *rest, buffers)

    columns = trade_mp([wide_part(grad_low, mp_index ^ r, 1) for r in range(4)])
    columns[0] = gate(columns[0], token)
    columns = jnp.concatenate(columns, axis=0)
    grad_embed = jnp.dot(columns.T, tokens.reshape(TOKENS, D), preferred_element_type=f32)
    embed_rows = grad_embed.reshape(32, EMBED_ROWS, 128)
    head_rows = jnp.pad(grad_head, ((0, 0), (0, 24))).reshape(32, HEAD_ROWS, 128)
    vector_part = jnp.concatenate([jnp.concatenate(gain_grads), jnp.stack(head_gain_grads).reshape(-1)])
    vector_sum = jnp.concatenate([total_mp(vector_part), grad_bias, jnp.zeros((24,), f32)])
    vector_rows = jnp.pad(vector_sum.reshape(32, 160), ((0, 0), (0, 1536 - 160))).reshape(32, 12, 128)
    small = jnp.concatenate([embed_rows, head_rows, vector_rows], axis=1).astype(bf16)
    small = by_partner(small, dp_index).reshape(16, 2, SMALL, 128)
    keep_buffer = buffers[0].at[:, 3 * PACK :].set(small[:, 0])
    send_buffer = buffers[1].at[:, 3 * PACK :].set(small[:, 1])

    sums = run_add_core(keep_buffer, swap_dp(send_buffer, 1))
    sums = run_add_axis(
        [sums[0]] + [swap_dp(sums[r], 8 * r) for r in (1, 2, 3)],
        [sums[4]] + [swap_dp(sums[4 + r], 2 * r) for r in (1, 2, 3)],
    )
    mine = jnp.concatenate(
        [
            sum_four([sums[0]] + [swap_dp(sums[r], 2 * r).astype(f32) for r in (1, 2, 3)]),
            sum_four([sums[4]] + [swap_dp(sums[4 + r], 8 * r).astype(f32) for r in (1, 2, 3)]),
        ],
        axis=0,
    )
    mine_slots = mine[: 3 * PACK]
    share = mine[3 * PACK :]
    cut_at = EMBED_ROWS + HEAD_ROWS
    local_squares = (
        jnp.sum(mine_slots * mine_slots)
        + jnp.sum(share[:cut_at] * share[:cut_at])
        + jnp.sum(share[cut_at:] * share[cut_at:]) * 0.25
    )
    def flat(tiles):
        return tiles.reshape(3, TILE * TILE)

    grad_tiles, turned, left_new, right_new, gram_left, gram_right = run_soap_mid(
        flips.astype(jnp.int32), mine_slots.reshape(3, PACK, 128), left, right
    )
    rows = jnp.arange(8)[:, None] + jnp.zeros((8, 128), jnp.int32)
    squares = total_mp(jnp.where(rows == 0, local_squares, local_loss * 0.25))
    squares = squares + swap_dp(squares, 1)
    squares = sum_four([squares] + [swap_dp(squares, 2 * r) for r in (1, 2, 3)])
    flats = [flat(grad_tiles), flat(turned), flat(gram_left), flat(gram_right)]
    squares = gate(squares, *flats)
    squares = sum_four([squares] + [swap_dp(squares, 8 * r) for r in (1, 2, 3)])
    squares, loss_total = (squares[0, 0], squares[1, 0])
    shares = lax.all_gather(share, "dp", axis=0)
    grad_norm = jnp.sqrt(squares)
    factor = clip_limit / jnp.maximum(grad_norm, clip_limit)

    grad_flat, turned_flat, gram_left, gram_right = flats
    weight_new, left_basis, right_basis, weight_low = run_soap_late(
        factor.reshape(1, 1), second_tiles, left, right, master, turned, turned_first,
        left_old, right_old, left_new, right_new,
    )
    turned_flat = turned_flat * factor
    soap_new = (
        flat(weight_new),
        first_decay * soap_first + (1.0 - first_decay) * (grad_flat * factor),
        second_decay * soap_second + (1.0 - second_decay) * turned_flat * turned_flat,
        second_decay * stat_left + (1.0 - second_decay) * (factor * (factor * gram_left)),
        second_decay * stat_right + (1.0 - second_decay) * (factor * (factor * gram_right)),
        flat(left_basis),
        flat(right_basis),
        flat(weight_low),
    )

    grad_embed = shares[:, :EMBED_ROWS].reshape(TILE, D)
    grad_head = shares[:, EMBED_ROWS:cut_at].reshape(TILE, 1024)[:, :CLASSES]
    grad_vector = shares[:, cut_at:].reshape(32, 1536)[:, :160].reshape(-1)[: vectors.shape[0]]
    embed_new = adamw(
        embed_weight.T, grad_embed * factor, embed_first.T, embed_second.T, matrix_rate, weight_decay
    )
    embed_new = tuple(entry.T for entry in embed_new)
    head_new = adamw(
        head_weight, grad_head * factor, head_first, head_second, matrix_rate, weight_decay
    )
    vector_new = adamw(vectors, grad_vector * factor, vector_first, vector_second, vector_rate, 0.0)
    return (loss_total, image_total, grad_norm, *soap_new, *embed_new, *head_new, *vector_new)


def solution(mesh):
    by_slot = P(("dp", "mp"), None)
    columns = P(None, "mp")
    rows = P("mp", None)
    return jax.shard_map(
        shards,
        mesh=mesh,
        in_specs=(P("dp", None, None), P("dp", None), P("dp", None), P("dp", None), P())
        + (by_slot,) * 7
        + (columns,) * 3
        + (rows,) * 3
        + (P(),) * 3,
        out_specs=(P(),) * 3 + (by_slot,) * 8 + (columns,) * 3 + (rows,) * 3 + (P(),) * 3,
        check_vma=False,
    )
```

```python
import jax
import jax.numpy as jnp
from jax import lax
from jax.experimental import pallas as pl
from jax.experimental.pallas import tpu as pltpu
from jax.sharding import PartitionSpec as P

D = 768
HD = 64
HEADS = 3
CLASSES = 1000
LAYERS = 2
IMGS = 8
STEP = 10
TILE = 192
TOKENS = 1024
OWN = 256
PACK = 288
SMALL = 96
ROWS = 3 * PACK + SMALL
EMBED_ROWS = 36
HEAD_ROWS = 48

first_decay = 0.9
second_decay = 0.95
weight_decay = 0.05
matrix_rate = 0.03
vector_rate = 0.3
clip_limit = 0.01
adam_epsilon = 1e-08
norm_epsilon = 1e-06
masked_score = -1e30
highest = lax.Precision.HIGHEST
f32 = jnp.float32
bf16 = jnp.bfloat16
MIB = 2**20
VM = pl.BlockSpec(memory_space=pltpu.VMEM)
SM = pl.BlockSpec(memory_space=pltpu.SMEM)
ANY = pl.BlockSpec(memory_space=pl.ANY)


def in_hbm(*arrays):
    return [pltpu.with_memory_space_constraint(array, pltpu.HBM) for array in arrays]


def params(mib):
    return pltpu.CompilerParams(vmem_limit_bytes=mib * MIB)


def cost(flops, moved, exps=0):
    return pl.CostEstimate(flops=flops, bytes_accessed=moved, transcendentals=exps)


def shape(dims, kind=f32):
    return jax.ShapeDtypeStruct(dims, kind)


def mm(a, b, ca=1, cb=0):
    return lax.dot_general(a, b, (((ca,), (cb,)), ((), ())), preferred_element_type=f32)


def mm_full(a, b, ca, cb):
    return lax.dot_general(
        a, b, (((ca,), (cb,)), ((), ())), precision=highest, preferred_element_type=f32
    )


def mm_split(a, b, ca, cb):
    a_high, b_high = (a.astype(bf16), b.astype(bf16))
    a_low = (a - a_high.astype(f32)).astype(bf16)
    b_low = (b - b_high.astype(f32)).astype(bf16)
    return mm(a_high, b_high, ca, cb) + (mm(a_high, b_low, ca, cb) + mm(a_low, b_high, ca, cb))


def normalize(values):
    centered = values - jnp.mean(values, -1, keepdims=True)
    inverse = lax.rsqrt(jnp.mean(centered * centered, -1, keepdims=True) + norm_epsilon)
    return centered * inverse, inverse


def norm_back(grad, gain, normed, inverse):
    scaled = grad * gain
    return inverse * (
        scaled
        - jnp.mean(scaled, -1, keepdims=True)
        - normed * jnp.mean(scaled * normed, -1, keepdims=True)
    )


def gauss_parts(value):
    size = jnp.abs(value) * 0.7071067811865476
    bell = jnp.exp(-size * size)
    t = 1.0 / (1.0 + 0.3275911 * size)
    poly = t * (
        0.254829592
        + t * (-0.284496736 + t * (1.421413741 + t * (-1.453152027 + t * 1.061405429)))
    )
    tail = 0.5 * poly * bell
    return jnp.where(value >= 0, 1.0 - tail, tail), bell


def gelu(value):
    return value * gauss_parts(value)[0]


def widen(parts, axis):
    return jnp.concatenate(
        [lax.slice_in_dim(x, 0, 128, axis=axis) for x in parts]
        + [lax.slice_in_dim(x, 128, TILE, axis=axis) for x in parts],
        axis=axis,
    )


def wide_part(array, k, axis):
    return jnp.concatenate(
        [
            lax.dynamic_slice_in_dim(array, 128 * k, 128, axis),
            lax.dynamic_slice_in_dim(array, 512 + 64 * k, 64, axis),
        ],
        axis=axis,
    )


def wide_back(vector):
    return jnp.concatenate([vector[:512].reshape(4, 128), vector[512:].reshape(4, 64)], axis=1).reshape(D)


def pack_tile(tile):
    half = TILE // 2
    right = tile[..., 128:]
    return jnp.concatenate(
        [
            tile[..., :128],
            jnp.concatenate([right[..., :half, :], right[..., half:, :]], axis=-1),
        ],
        axis=-2,
    )


def unpack_tile(packed):
    half = TILE // 2
    right = packed[..., TILE:, :]
    return jnp.concatenate(
        [
            packed[..., :TILE, :],
            jnp.concatenate([right[..., :64], right[..., 64:]], axis=-2),
        ],
        axis=-1,
    )


def assemble(table, slots, groups):
    half = TILE // 2
    sizes = [4 * len(group) for group in groups]
    lines = sum(sizes)
    wanted = [96 * r + block for group in groups for r in range(4) for line in group for block in line]

    def kernel(table_ref, slots_ref, *refs):
        outs = refs[: len(groups)]
        tiles, stage, in_sems, out_sems = refs[len(groups) :]

        def fetch(at, place):
            return pltpu.make_async_copy(slots_ref.at[place], tiles.at[at], in_sems.at[at])

        for at, entry in enumerate(wanted):
            fetch(at, table_ref[entry]).start()
        base = 0
        for out_ref, size in zip(outs, sizes):

            def step(line, carry):
                at = base + line
                for t in range(4):
                    fetch(4 * at + t, 0).wait()
                for t in range(4):
                    stage[at, :, 128 * t : 128 * t + 128] = tiles[4 * at + t, :TILE]
                for t in (0, 2):
                    first = tiles[4 * at + t, TILE:]
                    second = tiles[4 * at + t + 1, TILE:]
                    cols = slice(512 + 64 * t, 640 + 64 * t)
                    stage[at, :half, cols] = jnp.concatenate([first[:, :64], second[:, :64]], axis=1)
                    stage[at, half:, cols] = jnp.concatenate([first[:, 64:], second[:, 64:]], axis=1)
                pltpu.make_async_copy(stage.at[at], out_ref.at[line], out_sems.at[at]).start()
                return carry

            lax.fori_loop(0, size, step, 0)
            base += size
        base = 0
        for out_ref, size in zip(outs, sizes):

            def finish(line, carry):
                pltpu.make_async_copy(stage.at[base + line], out_ref.at[line], out_sems.at[base + line]).wait()
                return carry

            lax.fori_loop(0, size, finish, 0)
            base += size

    mats = pl.pallas_call(
        kernel,
        in_specs=[SM, ANY],
        out_specs=[ANY] * len(groups),
        out_shape=[shape((size, TILE, D), bf16) for size in sizes],
        scratch_shapes=[
            pltpu.VMEM((4 * lines, PACK, 128), bf16),
            pltpu.VMEM((lines, TILE, D), bf16),
            pltpu.SemaphoreType.DMA((4 * lines,)),
            pltpu.SemaphoreType.DMA((lines,)),
        ],
        compiler_params=params(60),
        cost_estimate=cost(0, 4 * lines * TILE * TILE * 4),
        name="assemble",
    )(table, slots)
    return [mat.reshape(4, len(group) * TILE, D) for mat, group in zip(mats, groups)]


def layer_blocks(depth):
    base = 48 * depth
    qkv = [[base + 3 * r + c for r in range(4)] for c in range(3)]
    out = [[base + 12 + t for t in range(4)]]
    up = [[base + 16 + 4 * r + t for r in range(4)] for t in range(4)]
    down = [[base + 32 + 4 * t + r for r in range(4)] for t in range(4)]
    return [qkv, out, up, down]


def column_norm(values):
    centered = values - jnp.mean(values, 0, keepdims=True)
    inverse = lax.rsqrt(jnp.mean(centered * centered, 0, keepdims=True) + norm_epsilon)
    return centered * inverse, inverse


def by_three(step):
    def turn(i, carry):
        for j in range(3):
            carry = step(3 * i + j, carry)
        return carry

    lax.fori_loop(0, 4 * HEADS // 3, turn, 0)


def attend_fwd(w_ref, a0, a1, a2, a3, gain_ref, qid_ref, kid_ref, pre_ref, v_ref, lse_ref, o0, o1, o2, o3, q_s, k_s, o_s):
    for r, a_ref in enumerate((a0, a1, a2, a3)):
        cols = slice(OWN * r, OWN * r + OWN)
        projected = mm(w_ref[0], a_ref[...], 1, 1)
        v_ref[:, cols] = projected[2 * TILE :].astype(bf16)
        pre_ref[:, cols] = projected[: 2 * TILE]
        for c in range(2):
            for h in range(HEADS):
                rows = slice(HD * h, HD * h + HD)
                part = projected[TILE * c + HD * h : TILE * c + HD * h + HD]
                low = (column_norm(part)[0] * gain_ref[:, c : c + 1]).astype(bf16)
                if c == 0:
                    q_s[r, rows, :] = low * bf16(0.125)
                else:
                    k_s[h, cols, :] = low.T

    def step(i, carry):
        h, t = (i // 4, i % 4)
        rows = pl.ds(pl.multiple_of(h * HD, HD), HD)
        cols = pl.ds(pl.multiple_of(t * OWN, OWN), OWN)
        scores = mm(k_s[h], q_s[t, rows, :])
        scores = jnp.where(kid_ref[...] == qid_ref[:, cols], scores, masked_score)
        top = jnp.max(scores, 0, keepdims=True)
        weights = jnp.exp(scores - top)
        total = jnp.sum(weights, 0, keepdims=True)
        lse_ref[h, :, cols] = top + jnp.log(total)
        probs = (weights * (1.0 / total)).astype(bf16)
        o_s[t, rows, :] = mm(v_ref[rows, :], probs).astype(bf16)
        return carry

    by_three(step)
    for r, ref in enumerate((o0, o1, o2, o3)):
        ref[...] = o_s[r]


def run_attend_fwd(w, acts, gains, qid, kid):
    return pl.pallas_call(
        attend_fwd,
        grid=(1,),
        in_specs=[pl.BlockSpec((1, 3 * TILE, D), lambda i: (0, 0, 0))] + [VM] * 7,
        out_specs=[VM] * 7,
        out_shape=[
            shape((2 * TILE, TOKENS)),
            shape((TILE, TOKENS), bf16),
            shape((HEADS, 1, TOKENS)),
        ]
        + [shape((TILE, OWN), bf16)] * 4,
        scratch_shapes=[
            pltpu.VMEM((4, TILE, OWN), bf16),
            pltpu.VMEM((HEADS, TOKENS, HD), bf16),
            pltpu.VMEM((4, TILE, OWN), bf16),
        ],
        compiler_params=params(60),
        cost_estimate=cost(10**10, 6 * 10**6, 3 * 2**20),
        name="attend_fwd",
    )(*in_hbm(w), *acts, gains, qid, kid)


def attend_bwd(
    pre_ref, v_ref, lse_ref, g0, g1, g2, g3, gain_ref, qid_ref, kid_ref,
    p0, p1, p2, p3, dgain_ref, q_s, qn_s, k_s, kt_s, vn_s, do_s, dq_s, dk_s, dv_s,
):
    dp_refs = (p0, p1, p2, p3)
    for r, ref in enumerate((g0, g1, g2, g3)):
        do_s[r] = ref[...]
    for h in range(HEADS):
        rows = slice(HD * h, HD * h + HD)
        low = (column_norm(pre_ref[rows, :])[0] * gain_ref[:, 0:1]).astype(bf16)
        q_s[rows, :] = low * bf16(0.125)
        qn_s[h] = q_s[rows, :].T
        low = (column_norm(pre_ref[TILE + HD * h : TILE + HD * h + HD, :])[0] * gain_ref[:, 1:2]).astype(bf16)
        kt_s[rows, :] = low
        k_s[h] = low.T
        vn_s[h] = v_ref[rows, :].T
    dk_s[...] = jnp.zeros_like(dk_s)
    dv_s[...] = jnp.zeros_like(dv_s)

    def step(i, carry):
        h, t = (i // 4, i % 4)
        rows = pl.ds(pl.multiple_of(h * HD, HD), HD)
        cols = pl.ds(pl.multiple_of(t * OWN, OWN), OWN)
        scores = mm(k_s[h], q_s[rows, cols])
        scores = jnp.where(kid_ref[...] == qid_ref[:, cols], scores, masked_score)
        weights = jnp.exp(scores - lse_ref[h, :, cols])
        grad_out = do_s[t, rows, :]
        grad_weights = mm(vn_s[h], grad_out)
        dv_s[h] += mm(weights.astype(bf16), grad_out.T)
        inner = jnp.sum(weights * grad_weights, 0, keepdims=True)
        grad_scores = (weights * (grad_weights - inner)).astype(bf16)
        dq_s[rows, cols] = mm(kt_s[rows, :], grad_scores) * 0.125
        dk_s[h] += mm(grad_scores, qn_s[h, cols, :])
        return carry

    by_three(step)
    for c in range(2):
        total = jnp.zeros((HD, 1), f32)
        for h in range(HEADS):
            grad = dq_s[HD * h : HD * h + HD, :] if c == 0 else dk_s[h].T
            base = TILE * c + HD * h
            normed, inverse = column_norm(pre_ref[base : base + HD, :])
            total = total + jnp.sum(grad * normed, 1, keepdims=True)
            scaled = grad * gain_ref[:, c : c + 1]
            back = inverse * (
                scaled
                - jnp.mean(scaled, 0, keepdims=True)
                - normed * jnp.mean(scaled * normed, 0, keepdims=True)
            )
            for r in range(4):
                dp_refs[r][base : base + HD, :] = back[:, OWN * r : OWN * r + OWN].astype(bf16)
        dgain_ref[:, c : c + 1] = total
    for h in range(HEADS):
        back = dv_s[h].T.astype(bf16)
        for r in range(4):
            dp_refs[r][2 * TILE + HD * h : 2 * TILE + HD * h + HD, :] = back[:, OWN * r : OWN * r + OWN]


def run_attend_bwd(pre, v, lse, grads, gains, qid, kid):
    return pl.pallas_call(
        attend_bwd,
        in_specs=[VM] * 10,
        out_specs=[VM] * 5,
        out_shape=[shape((3 * TILE, OWN), bf16)] * 4 + [shape((HD, 2))],
        scratch_shapes=[
            pltpu.VMEM((TILE, TOKENS), bf16),
            pltpu.VMEM((HEADS, TOKENS, HD), bf16),
            pltpu.VMEM((HEADS, TOKENS, HD), bf16),
            pltpu.VMEM((TILE, TOKENS), bf16),
            pltpu.VMEM((HEADS, TOKENS, HD), bf16),
            pltpu.VMEM((4, TILE, OWN), bf16),
            pltpu.VMEM((TILE, TOKENS), f32),
            pltpu.VMEM((HEADS, TOKENS, HD), f32),
            pltpu.VMEM((HEADS, TOKENS, HD), f32),
        ],
        compiler_params=params(60),
        cost_estimate=cost(2 * 10**10, 6 * 10**6, 3 * 2**20),
        name="attend_bwd",
    )(pre, v, lse, *grads, gains, qid, kid)


def fetches(sources, targets, sems):
    copies = [
        pltpu.make_async_copy(source, target, sems.at[at])
        for at, (source, target) in enumerate(zip(sources, targets))
    ]
    for copy in copies:
        copy.start()
    return copies


def mix_fwd(x_ref, o0, o1, o2, o3, gain_ref, next_ref, out_hbm, up_hbm, down_hbm,
            mid_ref, c_ref, x_out, a_out, out_s, up_s, down_s, sems):
    sources, targets = ([out_hbm], [out_s])
    for r in range(4):
        sources += [up_hbm.at[r], down_hbm.at[r]]
        targets += [up_s.at[r], down_s.at[r]]
    copies = fetches(sources, targets, sems)
    copies[0].wait()
    total = x_ref[...]
    for k, ref in enumerate((o0, o1, o2, o3)):
        total = total + mm(ref[...], out_s[TILE * k : TILE * k + TILE, :], 0, 0)
    mid_ref[...] = total
    low = (normalize(total)[0] * gain_ref[...]).astype(bf16)
    c_ref[...] = low
    x_out[...] = total
    for r in range(4):
        copies[1 + 2 * r].wait()
        u = mm(low, up_s[r], 1, 1)
        copies[2 + 2 * r].wait()
        x_out[...] += mm(gelu(u).astype(bf16), down_s[r])
    a_out[...] = (normalize(x_out[...])[0] * next_ref[...]).astype(bf16)


def weight_scratch():
    return [
        pltpu.VMEM((D, D), bf16),
        pltpu.VMEM((4, D, D), bf16),
        pltpu.VMEM((4, D, D), bf16),
        pltpu.SemaphoreType.DMA((9,)),
    ]


def run_mix_fwd(x, outs, w_out, gain, gain_next, up, down):
    return pl.pallas_call(
        mix_fwd,
        in_specs=[VM] * 7 + [ANY] * 3,
        out_specs=[VM] * 4,
        out_shape=[shape((OWN, D)), shape((OWN, D), bf16), shape((OWN, D)), shape((OWN, D), bf16)],
        scratch_shapes=weight_scratch(),
        compiler_params=params(60),
        cost_estimate=cost(6 * 10**9, 17 * 10**6, 10**6),
        name="mix_fwd",
    )(x, *outs, gain, gain_next, *in_hbm(w_out, up, down))


def mix_bwd(g_ref, low_ref, mid_ref, c_ref, gain_ref, out_hbm, up_hbm, down_hbm,
            mid_grad, mid_low, dgain_ref, do0, do1, do2, do3, out_s, up_s, down_s, sems, acc):
    sources, targets = ([], [])
    for r in range(4):
        sources += [down_hbm.at[r], up_hbm.at[r]]
        targets += [down_s.at[r], up_s.at[r]]
    copies = fetches(sources + [out_hbm], targets + [out_s], sems)
    acc[...] = jnp.zeros_like(acc)
    for r in range(4):
        copies[2 * r].wait()
        df = mm(low_ref[...], down_s[r], 1, 1)
        copies[2 * r + 1].wait()
        u = mm(c_ref[...], up_s[r], 1, 1)
        cdf, bell = gauss_parts(u)
        du = (df * (cdf + u * bell * 0.3989422804014327)).astype(bf16)
        acc[...] += mm(du, up_s[r])
    normed, inverse = normalize(mid_ref[...])
    grad = acc[...]
    dgain_ref[...] = jnp.sum(grad * normed, 0, keepdims=True)
    total = g_ref[...] + norm_back(grad, gain_ref[...], normed, inverse)
    mid_grad[...] = total
    low = total.astype(bf16)
    mid_low[...] = low
    copies[8].wait()
    for k, ref in enumerate((do0, do1, do2, do3)):
        ref[...] = mm(out_s[TILE * k : TILE * k + TILE, :], low, 1, 1).astype(bf16)


def run_mix_bwd(grad, grad_low, mid, normed, gain, w_out, up, down):
    return pl.pallas_call(
        mix_bwd,
        in_specs=[VM] * 5 + [ANY] * 3,
        out_specs=[VM] * 7,
        out_shape=[shape((OWN, D)), shape((OWN, D), bf16), shape((1, D))] + [shape((TILE, OWN), bf16)] * 4,
        scratch_shapes=weight_scratch() + [pltpu.VMEM((OWN, D), f32)],
        compiler_params=params(60),
        cost_estimate=cost(6 * 10**9, 17 * 10**6, 10**6),
        name="mix_bwd",
    )(grad, grad_low, mid, normed, gain, *in_hbm(w_out, up, down))


def input_bwd(mid_grad, d0, d1, d2, d3, w_ref, x_ref, gain_ref, grad_ref, low_ref, dgain_ref):
    grad = mm(d0[...], w_ref[0], 0, 0)
    for k, ref in ((1, d1), (2, d2), (3, d3)):
        grad = grad + mm(ref[...], w_ref[k], 0, 0)
    normed, inverse = normalize(x_ref[...])
    dgain_ref[...] = jnp.sum(grad * normed, 0, keepdims=True)
    total = mid_grad[...] + norm_back(grad, gain_ref[...], normed, inverse)
    grad_ref[...] = total
    low_ref[...] = total.astype(bf16)


def run_input_bwd(mid_grad, grads, w, x, gain):
    return pl.pallas_call(
        input_bwd,
        in_specs=[VM] * 8,
        out_specs=[VM] * 3,
        out_shape=[shape((OWN, D)), shape((OWN, D), bf16), shape((1, D))],
        compiler_params=params(48),
        cost_estimate=cost(10**9, 6 * 10**6),
        name="input_bwd",
    )(mid_grad, *grads, w, x, gain)


def pack_wide(line, t):
    half = TILE // 2
    right = line[:, 512 + 64 * t : 576 + 64 * t]
    return jnp.concatenate(
        [
            line[:, 128 * t : 128 * t + 128],
            jnp.concatenate([right[:half], right[half:]], axis=1),
        ],
        axis=0,
    )


def send_line(places, stage, sems, keep, send, line, blocks, base):
    line = line.astype(bf16)
    for t, block in enumerate(blocks):
        at = base + t
        stage[at] = pack_wide(line, t)
        place = places[block]
        rows = pl.ds(pl.multiple_of((place % 3) * PACK, 16), PACK)

        @pl.when(place < 48)
        def _():
            pltpu.make_async_copy(stage.at[at], keep.at[place // 3, rows], sems.at[at]).start()

        @pl.when(place >= 48)
        def _():
            pltpu.make_async_copy(stage.at[at], send.at[place // 3 - 16, rows], sems.at[at]).start()


def wait_tiles(stage, sems, keep, count):
    for at in range(count):
        pltpu.make_async_copy(stage.at[at], keep.at[0, pl.ds(0, PACK)], sems.at[at]).wait()


def mlp_grads(depth, places, act_ref, low_ref, up_ref, down_ref, *refs):
    keep, send, token, stage, sems = refs[-5:]
    base = 48 * depth
    for i in range(4):
        rows = slice(TILE * i, TILE * i + TILE)
        u = mm(up_ref[0, rows, :], act_ref[...], 1, 1)
        df = mm(down_ref[0, rows, :], low_ref[...], 1, 1)
        cdf, bell = gauss_parts(u)
        f_low = (u * cdf).astype(bf16)
        du_low = (df * (cdf + u * bell * 0.3989422804014327)).astype(bf16)
        line = mm(du_low, act_ref[...])
        send_line(places, stage, sems, keep, send, line, [base + 16 + 4 * t + i for t in range(4)], 4 * i)
        line = mm(f_low, low_ref[...])
        send_line(places, stage, sems, keep, send, line, [base + 32 + 4 * i + t for t in range(4)], 16 + 4 * i)
    token[...] = jnp.zeros_like(token)
    wait_tiles(stage, sems, keep, 32)


def head_grads(depth, places, index, mid_ref, *refs):
    outs, grads, acts = (refs[0:4], refs[4:8], refs[8:12])
    keep, send, token, stage, sems = refs[-5:]
    base = 48 * depth
    parts = []
    for r in range(4):
        rows = pl.ds(pl.multiple_of((index[0] ^ r) * OWN, OWN), OWN)
        parts.append(mm(outs[r][...], mid_ref[rows, :]))
    line = (parts[0] + parts[1]) + (parts[2] + parts[3])
    send_line(places, stage, sems, keep, send, line, [base + 12 + t for t in range(4)], 12)
    for c in range(3):
        rows = slice(TILE * c, TILE * c + TILE)
        parts = [mm(grads[r][rows, :], acts[r][...]) for r in range(4)]
        line = (parts[0] + parts[1]) + (parts[2] + parts[3])
        send_line(places, stage, sems, keep, send, line, [base + 3 * t + c for t in range(4)], 4 * c)
    token[...] = jnp.zeros_like(token)
    wait_tiles(stage, sems, keep, 16)


def grads_call(kernel, name, scalars, args, specs, buffers, count, flops):
    given = list(buffers) if buffers is not None else []
    first = len(scalars) + len(args)
    *buffers, token = pl.pallas_call(
        kernel,
        grid=(1,),
        in_specs=[SM] * len(scalars) + specs + [ANY] * len(given),
        out_specs=[ANY, ANY, VM],
        out_shape=[shape((16, ROWS, 128), bf16)] * 2 + [shape((8, 128))],
        input_output_aliases={first + i: i for i in range(len(given))},
        scratch_shapes=[pltpu.VMEM((count, PACK, 128), bf16), pltpu.SemaphoreType.DMA((count,))],
        compiler_params=params(56),
        cost_estimate=cost(flops, 10**7),
        name=name,
    )(*scalars, *args, *given)
    return buffers, token


def run_mlp_grads(depth, places, pair, up, down, buffers):
    first = pl.BlockSpec((1, D, D), lambda i: (0, 0, 0))
    sides = [pl.BlockSpec((TOKENS, D), lambda i, side=side: (0, side)) for side in range(2)]
    if isinstance(pair, tuple):
        sides = [VM] * 2
    else:
        pair = (pair, pair)
    return grads_call(
        lambda *refs: mlp_grads(depth, *refs), "mlp_grads", [places],
        in_hbm(*pair, up, down), sides + [first] * 2, buffers, 32, 5 * 10**9,
    )


def run_head_grads(depth, places, index, mid_low, outs, grads, acts, buffers):
    return grads_call(
        lambda *refs: head_grads(depth, *refs), "head_grads", [places, index],
        [*in_hbm(mid_low), *outs, *grads, *acts], [VM] * 13, buffers, 16, 2 * 10**9,
    )


def whole(*dims):
    return pl.BlockSpec(dims, lambda r: (0,) * len(dims))


def part(*dims):
    return pl.BlockSpec((1, *dims), lambda r: (r,) + (0,) * len(dims))


def add_core(keep, got, own_a, a1, a2, a3, own_b, b1, b2, b3):
    step = pl.program_id(0)
    half = ROWS // 2
    total = keep[...].astype(f32) + got[...].astype(f32)

    @pl.when(step == 0)
    def _():
        own_a[...] = total[:, :half]

    for k, ref in ((1, a1), (2, a2), (3, a3)):

        @pl.when(step == k)
        def _():
            ref[...] = total[:, :half].astype(bf16)

    own_b[0] = total[0, half:]
    for k, ref in ((1, b1), (2, b2), (3, b3)):
        ref[0] = total[k, half:].astype(bf16)


def run_add_core(keep, got):
    half = ROWS // 2
    block = pl.BlockSpec((4, ROWS, 128), lambda r: (r, 0, 0))
    one, many = (whole(4, half, 128), part(half, 128))
    return pl.pallas_call(
        add_core, grid=(4,), in_specs=[block] * 2, out_specs=[one] * 4 + [many] * 4,
        out_shape=([shape((4, half, 128))] + [shape((4, half, 128), bf16)] * 3) * 2,
        compiler_params=params(32), cost_estimate=cost(10**7, 14 * 10**6), name="add_core",
    )(keep, got)


def add_axis(*refs):
    ins, outs = (refs[:8], refs[8:])
    for side in range(2):
        own, r1, r2, r3 = ins[4 * side : 4 * side + 4]
        for k in range(4):
            total = (own[k] + r1[k].astype(f32)) + (r2[k].astype(f32) + r3[k].astype(f32))
            out = outs[4 * side + k]
            out[...] = total.astype(out.dtype)


def run_add_axis(a, b):
    half = ROWS // 2
    return pl.pallas_call(
        add_axis, in_specs=[VM] * 8, out_specs=[VM] * 8,
        out_shape=([shape((half, 128))] + [shape((half, 128), bf16)] * 3) * 2,
        compiler_params=params(32), cost_estimate=cost(10**7, 6 * 10**6), name="add_axis",
    )(*a, *b)


def gate(array, *others):
    return pl.pallas_call(
        lambda *refs: None, in_specs=[ANY] * (1 + len(others)), out_specs=ANY,
        out_shape=shape(array.shape, array.dtype), input_output_aliases={0: 0},
        compiler_params=params(16), name="gate",
    )(array, *[in_hbm(other)[0] if other.size > 2**17 else other for other in others])


def soap_early(first, stat_l, stat_r, left, right, turned_ref, l_ref, r_ref):
    turned_ref[0] = mm_split(mm_split(left[0], first[0], 0, 0), right[0], 1, 0)
    l_ref[0] = mm_full(stat_l[0], left[0], 1, 0)
    r_ref[0] = mm_full(stat_r[0], right[0], 1, 0)


def soap_mid(flip_ref, packed, left, right, grad_ref, turned_ref, yl_ref, yr_ref, gl_ref, gr_ref):
    tile = unpack_tile(packed[0])
    turned_tile = tile.T
    flip = flip_ref[pl.program_id(0)] == 1
    grad = jnp.where(flip, turned_tile, tile)
    grad_t = jnp.where(flip, tile, turned_tile)
    grad_ref[0] = grad
    right_part = mm_full(grad, right[0], 1, 0)
    turned_ref[0] = mm_split(left[0], right_part, 0, 0)
    yr_ref[0] = mm_full(grad_t, right_part, 1, 0)
    yl_ref[0] = mm_full(grad, mm_full(grad_t, left[0], 1, 0), 1, 0)
    gl_ref[0] = mm_full(grad, grad_t, 1, 0)
    gr_ref[0] = mm_full(grad_t, grad, 1, 0)


def factor_inverses(grams, fillers=()):
    size = 64
    fillers = list(fillers)
    row = lax.broadcasted_iota(jnp.int32, (8, 128), 0)
    lane = lax.broadcasted_iota(jnp.int32, (8, 128), 1)
    on_diagonal = lax.broadcasted_iota(jnp.int32, (size, size), 0) == lax.broadcasted_iota(
        jnp.int32, (size, size), 1
    )
    states, scales = ([], [])
    for gram in grams:
        diagonal = jnp.where(on_diagonal, gram, 0.0)
        scale_row = lax.rsqrt(jnp.sum(diagonal, axis=0, keepdims=True))
        scale_column = lax.rsqrt(jnp.sum(diagonal, axis=1, keepdims=True))
        scales.append(scale_row)
        wide = jnp.concatenate([gram * scale_row * scale_column, jnp.zeros((size, size), f32)], axis=1)
        states.append(
            [jnp.where(lane == row + (size + 8 * t), 1.0, wide[8 * t : 8 * t + 8, :]) for t in range(8)]
        )
    for k in range(0, size, 2):
        home, at = divmod(k, 8)
        for tiles in states:
            own = tiles[home]
            first, second = (own[at : at + 1, :], own[at + 1 : at + 2, :])
            a, b, c = (
                jnp.broadcast_to(entry, (1, 128))
                for entry in (first[:, k : k + 1], first[:, k + 1 : k + 2], second[:, k + 1 : k + 2])
            )
            inverse = 1.0 / (a * c - b * b)
            line_first = (c * first - b * second) * inverse
            line_second = (a * second - b * first) * inverse
            for t in range(home, 8):
                update = tiles[t][:, k : k + 1] * line_first + tiles[t][:, k + 1 : k + 2] * line_second
                if t == home:
                    inside = jnp.where(row == at + 1, first * (b / a), 0.0)
                    update = jnp.where(row > at + 1, update, inside)
                tiles[t] = tiles[t] - update
        if fillers:
            fillers.pop(0)()
    for filler in fillers:
        filler()
    inverses = []
    for tiles, scale_row in zip(states, scales):
        done = []
        for t in range(8):
            diagonal = jnp.sum(jnp.where(lane == row + 8 * t, tiles[t], 0.0), axis=1, keepdims=True)
            done.append(tiles[t] * lax.rsqrt(diagonal))
        inverses.append(jnp.concatenate(done, axis=0)[:, size:] * scale_row)
    return inverses


def soap_late(
    f_ref, second, left, right, weight, turned, turned_first, xl, xr, yl, yr,
    weight_ref, left_ref, right_ref, panels, work,
):
    factor = f_ref[0, 0]
    bias_one = 1.0 - first_decay**STEP
    bias_two = 1.0 - second_decay**STEP
    outs = (left_ref, right_ref)

    def product(i):
        n, (old, new) = (i // 2, ((xl, yl), (xr, yr))[i % 2])
        total = second_decay * old[n] + (1.0 - second_decay) * (factor * (factor * new[n]))
        for j in range(3):
            panels[i, j] = total[:, 64 * j : 64 * j + 64]

    def scaled(n):
        rotated = turned[n] * factor
        second_new = second_decay * second[n] + (1.0 - second_decay) * rotated * rotated
        work[n] = (
            (first_decay * turned_first[n] + (1.0 - first_decay) * rotated)
            / bias_one
            / (jnp.sqrt(second_new / bias_two) + adam_epsilon)
        )

    def half_back(n):
        work[n] = mm_split(left[n], work[n], 1, 0)

    def move(n):
        back = mm_split(work[n], right[n], 1, 1)
        weight_new = weight[n] * (1.0 - matrix_rate * weight_decay) - matrix_rate * back
        weight_ref[n] = weight_new

    def remove(i, basis, k):
        panel = panels[i, k]
        panels[i, k] = panel - mm_full(basis, mm_full(basis, panel, 0, 0), 1, 0)

    def grams(j):
        return [mm_full(panels[i, j], panels[i, j], 0, 0) for i in range(6)]

    def bases(j, inverses):
        found = []
        for i in range(6):
            basis = mm_full(panels[i, j], inverses[i], 1, 1)
            outs[i % 2][i // 2, :, 64 * j : 64 * j + 64] = basis
            found.append(basis)
        return found

    for i in range(6):
        product(i)
    pieces = [lambda step=step, n=n: step(n) for n in range(3) for step in (scaled, half_back, move)]
    found = bases(0, factor_inverses(grams(0), pieces))
    for i in range(6):
        remove(i, found[i], 1)
    pieces = [lambda i=i, basis=found[i]: remove(i, basis, 2) for i in range(6)]
    found = bases(1, factor_inverses(grams(1), pieces))
    for i in range(6):
        remove(i, found[i], 2)
    bases(2, factor_inverses(grams(2)))


def tile_spec():
    return pl.BlockSpec((1, TILE, TILE), lambda i: (i, 0, 0))


def tiles_of_three(count):
    return [shape((3, TILE, TILE))] * count


def run_soap_early(first, stat_l, stat_r, left, right):
    return pl.pallas_call(
        soap_early, grid=(3,), in_specs=[tile_spec()] * 5, out_specs=[tile_spec()] * 3,
        out_shape=tiles_of_three(3), compiler_params=params(32), cost_estimate=cost(10**9, 4 * 10**6), name="soap_early",
    )(first, stat_l, stat_r, left, right)


def run_soap_mid(flips, packed, left, right):
    return pl.pallas_call(
        soap_mid, grid=(3,),
        in_specs=[SM, pl.BlockSpec((1, PACK, 128), lambda i: (i, 0, 0)), tile_spec(), tile_spec()],
        out_specs=[tile_spec()] * 6, out_shape=tiles_of_three(6),
        compiler_params=params(32), cost_estimate=cost(10**9, 4 * 10**6), name="soap_mid",
    )(flips, packed, left, right)


def run_soap_late(*args):
    return pl.pallas_call(
        soap_late, in_specs=[SM] + [VM] * 10, out_specs=[VM] * 3,
        out_shape=tiles_of_three(3),
        scratch_shapes=[pltpu.VMEM((6, 3, TILE, 64), f32), pltpu.VMEM((3, TILE, TILE), f32)],
        compiler_params=params(56), cost_estimate=cost(10**9, 10**7), name="soap_late",
    )(*args)


def adamw(master, gradient, first, second, rate, decay):
    first_new = first_decay * first + (1.0 - first_decay) * gradient
    second_new = second_decay * second + (1.0 - second_decay) * gradient * gradient
    step_dir = (
        first_new
        / (1.0 - first_decay**STEP)
        / (jnp.sqrt(second_new / (1.0 - second_decay**STEP)) + adam_epsilon)
    )
    return (master * (1.0 - rate * decay) - rate * step_dir, first_new, second_new)


def swap(array, axis, r, size):
    return lax.ppermute(array, axis, [(i, i ^ r) for i in range(size)])


def swap_mp(array, r):
    return swap(array, "mp", r, 4)


def swap_dp(array, r):
    return swap(array, "dp", r, 32)


def gather_mp(array):
    return [array] + [swap_mp(array, r) for r in (1, 2, 3)]


def trade_mp(pieces):
    return [pieces[0]] + [swap_mp(pieces[r], r) for r in (1, 2, 3)]


def sum_four(pieces):
    return (pieces[0] + pieces[1]) + (pieces[2] + pieces[3])


def total_mp(array):
    return sum_four(gather_mp(array))


def total_dp(array):
    array = array + swap_dp(array, 1)
    array = sum_four([array] + [swap_dp(array, 2 * r) for r in (1, 2, 3)])
    return sum_four([array] + [swap_dp(array, 8 * r) for r in (1, 2, 3)])


def by_partner(array, index):
    return jnp.take(array, jnp.arange(array.shape[0]) ^ index, axis=0)


def shards(
    patches, image_ids, keep, labels, owners,
    soap_weight, soap_first, soap_second, stat_left, stat_right, basis_left, basis_right,
    embed_weight, embed_first, embed_second, head_weight, head_first, head_second,
    vectors, vector_first, vector_second,
):
    mp_index = lax.axis_index("mp")
    dp_index = lax.axis_index("dp")

    def tiled(flat_rows):
        return flat_rows.reshape(3, TILE, TILE)

    device, within = (owners // 3, owners % 3)
    partners = jnp.arange(4) ^ mp_index
    table = (device * 12 + within)[None, :] + 3 * partners[:, None]
    table = table.reshape(-1).astype(jnp.int32)
    relative = device ^ dp_index
    places = (((relative & 1) * 16 + (relative >> 1)) * 3 + within).astype(jnp.int32)
    my_slots = dp_index * 3 + jnp.arange(3)
    my_blocks = jnp.sum(
        jnp.where(owners[None, :] == my_slots[:, None], jnp.arange(96)[None, :], 0), axis=1
    )
    kind = my_blocks % 48
    flips = (kind < 12) | ((kind >= 16) & (kind < 32))

    master = tiled(soap_weight)
    low = master.astype(bf16)
    low = jnp.where(flips[:, None, None], jnp.swapaxes(low, 1, 2), low)
    slots = lax.all_gather(pack_tile(low), ("dp", "mp"), axis=0, tiled=True)

    head_low = lax.all_gather(head_weight.astype(bf16), "mp", axis=0, tiled=True)

    split_one = (2 * LAYERS + 1) * D
    split_two = split_one + 2 * LAYERS * HD
    gain_rows = vectors[:split_one].reshape(2 * LAYERS + 1, 4, TILE)
    gain_rows = widen([gain_rows[:, t] for t in range(4)], 1)[:, None, :]
    head_gains = vectors[split_one : split_one + 2 * LAYERS * HD].reshape(LAYERS, 2, HD)
    class_bias = vectors[vectors.shape[0] - CLASSES :]

    tokens = by_partner(patches.reshape(4, OWN, D), mp_index)
    ids = by_partner(image_ids.reshape(4, OWN), mp_index)
    kept = by_partner(keep.reshape(4, OWN), mp_index) == 1
    query_ids = ids.reshape(1, TOKENS)
    key_ids = jnp.where(kept, ids, -1).reshape(TOKENS, 1)
    member_all = (image_ids[0, :, None] == jnp.arange(IMGS)[None, :]) & (keep[0, :, None] == 1)
    counts = jnp.sum(member_all.astype(f32), axis=0)
    present = (counts > 0).astype(f32)
    divisor = jnp.maximum(counts, 1.0)
    member = ((ids[0][:, None] == jnp.arange(IMGS)[None, :]) & kept[0][:, None]).astype(f32)
    image_sum = total_dp(jnp.full((8, 128), jnp.sum(present), f32))
    image_total = image_sum[0, 0]

    first_tiles, second_tiles = (tiled(soap_first), tiled(soap_second))
    left_stat, right_stat = (tiled(stat_left), tiled(stat_right))
    left, right = (tiled(basis_left), tiled(basis_right))
    turned_first, left_old, right_old = run_soap_early(first_tiles, left_stat, right_stat, left, right)

    embedded = jnp.dot(tokens.reshape(TOKENS, D), embed_weight.astype(bf16), preferred_element_type=f32)
    embedded = embedded.astype(bf16).reshape(4, OWN, TILE)
    embedded = by_partner(jnp.stack(trade_mp([embedded[r] for r in range(4)])), mp_index)
    resid = widen([embedded[t] for t in range(4)], 1).astype(f32)
    act = (normalize(resid)[0] * gain_rows[0]).astype(bf16)

    blocks = [layer_blocks(depth) for depth in range(LAYERS)]
    weights = [assemble(table, slots, blocks[0][:1]) + assemble(table, slots, blocks[0][1:])]
    weights += [assemble(table, slots, blocks[depth]) for depth in range(1, LAYERS)]
    index = jnp.full((1,), mp_index, jnp.int32)
    saved = []
    normed = None
    for depth in range(LAYERS):
        qkv, out, up, down = weights[depth]
        out = out.reshape(D, D)
        gains = head_gains[depth].T
        acts = gather_mp(act)
        if depth == 0:
            acts[0] = gate(acts[0], turned_first, second_tiles, image_sum)
        else:
            normed = gate(normed, *acts[1:], qkv)
            gains = gate(gains, head_low)
            saved[-1].append(lax.all_gather(normed, "mp", axis=0, tiled=True))
        pre, v, lse, *o = run_attend_fwd(qkv, acts, gains, query_ids, key_ids)
        outs = trade_mp(o)
        mid, normed, resid_next, act = run_mix_fwd(
            resid, outs, out, gain_rows[2 * depth + 1], gain_rows[2 * depth + 2], up, down
        )
        saved.append([resid, acts, pre, v, lse, o, mid, normed])
        resid = resid_next
    saved[-1].append(None)

    final, final_inverse = normalize(resid)
    gain_last = gate(gain_rows[2 * LAYERS], saved[0][-1])
    pooled = total_mp(jnp.dot(member.T, final * gain_last, precision=highest)) / divisor[:, None]
    pooled = jnp.concatenate([pooled[:, :512].reshape(IMGS, 4, 128), pooled[:, 512:].reshape(IMGS, 4, 64)], axis=2)
    pooled_low = pooled.reshape(IMGS, D).astype(bf16)
    logits = jnp.dot(pooled_low, head_low, preferred_element_type=f32) + class_bias
    row_max = jnp.max(logits, -1, keepdims=True)
    exps = jnp.exp(logits - row_max)
    row_sum = jnp.sum(exps, -1, keepdims=True)
    log_norm = row_max[:, 0] + jnp.log(row_sum[:, 0])
    onehot = (jnp.arange(CLASSES)[None, :] == labels.reshape(-1)[:, None]).astype(f32)
    local_loss = jnp.sum((log_norm - jnp.sum(onehot * logits, -1)) * present)
    grad_logits = (exps / row_sum - onehot) * present[:, None] / image_total
    grad_bias = jnp.sum(grad_logits, 0)
    grad_logit_low = grad_logits.astype(bf16)
    pooled_mine = lax.dynamic_slice_in_dim(pooled_low, mp_index * TILE, TILE, 1)
    grad_head = jnp.dot(pooled_mine.T, grad_logit_low, preferred_element_type=f32)
    grad_pooled = jnp.dot(grad_logit_low, head_low.T, preferred_element_type=f32)
    grad_pooled = grad_pooled / divisor[:, None]
    grad_pooled = widen([grad_pooled[:, TILE * t : TILE * t + TILE] for t in range(4)], 1)
    grad_final = jnp.dot(member, grad_pooled, precision=highest)
    gain_grads = [wide_back(jnp.sum(grad_final * final, 0))]
    grad = norm_back(grad_final, gain_last, final, final_inverse)
    grad_low = grad.astype(bf16)

    buffers = waiting = None
    head_gain_grads = []
    for depth in reversed(range(LAYERS)):
        qkv, out, up, down = weights[depth]
        resid, acts, pre, v, lse, o, mid, own_normed, normed = saved[depth]
        gains = head_gains[depth].T
        out = out.reshape(D, D)
        if normed is None:
            pair = lax.all_gather(jnp.concatenate([own_normed, grad_low], axis=1), "mp", axis=0, tiled=True)
        else:
            pair = (normed, lax.all_gather(grad_low, "mp", axis=0, tiled=True))
        mid_grad, mid_low, gain_two, *do = run_mix_bwd(
            grad, grad_low, mid, own_normed, gain_rows[2 * depth + 1], out, up, down
        )
        dos = trade_mp(do)
        mid_lows = lax.all_gather(gate(mid_low, *dos[1:]), "mp", axis=0, tiled=True)
        if waiting is not None:
            deeper, given, *rest = waiting
            buffers, token = run_head_grads(deeper, places, gate(index, dos[1]), given, *rest, buffers)
            gains = gate(gains, token)
        *dp, gain_heads = run_attend_bwd(pre, v, lse, dos, gains, query_ids, key_ids)
        dps = trade_mp(dp)
        buffers, token = run_mlp_grads(depth, places, pair, up, down, buffers)
        gain = gate(gain_rows[2 * depth], token)
        grad, grad_low, gain_one = run_input_bwd(mid_grad, dps, qkv, resid, gain)
        waiting = (depth, mid_lows, o, dp, acts)
        gain_grads = [wide_back(gain_one[0]), wide_back(gain_two[0])] + gain_grads
        head_gain_grads.insert(0, gain_heads.T)

    deeper, *rest = waiting
    buffers, token = run_head_grads(deeper, places, index, *rest, buffers)

    vector_part = jnp.concatenate([jnp.concatenate(gain_grads), jnp.stack(head_gain_grads).reshape(-1)])
    vector_part = jnp.pad(vector_part, (0, 32 * TILE - vector_part.shape[0])).reshape(32, TILE).astype(bf16)
    traded = trade_mp(
        [jnp.concatenate([wide_part(grad_low, mp_index ^ r, 1), vector_part], axis=0) for r in range(4)]
    )
    traded[0] = gate(traded[0], token)
    columns = jnp.concatenate([piece[:OWN] for piece in traded], axis=0)
    grad_embed = jnp.dot(columns.T, tokens.reshape(TOKENS, D), preferred_element_type=f32)
    embed_rows = grad_embed.reshape(32, EMBED_ROWS, 128)
    vector_total = sum_four([piece[OWN:].astype(f32) for piece in traded]).reshape(-1)
    head_rows = jnp.pad(grad_head, ((0, 0), (0, 24))).reshape(32, HEAD_ROWS, 128)
    vector_sum = jnp.concatenate([vector_total[:split_two], grad_bias, jnp.zeros((24,), f32)])
    vector_rows = jnp.pad(vector_sum.reshape(32, 160), ((0, 0), (0, 1536 - 160))).reshape(32, 12, 128)
    small = jnp.concatenate([embed_rows, head_rows, vector_rows], axis=1).astype(bf16)
    small = by_partner(small, dp_index).reshape(16, 2, SMALL, 128)
    keep_buffer = buffers[0].at[:, 3 * PACK :].set(small[:, 0])
    send_buffer = buffers[1].at[:, 3 * PACK :].set(small[:, 1])

    sums = run_add_core(keep_buffer, swap_dp(send_buffer, 1))
    sums = run_add_axis(
        [sums[0]] + [swap_dp(sums[r], 8 * r) for r in (1, 2, 3)],
        [sums[4]] + [swap_dp(sums[4 + r], 2 * r) for r in (1, 2, 3)],
    )
    mine = jnp.concatenate(
        [
            sum_four([sums[0]] + [swap_dp(sums[r], 2 * r).astype(f32) for r in (1, 2, 3)]),
            sum_four([sums[4]] + [swap_dp(sums[4 + r], 8 * r).astype(f32) for r in (1, 2, 3)]),
        ],
        axis=0,
    )
    mine_slots = mine[: 3 * PACK]
    share = mine[3 * PACK :]
    cut_at = EMBED_ROWS + HEAD_ROWS
    local_squares = (
        jnp.sum(mine_slots * mine_slots)
        + jnp.sum(share[:cut_at] * share[:cut_at])
        + jnp.sum(share[cut_at:] * share[cut_at:]) * 0.25
    )
    def flat(tiles):
        return tiles.reshape(3, TILE * TILE)

    grad_tiles, turned, left_new, right_new, gram_left, gram_right = run_soap_mid(
        flips.astype(jnp.int32), mine_slots.reshape(3, PACK, 128), left, right
    )
    rows = jnp.arange(8)[:, None] + jnp.zeros((8, 128), jnp.int32)
    squares = total_mp(jnp.where(rows == 0, local_squares, local_loss * 0.25))
    squares = squares + swap_dp(squares, 1)
    squares = sum_four([squares] + [swap_dp(squares, 2 * r) for r in (1, 2, 3)])
    flats = [flat(grad_tiles), flat(turned), flat(gram_left), flat(gram_right)]
    squares = gate(squares, *flats)
    squares = sum_four([squares] + [swap_dp(squares, 8 * r) for r in (1, 2, 3)])
    squares, loss_total = (squares[0, 0], squares[1, 0])
    shares = lax.all_gather(share, "dp", axis=0)
    grad_norm = jnp.sqrt(squares)
    factor = clip_limit / jnp.maximum(grad_norm, clip_limit)

    grad_flat, turned_flat, gram_left, gram_right = flats
    weight_new, left_basis, right_basis = run_soap_late(
        factor.reshape(1, 1), second_tiles, left, right, master, turned, turned_first,
        left_old, right_old, left_new, right_new,
    )
    turned_flat = turned_flat * factor
    weight_flat = flat(weight_new)
    soap_new = (
        weight_flat,
        first_decay * soap_first + (1.0 - first_decay) * (grad_flat * factor),
        second_decay * soap_second + (1.0 - second_decay) * turned_flat * turned_flat,
        second_decay * stat_left + (1.0 - second_decay) * (factor * (factor * gram_left)),
        second_decay * stat_right + (1.0 - second_decay) * (factor * (factor * gram_right)),
        flat(left_basis),
        flat(right_basis),
        weight_flat.astype(bf16),
    )

    grad_embed = shares[:, :EMBED_ROWS].reshape(TILE, D)
    grad_head = shares[:, EMBED_ROWS:cut_at].reshape(TILE, 1024)[:, :CLASSES]
    grad_vector = shares[:, cut_at:].reshape(32, 1536)[:, :160].reshape(-1)[: vectors.shape[0]]
    embed_new = adamw(
        embed_weight.T, grad_embed * factor, embed_first.T, embed_second.T, matrix_rate, weight_decay
    )
    embed_new = tuple(entry.T for entry in embed_new)
    head_new = adamw(
        head_weight, grad_head * factor, head_first, head_second, matrix_rate, weight_decay
    )
    vector_new = adamw(vectors, grad_vector * factor, vector_first, vector_second, vector_rate, 0.0)
    return (loss_total, image_total, grad_norm, *soap_new, *embed_new, *head_new, *vector_new)


def solution(mesh):
    by_slot = P(("dp", "mp"), None)
    columns = P(None, "mp")
    rows = P("mp", None)
    return jax.shard_map(
        shards,
        mesh=mesh,
        in_specs=(P("dp", None, None), P("dp", None), P("dp", None), P("dp", None), P())
        + (by_slot,) * 7
        + (columns,) * 3
        + (rows,) * 3
        + (P(),) * 3,
        out_specs=(P(),) * 3 + (by_slot,) * 8 + (columns,) * 3 + (rows,) * 3 + (P(),) * 3,
        check_vma=False,
    )
```

```python
import jax
import jax.numpy as jnp
from jax import lax
from jax.experimental import pallas as pl
from jax.experimental.pallas import tpu as pltpu
from jax.sharding import PartitionSpec as P

D = 768
HD = 64
HEADS = 3
CLASSES = 1000
LAYERS = 2
IMGS = 8
STEP = 10
TILE = 192
TOKENS = 1024
OWN = 256
PACK = 288
SMALL = 96
ROWS = 3 * PACK + SMALL
EMBED_ROWS = 36
HEAD_ROWS = 48

first_decay = 0.9
second_decay = 0.95
weight_decay = 0.05
matrix_rate = 0.03
vector_rate = 0.3
clip_limit = 0.01
adam_epsilon = 1e-08
norm_epsilon = 1e-06
masked_score = -1e30
highest = lax.Precision.HIGHEST
f32 = jnp.float32
bf16 = jnp.bfloat16
MIB = 2**20
VM = pl.BlockSpec(memory_space=pltpu.VMEM)
SM = pl.BlockSpec(memory_space=pltpu.SMEM)
ANY = pl.BlockSpec(memory_space=pl.ANY)


def in_hbm(*arrays):
    return [pltpu.with_memory_space_constraint(array, pltpu.HBM) for array in arrays]


def params(mib):
    return pltpu.CompilerParams(vmem_limit_bytes=mib * MIB)


def cost(flops, moved, exps=0):
    return pl.CostEstimate(flops=flops, bytes_accessed=moved, transcendentals=exps)


def shape(dims, kind=f32):
    return jax.ShapeDtypeStruct(dims, kind)


def mm(a, b, ca=1, cb=0):
    return lax.dot_general(a, b, (((ca,), (cb,)), ((), ())), preferred_element_type=f32)


def mm_full(a, b, ca, cb):
    return lax.dot_general(
        a, b, (((ca,), (cb,)), ((), ())), precision=highest, preferred_element_type=f32
    )


def mm_split(a, b, ca, cb):
    a_high, b_high = (a.astype(bf16), b.astype(bf16))
    a_low = (a - a_high.astype(f32)).astype(bf16)
    b_low = (b - b_high.astype(f32)).astype(bf16)
    return mm(a_high, b_high, ca, cb) + (mm(a_high, b_low, ca, cb) + mm(a_low, b_high, ca, cb))


def normalize(values):
    centered = values - jnp.mean(values, -1, keepdims=True)
    inverse = lax.rsqrt(jnp.mean(centered * centered, -1, keepdims=True) + norm_epsilon)
    return centered * inverse, inverse


def norm_back(grad, gain, normed, inverse):
    scaled = grad * gain
    return inverse * (
        scaled
        - jnp.mean(scaled, -1, keepdims=True)
        - normed * jnp.mean(scaled * normed, -1, keepdims=True)
    )


def gauss_parts(value):
    size = jnp.abs(value) * 0.7071067811865476
    bell = jnp.exp(-size * size)
    t = 1.0 / (1.0 + 0.3275911 * size)
    poly = t * (
        0.254829592
        + t * (-0.284496736 + t * (1.421413741 + t * (-1.453152027 + t * 1.061405429)))
    )
    tail = 0.5 * poly * bell
    return jnp.where(value >= 0, 1.0 - tail, tail), bell


def gelu(value):
    return value * gauss_parts(value)[0]


def widen(parts, axis):
    return jnp.concatenate(
        [lax.slice_in_dim(x, 0, 128, axis=axis) for x in parts]
        + [lax.slice_in_dim(x, 128, TILE, axis=axis) for x in parts],
        axis=axis,
    )


def wide_part(array, k, axis):
    return jnp.concatenate(
        [
            lax.dynamic_slice_in_dim(array, 128 * k, 128, axis),
            lax.dynamic_slice_in_dim(array, 512 + 64 * k, 64, axis),
        ],
        axis=axis,
    )


def wide_back(vector):
    return jnp.concatenate([vector[:512].reshape(4, 128), vector[512:].reshape(4, 64)], axis=1).reshape(D)


def pack_tile(tile):
    half = TILE // 2
    right = tile[..., 128:]
    return jnp.concatenate(
        [
            tile[..., :128],
            jnp.concatenate([right[..., :half, :], right[..., half:, :]], axis=-1),
        ],
        axis=-2,
    )


def unpack_tile(packed):
    half = TILE // 2
    right = packed[..., TILE:, :]
    return jnp.concatenate(
        [
            packed[..., :TILE, :],
            jnp.concatenate([right[..., :64], right[..., 64:]], axis=-2),
        ],
        axis=-1,
    )


def assemble(table, slots, groups):
    half = TILE // 2
    sizes = [4 * len(group) for group in groups]
    lines = sum(sizes)
    wanted = [96 * r + block for group in groups for r in range(4) for line in group for block in line]

    def kernel(table_ref, slots_ref, *refs):
        outs = refs[: len(groups)]
        tiles, stage, in_sems, out_sems = refs[len(groups) :]

        def fetch(at, place):
            return pltpu.make_async_copy(slots_ref.at[place], tiles.at[at], in_sems.at[at])

        for at, entry in enumerate(wanted):
            fetch(at, table_ref[entry]).start()
        base = 0
        for out_ref, size in zip(outs, sizes):

            def step(line, carry):
                at = base + line
                for t in range(4):
                    fetch(4 * at + t, 0).wait()
                for t in range(4):
                    stage[at, :, 128 * t : 128 * t + 128] = tiles[4 * at + t, :TILE]
                for t in (0, 2):
                    first = tiles[4 * at + t, TILE:]
                    second = tiles[4 * at + t + 1, TILE:]
                    cols = slice(512 + 64 * t, 640 + 64 * t)
                    stage[at, :half, cols] = jnp.concatenate([first[:, :64], second[:, :64]], axis=1)
                    stage[at, half:, cols] = jnp.concatenate([first[:, 64:], second[:, 64:]], axis=1)
                pltpu.make_async_copy(stage.at[at], out_ref.at[line], out_sems.at[at]).start()
                return carry

            lax.fori_loop(0, size, step, 0)
            base += size
        base = 0
        for out_ref, size in zip(outs, sizes):

            def finish(line, carry):
                pltpu.make_async_copy(stage.at[base + line], out_ref.at[line], out_sems.at[base + line]).wait()
                return carry

            lax.fori_loop(0, size, finish, 0)
            base += size

    mats = pl.pallas_call(
        kernel,
        in_specs=[SM, ANY],
        out_specs=[ANY] * len(groups),
        out_shape=[shape((size, TILE, D), bf16) for size in sizes],
        scratch_shapes=[
            pltpu.VMEM((4 * lines, PACK, 128), bf16),
            pltpu.VMEM((lines, TILE, D), bf16),
            pltpu.SemaphoreType.DMA((4 * lines,)),
            pltpu.SemaphoreType.DMA((lines,)),
        ],
        compiler_params=params(60),
        cost_estimate=cost(0, 4 * lines * TILE * TILE * 4),
        name="assemble",
    )(table, slots)
    return [mat.reshape(4, len(group) * TILE, D) for mat, group in zip(mats, groups)]


def layer_blocks(depth):
    base = 48 * depth
    qkv = [[base + 3 * r + c for r in range(4)] for c in range(3)]
    out = [[base + 12 + t for t in range(4)]]
    up = [[base + 16 + 4 * r + t for r in range(4)] for t in range(4)]
    down = [[base + 32 + 4 * t + r for r in range(4)] for t in range(4)]
    return [qkv, out, up, down]


def column_norm(values):
    centered = values - jnp.mean(values, 0, keepdims=True)
    inverse = lax.rsqrt(jnp.mean(centered * centered, 0, keepdims=True) + norm_epsilon)
    return centered * inverse, inverse


def by_three(step):
    def turn(i, carry):
        for j in range(3):
            carry = step(3 * i + j, carry)
        return carry

    lax.fori_loop(0, 4 * HEADS // 3, turn, 0)


def attend_fwd(w_ref, a0, a1, a2, a3, gain_ref, qid_ref, kid_ref, pre_ref, v_ref, lse_ref, o0, o1, o2, o3, q_s, k_s, o_s):
    for r, a_ref in enumerate((a0, a1, a2, a3)):
        cols = slice(OWN * r, OWN * r + OWN)
        projected = mm(w_ref[0], a_ref[...], 1, 1)
        v_ref[:, cols] = projected[2 * TILE :].astype(bf16)
        pre_ref[:, cols] = projected[: 2 * TILE]
        for c in range(2):
            for h in range(HEADS):
                rows = slice(HD * h, HD * h + HD)
                part = projected[TILE * c + HD * h : TILE * c + HD * h + HD]
                low = (column_norm(part)[0] * gain_ref[:, c : c + 1]).astype(bf16)
                if c == 0:
                    q_s[r, rows, :] = low * bf16(0.125)
                else:
                    k_s[h, cols, :] = low.T

    def step(i, carry):
        h, t = (i // 4, i % 4)
        rows = pl.ds(pl.multiple_of(h * HD, HD), HD)
        cols = pl.ds(pl.multiple_of(t * OWN, OWN), OWN)
        scores = mm(k_s[h], q_s[t, rows, :])
        scores = jnp.where(kid_ref[...] == qid_ref[:, cols], scores, masked_score)
        top = jnp.max(scores, 0, keepdims=True)
        weights = jnp.exp(scores - top)
        total = jnp.sum(weights, 0, keepdims=True)
        lse_ref[h, :, cols] = top + jnp.log(total)
        probs = (weights * (1.0 / total)).astype(bf16)
        o_s[t, rows, :] = mm(v_ref[rows, :], probs).astype(bf16)
        return carry

    by_three(step)
    for r, ref in enumerate((o0, o1, o2, o3)):
        ref[...] = o_s[r]


def run_attend_fwd(w, acts, gains, qid, kid):
    return pl.pallas_call(
        attend_fwd,
        grid=(1,),
        in_specs=[pl.BlockSpec((1, 3 * TILE, D), lambda i: (0, 0, 0))] + [VM] * 7,
        out_specs=[VM] * 7,
        out_shape=[
            shape((2 * TILE, TOKENS)),
            shape((TILE, TOKENS), bf16),
            shape((HEADS, 1, TOKENS)),
        ]
        + [shape((TILE, OWN), bf16)] * 4,
        scratch_shapes=[
            pltpu.VMEM((4, TILE, OWN), bf16),
            pltpu.VMEM((HEADS, TOKENS, HD), bf16),
            pltpu.VMEM((4, TILE, OWN), bf16),
        ],
        compiler_params=params(60),
        cost_estimate=cost(10**10, 6 * 10**6, 3 * 2**20),
        name="attend_fwd",
    )(*in_hbm(w), *acts, gains, qid, kid)


def attend_bwd(
    pre_ref, v_ref, lse_ref, g0, g1, g2, g3, gain_ref, qid_ref, kid_ref,
    p0, p1, p2, p3, dgain_ref, q_s, qn_s, k_s, kt_s, vn_s, do_s, dq_s, dk_s, dv_s,
):
    dp_refs = (p0, p1, p2, p3)
    for r, ref in enumerate((g0, g1, g2, g3)):
        do_s[r] = ref[...]
    for h in range(HEADS):
        rows = slice(HD * h, HD * h + HD)
        low = (column_norm(pre_ref[rows, :])[0] * gain_ref[:, 0:1]).astype(bf16)
        q_s[rows, :] = low * bf16(0.125)
        qn_s[h] = q_s[rows, :].T
        low = (column_norm(pre_ref[TILE + HD * h : TILE + HD * h + HD, :])[0] * gain_ref[:, 1:2]).astype(bf16)
        kt_s[rows, :] = low
        k_s[h] = low.T
        vn_s[h] = v_ref[rows, :].T
    dk_s[...] = jnp.zeros_like(dk_s)
    dv_s[...] = jnp.zeros_like(dv_s)

    def step(i, carry):
        h, t = (i // 4, i % 4)
        rows = pl.ds(pl.multiple_of(h * HD, HD), HD)
        cols = pl.ds(pl.multiple_of(t * OWN, OWN), OWN)
        scores = mm(k_s[h], q_s[rows, cols])
        scores = jnp.where(kid_ref[...] == qid_ref[:, cols], scores, masked_score)
        weights = jnp.exp(scores - lse_ref[h, :, cols])
        grad_out = do_s[t, rows, :]
        grad_weights = mm(vn_s[h], grad_out)
        dv_s[h] += mm(weights.astype(bf16), grad_out.T)
        inner = jnp.sum(weights * grad_weights, 0, keepdims=True)
        grad_scores = (weights * (grad_weights - inner)).astype(bf16)
        dq_s[rows, cols] = mm(kt_s[rows, :], grad_scores) * 0.125
        dk_s[h] += mm(grad_scores, qn_s[h, cols, :])
        return carry

    by_three(step)
    for c in range(2):
        total = jnp.zeros((HD, 1), f32)
        for h in range(HEADS):
            grad = dq_s[HD * h : HD * h + HD, :] if c == 0 else dk_s[h].T
            base = TILE * c + HD * h
            normed, inverse = column_norm(pre_ref[base : base + HD, :])
            total = total + jnp.sum(grad * normed, 1, keepdims=True)
            scaled = grad * gain_ref[:, c : c + 1]
            back = inverse * (
                scaled
                - jnp.mean(scaled, 0, keepdims=True)
                - normed * jnp.mean(scaled * normed, 0, keepdims=True)
            )
            for r in range(4):
                dp_refs[r][base : base + HD, :] = back[:, OWN * r : OWN * r + OWN].astype(bf16)
        dgain_ref[:, c : c + 1] = total
    for h in range(HEADS):
        back = dv_s[h].T.astype(bf16)
        for r in range(4):
            dp_refs[r][2 * TILE + HD * h : 2 * TILE + HD * h + HD, :] = back[:, OWN * r : OWN * r + OWN]


def run_attend_bwd(pre, v, lse, grads, gains, qid, kid):
    return pl.pallas_call(
        attend_bwd,
        in_specs=[VM] * 10,
        out_specs=[VM] * 5,
        out_shape=[shape((3 * TILE, OWN), bf16)] * 4 + [shape((HD, 2))],
        scratch_shapes=[
            pltpu.VMEM((TILE, TOKENS), bf16),
            pltpu.VMEM((HEADS, TOKENS, HD), bf16),
            pltpu.VMEM((HEADS, TOKENS, HD), bf16),
            pltpu.VMEM((TILE, TOKENS), bf16),
            pltpu.VMEM((HEADS, TOKENS, HD), bf16),
            pltpu.VMEM((4, TILE, OWN), bf16),
            pltpu.VMEM((TILE, TOKENS), f32),
            pltpu.VMEM((HEADS, TOKENS, HD), f32),
            pltpu.VMEM((HEADS, TOKENS, HD), f32),
        ],
        compiler_params=params(60),
        cost_estimate=cost(2 * 10**10, 6 * 10**6, 3 * 2**20),
        name="attend_bwd",
    )(pre, v, lse, *grads, gains, qid, kid)


def fetches(sources, targets, sems):
    copies = [
        pltpu.make_async_copy(source, target, sems.at[at])
        for at, (source, target) in enumerate(zip(sources, targets))
    ]
    for copy in copies:
        copy.start()
    return copies


def mix_fwd(x_ref, o0, o1, o2, o3, gain_ref, next_ref, out_hbm, up_hbm, down_hbm,
            mid_ref, c_ref, x_out, a_out, out_s, up_s, down_s, sems):
    sources, targets = ([out_hbm], [out_s])
    for r in range(4):
        sources += [up_hbm.at[r], down_hbm.at[r]]
        targets += [up_s.at[r], down_s.at[r]]
    copies = fetches(sources, targets, sems)
    copies[0].wait()
    total = x_ref[...]
    for k, ref in enumerate((o0, o1, o2, o3)):
        total = total + mm(ref[...], out_s[TILE * k : TILE * k + TILE, :], 0, 0)
    mid_ref[...] = total
    low = (normalize(total)[0] * gain_ref[...]).astype(bf16)
    c_ref[...] = low
    x_out[...] = total
    for r in range(4):
        copies[1 + 2 * r].wait()
        u = mm(low, up_s[r], 1, 1)
        copies[2 + 2 * r].wait()
        x_out[...] += mm(gelu(u).astype(bf16), down_s[r])
    a_out[...] = (normalize(x_out[...])[0] * next_ref[...]).astype(bf16)


def weight_scratch():
    return [
        pltpu.VMEM((D, D), bf16),
        pltpu.VMEM((4, D, D), bf16),
        pltpu.VMEM((4, D, D), bf16),
        pltpu.SemaphoreType.DMA((9,)),
    ]


def run_mix_fwd(x, outs, w_out, gain, gain_next, up, down):
    return pl.pallas_call(
        mix_fwd,
        in_specs=[VM] * 7 + [ANY] * 3,
        out_specs=[VM] * 4,
        out_shape=[shape((OWN, D)), shape((OWN, D), bf16), shape((OWN, D)), shape((OWN, D), bf16)],
        scratch_shapes=weight_scratch(),
        compiler_params=params(60),
        cost_estimate=cost(6 * 10**9, 17 * 10**6, 10**6),
        name="mix_fwd",
    )(x, *outs, gain, gain_next, *in_hbm(w_out, up, down))


def mix_bwd(g_ref, low_ref, mid_ref, c_ref, gain_ref, out_hbm, up_hbm, down_hbm,
            mid_grad, mid_low, dgain_ref, do0, do1, do2, do3, out_s, up_s, down_s, sems, acc):
    sources, targets = ([], [])
    for r in range(4):
        sources += [down_hbm.at[r], up_hbm.at[r]]
        targets += [down_s.at[r], up_s.at[r]]
    copies = fetches(sources + [out_hbm], targets + [out_s], sems)
    acc[...] = jnp.zeros_like(acc)
    for r in range(4):
        copies[2 * r].wait()
        df = mm(low_ref[...], down_s[r], 1, 1)
        copies[2 * r + 1].wait()
        u = mm(c_ref[...], up_s[r], 1, 1)
        cdf, bell = gauss_parts(u)
        du = (df * (cdf + u * bell * 0.3989422804014327)).astype(bf16)
        acc[...] += mm(du, up_s[r])
    normed, inverse = normalize(mid_ref[...])
    grad = acc[...]
    dgain_ref[...] = jnp.sum(grad * normed, 0, keepdims=True)
    total = g_ref[...] + norm_back(grad, gain_ref[...], normed, inverse)
    mid_grad[...] = total
    low = total.astype(bf16)
    mid_low[...] = low
    copies[8].wait()
    for k, ref in enumerate((do0, do1, do2, do3)):
        ref[...] = mm(out_s[TILE * k : TILE * k + TILE, :], low, 1, 1).astype(bf16)


def run_mix_bwd(grad, grad_low, mid, normed, gain, w_out, up, down):
    return pl.pallas_call(
        mix_bwd,
        in_specs=[VM] * 5 + [ANY] * 3,
        out_specs=[VM] * 7,
        out_shape=[shape((OWN, D)), shape((OWN, D), bf16), shape((1, D))] + [shape((TILE, OWN), bf16)] * 4,
        scratch_shapes=weight_scratch() + [pltpu.VMEM((OWN, D), f32)],
        compiler_params=params(60),
        cost_estimate=cost(6 * 10**9, 17 * 10**6, 10**6),
        name="mix_bwd",
    )(grad, grad_low, mid, normed, gain, *in_hbm(w_out, up, down))


def input_bwd(mid_grad, d0, d1, d2, d3, w_ref, x_ref, gain_ref, grad_ref, low_ref, dgain_ref):
    grad = mm(d0[...], w_ref[0], 0, 0)
    for k, ref in ((1, d1), (2, d2), (3, d3)):
        grad = grad + mm(ref[...], w_ref[k], 0, 0)
    normed, inverse = normalize(x_ref[...])
    dgain_ref[...] = jnp.sum(grad * normed, 0, keepdims=True)
    total = mid_grad[...] + norm_back(grad, gain_ref[...], normed, inverse)
    grad_ref[...] = total
    low_ref[...] = total.astype(bf16)


def run_input_bwd(mid_grad, grads, w, x, gain):
    return pl.pallas_call(
        input_bwd,
        in_specs=[VM] * 8,
        out_specs=[VM] * 3,
        out_shape=[shape((OWN, D)), shape((OWN, D), bf16), shape((1, D))],
        compiler_params=params(48),
        cost_estimate=cost(10**9, 6 * 10**6),
        name="input_bwd",
    )(mid_grad, *grads, w, x, gain)


def pack_wide(line, t):
    half = TILE // 2
    right = line[:, 512 + 64 * t : 576 + 64 * t]
    return jnp.concatenate(
        [
            line[:, 128 * t : 128 * t + 128],
            jnp.concatenate([right[:half], right[half:]], axis=1),
        ],
        axis=0,
    )


def send_line(places, stage, sems, keep, send, line, blocks, base):
    line = line.astype(bf16)
    for t, block in enumerate(blocks):
        at = base + t
        stage[at] = pack_wide(line, t)
        place = places[block]
        rows = pl.ds(pl.multiple_of((place % 3) * PACK, 16), PACK)

        @pl.when(place < 48)
        def _():
            pltpu.make_async_copy(stage.at[at], keep.at[place // 3, rows], sems.at[at]).start()

        @pl.when(place >= 48)
        def _():
            pltpu.make_async_copy(stage.at[at], send.at[place // 3 - 16, rows], sems.at[at]).start()


def wait_tiles(stage, sems, keep, count):
    for at in range(count):
        pltpu.make_async_copy(stage.at[at], keep.at[0, pl.ds(0, PACK)], sems.at[at]).wait()


def mlp_grads(depth, places, act_ref, low_ref, up_ref, down_ref, *refs):
    keep, send, token, stage, sems = refs[-5:]
    base = 48 * depth
    for i in range(4):
        rows = slice(TILE * i, TILE * i + TILE)
        u = mm(up_ref[0, rows, :], act_ref[...], 1, 1)
        df = mm(down_ref[0, rows, :], low_ref[...], 1, 1)
        cdf, bell = gauss_parts(u)
        f_low = (u * cdf).astype(bf16)
        du_low = (df * (cdf + u * bell * 0.3989422804014327)).astype(bf16)
        line = mm(du_low, act_ref[...])
        send_line(places, stage, sems, keep, send, line, [base + 16 + 4 * t + i for t in range(4)], 4 * i)
        line = mm(f_low, low_ref[...])
        send_line(places, stage, sems, keep, send, line, [base + 32 + 4 * i + t for t in range(4)], 16 + 4 * i)
    token[...] = jnp.zeros_like(token)
    wait_tiles(stage, sems, keep, 32)


def head_grads(depth, places, index, mid_ref, *refs):
    outs, grads, acts = (refs[0:4], refs[4:8], refs[8:12])
    keep, send, token, stage, sems = refs[-5:]
    base = 48 * depth
    parts = []
    for r in range(4):
        rows = pl.ds(pl.multiple_of((index[0] ^ r) * OWN, OWN), OWN)
        parts.append(mm(outs[r][...], mid_ref[rows, :]))
    line = (parts[0] + parts[1]) + (parts[2] + parts[3])
    send_line(places, stage, sems, keep, send, line, [base + 12 + t for t in range(4)], 12)
    for c in range(3):
        rows = slice(TILE * c, TILE * c + TILE)
        parts = [mm(grads[r][rows, :], acts[r][...]) for r in range(4)]
        line = (parts[0] + parts[1]) + (parts[2] + parts[3])
        send_line(places, stage, sems, keep, send, line, [base + 3 * t + c for t in range(4)], 4 * c)
    token[...] = jnp.zeros_like(token)
    wait_tiles(stage, sems, keep, 16)


def grads_call(kernel, name, scalars, args, specs, buffers, count, flops):
    given = list(buffers) if buffers is not None else []
    first = len(scalars) + len(args)
    *buffers, token = pl.pallas_call(
        kernel,
        grid=(1,),
        in_specs=[SM] * len(scalars) + specs + [ANY] * len(given),
        out_specs=[ANY, ANY, VM],
        out_shape=[shape((16, ROWS, 128), bf16)] * 2 + [shape((8, 128))],
        input_output_aliases={first + i: i for i in range(len(given))},
        scratch_shapes=[pltpu.VMEM((count, PACK, 128), bf16), pltpu.SemaphoreType.DMA((count,))],
        compiler_params=params(56),
        cost_estimate=cost(flops, 10**7),
        name=name,
    )(*scalars, *args, *given)
    return buffers, token


def run_mlp_grads(depth, places, pair, up, down, buffers):
    first = pl.BlockSpec((1, D, D), lambda i: (0, 0, 0))
    sides = [pl.BlockSpec((TOKENS, D), lambda i, side=side: (0, side)) for side in range(2)]
    if isinstance(pair, tuple):
        sides = [VM] * 2
    else:
        pair = (pair, pair)
    return grads_call(
        lambda *refs: mlp_grads(depth, *refs), "mlp_grads", [places],
        in_hbm(*pair, up, down), sides + [first] * 2, buffers, 32, 5 * 10**9,
    )


def run_head_grads(depth, places, index, mid_low, outs, grads, acts, buffers):
    return grads_call(
        lambda *refs: head_grads(depth, *refs), "head_grads", [places, index],
        [*in_hbm(mid_low), *outs, *grads, *acts], [VM] * 13, buffers, 16, 2 * 10**9,
    )


def whole(*dims):
    return pl.BlockSpec(dims, lambda r: (0,) * len(dims))


def part(*dims):
    return pl.BlockSpec((1, *dims), lambda r: (r,) + (0,) * len(dims))


def add_core(keep, got, own_a, a1, a2, a3, own_b, b1, b2, b3):
    step = pl.program_id(0)
    half = ROWS // 2
    total = keep[...].astype(f32) + got[...].astype(f32)

    @pl.when(step == 0)
    def _():
        own_a[...] = total[:, :half]

    for k, ref in ((1, a1), (2, a2), (3, a3)):

        @pl.when(step == k)
        def _():
            ref[...] = total[:, :half].astype(bf16)

    own_b[0] = total[0, half:]
    for k, ref in ((1, b1), (2, b2), (3, b3)):
        ref[0] = total[k, half:].astype(bf16)


def run_add_core(keep, got):
    half = ROWS // 2
    block = pl.BlockSpec((4, ROWS, 128), lambda r: (r, 0, 0))
    one, many = (whole(4, half, 128), part(half, 128))
    return pl.pallas_call(
        add_core, grid=(4,), in_specs=[block] * 2, out_specs=[one] * 4 + [many] * 4,
        out_shape=([shape((4, half, 128))] + [shape((4, half, 128), bf16)] * 3) * 2,
        compiler_params=params(32), cost_estimate=cost(10**7, 14 * 10**6), name="add_core",
    )(keep, got)


def add_axis(*refs):
    ins, outs = (refs[:8], refs[8:])
    for side in range(2):
        own, r1, r2, r3 = ins[4 * side : 4 * side + 4]
        for k in range(4):
            total = (own[k] + r1[k].astype(f32)) + (r2[k].astype(f32) + r3[k].astype(f32))
            out = outs[4 * side + k]
            out[...] = total.astype(out.dtype)


def run_add_axis(a, b):
    half = ROWS // 2
    return pl.pallas_call(
        add_axis, in_specs=[VM] * 8, out_specs=[VM] * 8,
        out_shape=([shape((half, 128))] + [shape((half, 128), bf16)] * 3) * 2,
        compiler_params=params(32), cost_estimate=cost(10**7, 6 * 10**6), name="add_axis",
    )(*a, *b)


def add_last(loss_ref, *refs):
    ins, (slots, share, squares) = (refs[:8], refs[8:])
    halves = []
    for side in range(2):
        own, r1, r2, r3 = ins[4 * side : 4 * side + 4]
        halves.append((own[...] + r1[...].astype(f32)) + (r2[...].astype(f32) + r3[...].astype(f32)))
    mine = jnp.concatenate(halves, axis=0)
    for j in range(3):
        slots[j] = mine[PACK * j : PACK * j + PACK]
    small = mine[3 * PACK :]
    share[...] = small
    lower = lax.broadcasted_iota(jnp.int32, (SMALL, 128), 0) < EMBED_ROWS + HEAD_ROWS
    weighted = small * small * jnp.where(lower, 1.0, 0.25)
    own_part = jnp.sum(mine[: 3 * PACK] * mine[: 3 * PACK], keepdims=True) + jnp.sum(weighted, keepdims=True)
    row = lax.broadcasted_iota(jnp.int32, (8, 128), 0)
    squares[...] = jnp.where(row == 0, own_part, loss_ref[...] * 0.25)


def run_add_last(loss, a, b):
    return pl.pallas_call(
        add_last, in_specs=[VM] * 9, out_specs=[VM] * 3,
        out_shape=[shape((3, PACK, 128)), shape((SMALL, 128)), shape((8, 128))],
        compiler_params=params(32), cost_estimate=cost(10**6, 2 * 10**6), name="add_last",
    )(loss, *a, *b)


def gate(array, *others):
    return pl.pallas_call(
        lambda *refs: None, in_specs=[ANY] * (1 + len(others)), out_specs=ANY,
        out_shape=shape(array.shape, array.dtype), input_output_aliases={0: 0},
        compiler_params=params(16), name="gate",
    )(array, *[in_hbm(other)[0] if other.size > 2**17 else other for other in others])


def soap_early(first, stat_l, stat_r, left, right, turned_ref, l_ref, r_ref):
    turned_ref[0] = mm_split(mm_split(left[0], first[0], 0, 0), right[0], 1, 0)
    l_ref[0] = mm_full(stat_l[0], left[0], 1, 0)
    r_ref[0] = mm_full(stat_r[0], right[0], 1, 0)


def soap_mid(flip_ref, packed, left, right, grad_ref, turned_ref, yl_ref, yr_ref, gl_ref, gr_ref):
    tile = unpack_tile(packed[0])
    turned_tile = tile.T
    flip = flip_ref[pl.program_id(0)] == 1
    grad = jnp.where(flip, turned_tile, tile)
    grad_t = jnp.where(flip, tile, turned_tile)
    grad_ref[0] = grad
    right_part = mm_full(grad, right[0], 1, 0)
    turned_ref[0] = mm_split(left[0], right_part, 0, 0)
    yr_ref[0] = mm_full(grad_t, right_part, 1, 0)
    yl_ref[0] = mm_full(grad, mm_full(grad_t, left[0], 1, 0), 1, 0)
    gl_ref[0] = mm_full(grad, grad_t, 1, 0)
    gr_ref[0] = mm_full(grad_t, grad, 1, 0)


def factor_inverses(grams, fillers=()):
    size = 64
    fillers = list(fillers)
    row = lax.broadcasted_iota(jnp.int32, (8, 128), 0)
    lane = lax.broadcasted_iota(jnp.int32, (8, 128), 1)
    on_diagonal = lax.broadcasted_iota(jnp.int32, (size, size), 0) == lax.broadcasted_iota(
        jnp.int32, (size, size), 1
    )
    states, scales = ([], [])
    for gram in grams:
        diagonal = jnp.where(on_diagonal, gram, 0.0)
        scale_row = lax.rsqrt(jnp.sum(diagonal, axis=0, keepdims=True))
        scale_column = lax.rsqrt(jnp.sum(diagonal, axis=1, keepdims=True))
        scales.append(scale_row)
        wide = jnp.concatenate([gram * scale_row * scale_column, jnp.zeros((size, size), f32)], axis=1)
        states.append(
            [jnp.where(lane == row + (size + 8 * t), 1.0, wide[8 * t : 8 * t + 8, :]) for t in range(8)]
        )
    for k in range(0, size, 2):
        home, at = divmod(k, 8)
        for tiles in states:
            own = tiles[home]
            first, second = (own[at : at + 1, :], own[at + 1 : at + 2, :])
            a, b, c = (
                jnp.broadcast_to(entry, (1, 128))
                for entry in (first[:, k : k + 1], first[:, k + 1 : k + 2], second[:, k + 1 : k + 2])
            )
            inverse = 1.0 / (a * c - b * b)
            line_first = (c * first - b * second) * inverse
            line_second = (a * second - b * first) * inverse
            for t in range(home, 8):
                update = tiles[t][:, k : k + 1] * line_first + tiles[t][:, k + 1 : k + 2] * line_second
                if t == home:
                    inside = jnp.where(row == at + 1, first * (b / a), 0.0)
                    update = jnp.where(row > at + 1, update, inside)
                tiles[t] = tiles[t] - update
        if fillers:
            fillers.pop(0)()
    for filler in fillers:
        filler()
    inverses = []
    for tiles, scale_row in zip(states, scales):
        done = []
        for t in range(8):
            diagonal = jnp.sum(jnp.where(lane == row + 8 * t, tiles[t], 0.0), axis=1, keepdims=True)
            done.append(tiles[t] * lax.rsqrt(diagonal))
        inverses.append(jnp.concatenate(done, axis=0)[:, size:] * scale_row)
    return inverses


def soap_late(
    f_ref, second, left, right, weight, turned, turned_first, xl, xr, yl, yr,
    weight_ref, left_ref, right_ref, panels, work,
):
    factor = f_ref[0, 0]
    bias_one = 1.0 - first_decay**STEP
    bias_two = 1.0 - second_decay**STEP
    outs = (left_ref, right_ref)

    def product(i):
        n, (old, new) = (i // 2, ((xl, yl), (xr, yr))[i % 2])
        total = second_decay * old[n] + (1.0 - second_decay) * (factor * (factor * new[n]))
        for j in range(3):
            panels[i, j] = total[:, 64 * j : 64 * j + 64]

    def scaled(n):
        rotated = turned[n] * factor
        second_new = second_decay * second[n] + (1.0 - second_decay) * rotated * rotated
        work[n] = (
            (first_decay * turned_first[n] + (1.0 - first_decay) * rotated)
            / bias_one
            / (jnp.sqrt(second_new / bias_two) + adam_epsilon)
        )

    def half_back(n):
        work[n] = mm_split(left[n], work[n], 1, 0)

    def move(n):
        back = mm_split(work[n], right[n], 1, 1)
        weight_new = weight[n] * (1.0 - matrix_rate * weight_decay) - matrix_rate * back
        weight_ref[n] = weight_new

    def remove(i, basis, k):
        panel = panels[i, k]
        panels[i, k] = panel - mm_full(basis, mm_full(basis, panel, 0, 0), 1, 0)

    def grams(j):
        return [mm_full(panels[i, j], panels[i, j], 0, 0) for i in range(6)]

    def bases(j, inverses):
        found = []
        for i in range(6):
            basis = mm_full(panels[i, j], inverses[i], 1, 1)
            outs[i % 2][i // 2, :, 64 * j : 64 * j + 64] = basis
            found.append(basis)
        return found

    for i in range(6):
        product(i)
    pieces = [lambda step=step, n=n: step(n) for n in range(3) for step in (scaled, half_back, move)]
    found = bases(0, factor_inverses(grams(0), pieces))
    for i in range(6):
        remove(i, found[i], 1)
    pieces = [lambda i=i, basis=found[i]: remove(i, basis, 2) for i in range(6)]
    found = bases(1, factor_inverses(grams(1), pieces))
    for i in range(6):
        remove(i, found[i], 2)
    bases(2, factor_inverses(grams(2)))


def tile_spec():
    return pl.BlockSpec((1, TILE, TILE), lambda i: (i, 0, 0))


def tiles_of_three(count):
    return [shape((3, TILE, TILE))] * count


def run_soap_early(first, stat_l, stat_r, left, right):
    return pl.pallas_call(
        soap_early, grid=(3,), in_specs=[tile_spec()] * 5, out_specs=[tile_spec()] * 3,
        out_shape=tiles_of_three(3), compiler_params=params(32), cost_estimate=cost(10**9, 4 * 10**6), name="soap_early",
    )(first, stat_l, stat_r, left, right)


def run_soap_mid(flips, packed, left, right):
    return pl.pallas_call(
        soap_mid, grid=(3,),
        in_specs=[SM, pl.BlockSpec((1, PACK, 128), lambda i: (i, 0, 0)), tile_spec(), tile_spec()],
        out_specs=[tile_spec()] * 6, out_shape=tiles_of_three(6),
        compiler_params=params(32), cost_estimate=cost(10**9, 4 * 10**6), name="soap_mid",
    )(flips, packed, left, right)


def run_soap_late(*args):
    return pl.pallas_call(
        soap_late, in_specs=[SM] + [VM] * 10, out_specs=[VM] * 3,
        out_shape=tiles_of_three(3),
        scratch_shapes=[pltpu.VMEM((6, 3, TILE, 64), f32), pltpu.VMEM((3, TILE, TILE), f32)],
        compiler_params=params(56), cost_estimate=cost(10**9, 10**7), name="soap_late",
    )(*args)


def adamw(master, gradient, first, second, rate, decay):
    first_new = first_decay * first + (1.0 - first_decay) * gradient
    second_new = second_decay * second + (1.0 - second_decay) * gradient * gradient
    step_dir = (
        first_new
        / (1.0 - first_decay**STEP)
        / (jnp.sqrt(second_new / (1.0 - second_decay**STEP)) + adam_epsilon)
    )
    return (master * (1.0 - rate * decay) - rate * step_dir, first_new, second_new)


def swap(array, axis, r, size):
    return lax.ppermute(array, axis, [(i, i ^ r) for i in range(size)])


def swap_mp(array, r):
    return swap(array, "mp", r, 4)


def swap_dp(array, r):
    return swap(array, "dp", r, 32)


def gather_mp(array):
    return [array] + [swap_mp(array, r) for r in (1, 2, 3)]


def trade_mp(pieces):
    return [pieces[0]] + [swap_mp(pieces[r], r) for r in (1, 2, 3)]


def sum_four(pieces):
    return (pieces[0] + pieces[1]) + (pieces[2] + pieces[3])


def total_mp(array):
    return sum_four(gather_mp(array))


def total_dp(array):
    array = array + swap_dp(array, 1)
    array = sum_four([array] + [swap_dp(array, 2 * r) for r in (1, 2, 3)])
    return sum_four([array] + [swap_dp(array, 8 * r) for r in (1, 2, 3)])


def by_partner(array, index):
    return jnp.take(array, jnp.arange(array.shape[0]) ^ index, axis=0)


def shards(
    patches, image_ids, keep, labels, owners,
    soap_weight, soap_first, soap_second, stat_left, stat_right, basis_left, basis_right,
    embed_weight, embed_first, embed_second, head_weight, head_first, head_second,
    vectors, vector_first, vector_second,
):
    mp_index = lax.axis_index("mp")
    dp_index = lax.axis_index("dp")

    def tiled(flat_rows):
        return flat_rows.reshape(3, TILE, TILE)

    device, within = (owners // 3, owners % 3)
    partners = jnp.arange(4) ^ mp_index
    table = (device * 12 + within)[None, :] + 3 * partners[:, None]
    table = table.reshape(-1).astype(jnp.int32)
    relative = device ^ dp_index
    places = (((relative & 1) * 16 + (relative >> 1)) * 3 + within).astype(jnp.int32)
    my_slots = dp_index * 3 + jnp.arange(3)
    my_blocks = jnp.sum(
        jnp.where(owners[None, :] == my_slots[:, None], jnp.arange(96)[None, :], 0), axis=1
    )
    kind = my_blocks % 48
    flips = (kind < 12) | ((kind >= 16) & (kind < 32))

    master = tiled(soap_weight)
    low = master.astype(bf16)
    low = jnp.where(flips[:, None, None], jnp.swapaxes(low, 1, 2), low)
    slots = lax.all_gather(pack_tile(low), ("dp", "mp"), axis=0, tiled=True)

    head_low = lax.all_gather(head_weight.astype(bf16), "mp", axis=0, tiled=True)

    split_one = (2 * LAYERS + 1) * D
    split_two = split_one + 2 * LAYERS * HD
    gain_rows = vectors[:split_one].reshape(2 * LAYERS + 1, 4, TILE)
    gain_rows = widen([gain_rows[:, t] for t in range(4)], 1)[:, None, :]
    head_gains = vectors[split_one : split_one + 2 * LAYERS * HD].reshape(LAYERS, 2, HD)
    class_bias = vectors[vectors.shape[0] - CLASSES :]

    tokens = by_partner(patches.reshape(4, OWN, D), mp_index)
    ids = by_partner(image_ids.reshape(4, OWN), mp_index)
    kept = by_partner(keep.reshape(4, OWN), mp_index) == 1
    query_ids = ids.reshape(1, TOKENS)
    key_ids = jnp.where(kept, ids, -1).reshape(TOKENS, 1)
    member_all = (image_ids[0, :, None] == jnp.arange(IMGS)[None, :]) & (keep[0, :, None] == 1)
    counts = jnp.sum(member_all.astype(f32), axis=0)
    present = (counts > 0).astype(f32)
    divisor = jnp.maximum(counts, 1.0)
    member = ((ids[0][:, None] == jnp.arange(IMGS)[None, :]) & kept[0][:, None]).astype(f32)
    image_sum = total_dp(jnp.full((8, 128), jnp.sum(present), f32))
    image_total = image_sum[0, 0]

    first_tiles, second_tiles = (tiled(soap_first), tiled(soap_second))
    left_stat, right_stat = (tiled(stat_left), tiled(stat_right))
    left, right = (tiled(basis_left), tiled(basis_right))
    turned_first, left_old, right_old = run_soap_early(first_tiles, left_stat, right_stat, left, right)

    embedded = jnp.dot(tokens.reshape(TOKENS, D), embed_weight.astype(bf16), preferred_element_type=f32)
    embedded = embedded.astype(bf16).reshape(4, OWN, TILE)
    embedded = by_partner(jnp.stack(trade_mp([embedded[r] for r in range(4)])), mp_index)
    resid = widen([embedded[t] for t in range(4)], 1).astype(f32)
    act = (normalize(resid)[0] * gain_rows[0]).astype(bf16)

    blocks = [layer_blocks(depth) for depth in range(LAYERS)]
    weights = [assemble(table, slots, blocks[0][:1]) + assemble(table, slots, blocks[0][1:])]
    weights += [assemble(table, slots, blocks[depth]) for depth in range(1, LAYERS)]
    index = jnp.full((1,), mp_index, jnp.int32)
    saved = []
    normed = None
    for depth in range(LAYERS):
        qkv, out, up, down = weights[depth]
        out = out.reshape(D, D)
        gains = head_gains[depth].T
        acts = gather_mp(act)
        if depth == 0:
            acts[0] = gate(acts[0], turned_first, second_tiles, image_sum)
        else:
            normed = gate(normed, *acts[1:], qkv)
            gains = gate(gains, head_low)
            saved[-1].append(lax.all_gather(normed, "mp", axis=0, tiled=True))
        pre, v, lse, *o = run_attend_fwd(qkv, acts, gains, query_ids, key_ids)
        outs = trade_mp(o)
        mid, normed, resid_next, act = run_mix_fwd(
            resid, outs, out, gain_rows[2 * depth + 1], gain_rows[2 * depth + 2], up, down
        )
        saved.append([resid, acts, pre, v, lse, o, mid, normed])
        resid = resid_next
    saved[-1].append(None)

    final, final_inverse = normalize(resid)
    gain_last = gate(gain_rows[2 * LAYERS], saved[0][-1])
    pooled = total_mp(jnp.dot(member.T, final * gain_last, precision=highest)) / divisor[:, None]
    pooled = jnp.concatenate([pooled[:, :512].reshape(IMGS, 4, 128), pooled[:, 512:].reshape(IMGS, 4, 64)], axis=2)
    pooled_low = pooled.reshape(IMGS, D).astype(bf16)
    logits = jnp.dot(pooled_low, head_low, preferred_element_type=f32) + class_bias
    row_max = jnp.max(logits, -1, keepdims=True)
    exps = jnp.exp(logits - row_max)
    row_sum = jnp.sum(exps, -1, keepdims=True)
    log_norm = row_max[:, 0] + jnp.log(row_sum[:, 0])
    onehot = (jnp.arange(CLASSES)[None, :] == labels.reshape(-1)[:, None]).astype(f32)
    local_loss = jnp.sum((log_norm - jnp.sum(onehot * logits, -1)) * present)
    grad_logits = (exps / row_sum - onehot) * present[:, None] / image_total
    grad_bias = jnp.sum(grad_logits, 0)
    grad_logit_low = grad_logits.astype(bf16)
    pooled_mine = lax.dynamic_slice_in_dim(pooled_low, mp_index * TILE, TILE, 1)
    grad_head = jnp.dot(pooled_mine.T, grad_logit_low, preferred_element_type=f32)
    grad_pooled = jnp.dot(grad_logit_low, head_low.T, preferred_element_type=f32)
    grad_pooled = grad_pooled / divisor[:, None]
    grad_pooled = widen([grad_pooled[:, TILE * t : TILE * t + TILE] for t in range(4)], 1)
    grad_final = jnp.dot(member, grad_pooled, precision=highest)
    gain_grads = [wide_back(jnp.sum(grad_final * final, 0))]
    grad = norm_back(grad_final, gain_last, final, final_inverse)
    grad_low = grad.astype(bf16)

    buffers = waiting = None
    head_gain_grads = []
    for depth in reversed(range(LAYERS)):
        qkv, out, up, down = weights[depth]
        resid, acts, pre, v, lse, o, mid, own_normed, normed = saved[depth]
        gains = head_gains[depth].T
        out = out.reshape(D, D)
        if normed is None:
            pair = lax.all_gather(jnp.concatenate([own_normed, grad_low], axis=1), "mp", axis=0, tiled=True)
        else:
            pair = (normed, lax.all_gather(grad_low, "mp", axis=0, tiled=True))
        mid_grad, mid_low, gain_two, *do = run_mix_bwd(
            grad, grad_low, mid, own_normed, gain_rows[2 * depth + 1], out, up, down
        )
        dos = trade_mp(do)
        mid_lows = lax.all_gather(gate(mid_low, *dos[1:]), "mp", axis=0, tiled=True)
        if waiting is not None:
            deeper, given, *rest = waiting
            buffers, token = run_head_grads(deeper, places, gate(index, dos[1]), given, *rest, buffers)
            gains = gate(gains, token)
        *dp, gain_heads = run_attend_bwd(pre, v, lse, dos, gains, query_ids, key_ids)
        dps = trade_mp(dp)
        buffers, token = run_mlp_grads(depth, places, pair, up, down, buffers)
        gain = gate(gain_rows[2 * depth], token)
        grad, grad_low, gain_one = run_input_bwd(mid_grad, dps, qkv, resid, gain)
        waiting = (depth, mid_lows, o, dp, acts)
        gain_grads = [wide_back(gain_one[0]), wide_back(gain_two[0])] + gain_grads
        head_gain_grads.insert(0, gain_heads.T)

    deeper, *rest = waiting
    buffers, token = run_head_grads(deeper, places, index, *rest, buffers)

    vector_part = jnp.concatenate([jnp.concatenate(gain_grads), jnp.stack(head_gain_grads).reshape(-1)])
    vector_part = jnp.pad(vector_part, (0, 32 * TILE - vector_part.shape[0])).reshape(32, TILE).astype(bf16)
    traded = trade_mp(
        [jnp.concatenate([wide_part(grad_low, mp_index ^ r, 1), vector_part], axis=0) for r in range(4)]
    )
    traded[0] = gate(traded[0], token)
    columns = jnp.concatenate([piece[:OWN] for piece in traded], axis=0)
    grad_embed = jnp.dot(columns.T, tokens.reshape(TOKENS, D), preferred_element_type=f32)
    embed_rows = grad_embed.reshape(32, EMBED_ROWS, 128)
    vector_total = sum_four([piece[OWN:].astype(f32) for piece in traded]).reshape(-1)
    head_rows = jnp.pad(grad_head, ((0, 0), (0, 24))).reshape(32, HEAD_ROWS, 128)
    vector_sum = jnp.concatenate([vector_total[:split_two], grad_bias, jnp.zeros((24,), f32)])
    vector_rows = jnp.pad(vector_sum.reshape(32, 160), ((0, 0), (0, 1536 - 160))).reshape(32, 12, 128)
    small = jnp.concatenate([embed_rows, head_rows, vector_rows], axis=1).astype(bf16)
    small = by_partner(small, dp_index).reshape(16, 2, SMALL, 128)
    keep_buffer = buffers[0].at[:, 3 * PACK :].set(small[:, 0])
    send_buffer = buffers[1].at[:, 3 * PACK :].set(small[:, 1])

    sums = run_add_core(keep_buffer, swap_dp(send_buffer, 1))
    sums = run_add_axis(
        [sums[0]] + [swap_dp(sums[r], 8 * r) for r in (1, 2, 3)],
        [sums[4]] + [swap_dp(sums[4 + r], 2 * r) for r in (1, 2, 3)],
    )
    mine_slots, share, squares = run_add_last(
        local_loss.reshape(1, 1),
        [sums[0]] + [swap_dp(sums[r], 2 * r) for r in (1, 2, 3)],
        [sums[4]] + [swap_dp(sums[4 + r], 8 * r) for r in (1, 2, 3)],
    )
    shares = lax.all_gather(share, "dp", axis=0)
    cut_at = EMBED_ROWS + HEAD_ROWS

    def flat(tiles):
        return tiles.reshape(3, TILE * TILE)

    grad_tiles, turned, left_new, right_new, gram_left, gram_right = run_soap_mid(
        flips.astype(jnp.int32), mine_slots, left, right
    )
    squares = total_mp(squares)
    squares = squares + swap_dp(squares, 1)
    squares = sum_four([squares] + [swap_dp(squares, 2 * r) for r in (1, 2, 3)])
    flats = [flat(grad_tiles), flat(turned), flat(gram_left), flat(gram_right)]
    squares = gate(squares, *flats)
    squares = sum_four([squares] + [swap_dp(squares, 8 * r) for r in (1, 2, 3)])
    squares, loss_total = (squares[0, 0], squares[1, 0])
    grad_norm = jnp.sqrt(squares)
    factor = clip_limit / jnp.maximum(grad_norm, clip_limit)

    grad_flat, turned_flat, gram_left, gram_right = flats
    weight_new, left_basis, right_basis = run_soap_late(
        factor.reshape(1, 1), second_tiles, left, right, master, turned, turned_first,
        left_old, right_old, left_new, right_new,
    )
    turned_flat = turned_flat * factor
    weight_flat = flat(weight_new)
    soap_new = (
        weight_flat,
        first_decay * soap_first + (1.0 - first_decay) * (grad_flat * factor),
        second_decay * soap_second + (1.0 - second_decay) * turned_flat * turned_flat,
        second_decay * stat_left + (1.0 - second_decay) * (factor * (factor * gram_left)),
        second_decay * stat_right + (1.0 - second_decay) * (factor * (factor * gram_right)),
        flat(left_basis),
        flat(right_basis),
        weight_flat.astype(bf16),
    )

    grad_embed = shares[:, :EMBED_ROWS].reshape(TILE, D)
    grad_head = shares[:, EMBED_ROWS:cut_at].reshape(TILE, 1024)[:, :CLASSES]
    grad_vector = shares[:, cut_at:].reshape(32, 1536)[:, :160].reshape(-1)[: vectors.shape[0]]
    embed_new = adamw(
        embed_weight.T, grad_embed * factor, embed_first.T, embed_second.T, matrix_rate, weight_decay
    )
    embed_new = tuple(entry.T for entry in embed_new)
    head_new = adamw(
        head_weight, grad_head * factor, head_first, head_second, matrix_rate, weight_decay
    )
    vector_new = adamw(vectors, grad_vector * factor, vector_first, vector_second, vector_rate, 0.0)
    return (loss_total, image_total, grad_norm, *soap_new, *embed_new, *head_new, *vector_new)


def solution(mesh):
    by_slot = P(("dp", "mp"), None)
    columns = P(None, "mp")
    rows = P("mp", None)
    return jax.shard_map(
        shards,
        mesh=mesh,
        in_specs=(P("dp", None, None), P("dp", None), P("dp", None), P("dp", None), P())
        + (by_slot,) * 7
        + (columns,) * 3
        + (rows,) * 3
        + (P(),) * 3,
        out_specs=(P(),) * 3 + (by_slot,) * 8 + (columns,) * 3 + (rows,) * 3 + (P(),) * 3,
        check_vma=False,
    )
```
